32 devices in a mesh: tok: 4 (over y, x), cent: 8 (over z, core).
Axes of the slice: x: 2, y: 2, z: 4, core: 2. Of those that a mesh axis runs over, the one named last changes fastest.
Arguments:
- tokens: bfloat16 [8192, 128], P('tok'), may hold values from -80 to 80
- centroids: bfloat16 [262144, 128], P('cent'), may hold values from -0.6 to 0.6
Outputs:
- updated: float32 [262144, 128], P('cent')
- masses: float32 [262144], P('cent')
The draws below stay inside these ranges and needn't reach their ends.
All inputs are finite; a program needn't handle non-finite values.
Results may differ from the reference program's by a relative error of at most 0.0028.
Values may be sent and summed in bfloat16 or wider, within the bound.
No kernel may reach another device: no remote copies, remote signals or barrier semaphores. Data moves between devices by JAX's collectives and lax.ppermute only.
A program may use at most 128 MiB of HBM per device.

```python
import jax
import jax.numpy as jnp
from jax import lax

D = 128
K = 262144
TOK_DEV = 2048
TOKENS = 8192


def base_centroids(key):
    common = jnp.clip(jax.random.normal(jax.random.fold_in(key, 11), (K, D), jnp.float32) * 0.1, -0.6, 0.6)
    index = jnp.arange(K)
    previous = jnp.roll(common, 1, axis=0)
    paired = 0.99 * previous + 0.005 * common
    return jnp.where((index % 64 == 1)[:, None], paired, common)


def draw_centroids(key, part):
    common = base_centroids(key)
    return common.astype(jnp.bfloat16)


def draw_tokens(key, part):
    common = base_centroids(key)
    key = jax.random.fold_in(key, 3)
    values = jnp.clip(jax.random.normal(key, (TOKENS, D), jnp.float32), -6.0, 6.0)
    period = min(256, TOK_DEV)
    index = jnp.arange(TOKENS)
    group = index // period
    target = group * 37 % (K // 64) * 64
    levels = jnp.array([40.0, 80.0, 120.0], jnp.float32)
    strength = levels[group % 3] * (128 // D)
    aligned = strength[:, None] * common[target]
    values = jnp.where((index % period == 0)[:, None], aligned, values)
    return values.astype(jnp.bfloat16)


def setup_inputs(seed: int = 0) -> dict:
    key_of = jax.random.split(jax.random.key(seed), 3)
    return {
        "tokens": draw_tokens(jax.random.fold_in(key_of[2], 71), 0),
        "centroids": draw_centroids(jax.random.fold_in(key_of[2], 71), 0),
    }


inverse_temp = 2.0
prior_weight = 0.05


def reference(tokens, centroids):
    block_rows = min(512, TOKENS)
    tok_blocks = tokens.reshape(TOKENS // block_rows, block_rows, D)

    def step(accum, tok_block):
        cent_sums, masses = accum
        logits = jnp.dot(tok_block, centroids.T, preferred_element_type=jnp.float32) * inverse_temp
        row_max = jnp.max(logits, axis=1, keepdims=True)
        scaled = jnp.exp(logits - row_max)
        row_sum = jnp.sum(scaled, axis=1, keepdims=True)
        weights = (scaled / row_sum).astype(jnp.bfloat16)
        masses = masses + jnp.sum(weights.astype(jnp.float32), axis=0)
        cent_sums = cent_sums + jnp.einsum("tc,td->cd", weights.astype(jnp.float32), tok_block.astype(jnp.float32))
        return (cent_sums, masses), None

    start = (jnp.zeros((K, D), jnp.float32), jnp.zeros((K,), jnp.float32))
    (cent_sums, masses), _ = lax.scan(step, start, tok_blocks)
    updated = (cent_sums + prior_weight * centroids.astype(jnp.float32)) / (masses[:, None] + prior_weight)
    return updated, masses
```

```python
import functools

import jax
import jax.numpy as jnp
from jax import lax
from jax.experimental import pallas as pl
from jax.experimental.pallas import tpu as pltpu
from jax.sharding import PartitionSpec as P

inverse_temp = 2.0
prior_weight = 0.05
safe_sum = 1e30
vmem_bytes = 56 * 1024 * 1024


def divisor(count, most):
    size = min(count, most)
    while count % size:
        size //= 2
    return size


def dot_nt(a, b):
    return lax.dot_general(a, b, (((1,), (1,)), ((), ())), preferred_element_type=jnp.float32)


def fold_rows(x, combine):
    parts = [x[k * 8 : (k + 1) * 8, :] for k in range(x.shape[0] // 8)]
    while len(parts) > 1:
        half = len(parts) // 2
        parts = [combine(parts[2 * k], parts[2 * k + 1]) for k in range(half)] + parts[2 * half :]
    return parts[0]


def stats_kernel(sub_rows, tok_cols, tok_ref, cent_ref, out_ref, base_ref, shift_ref, sums_ref):
    step = pl.program_id(0)
    tok_count = tok_ref.shape[0]
    tile = divisor(sub_rows, 256)
    subs = cent_ref.shape[0] // sub_rows
    col_blocks = tok_count // tok_cols

    def columns(t):
        return pl.ds(pl.multiple_of(t * tok_cols, tok_cols), tok_cols)

    def scaled_tokens(t):
        return tok_ref[columns(t), :] * jnp.bfloat16(inverse_temp)

    @pl.when(step == 0)
    def _():
        @pl.loop(0, col_blocks)
        def _(t):
            logits = dot_nt(cent_ref[0:128, :], scaled_tokens(t))
            top = jnp.max(fold_rows(logits, jnp.maximum), axis=0, keepdims=True)
            base_ref[:, columns(t)] = top

    @pl.loop(0, col_blocks)
    def _(t):
        rhs = scaled_tokens(t)
        shift = base_ref[:, columns(t)]
        for sub in range(subs):
            total = jnp.zeros((8, tok_cols), jnp.float32)
            for k in range(sub_rows // tile):
                logits = dot_nt(cent_ref[pl.ds(sub * sub_rows + k * tile, tile), :], rhs)
                total = total + fold_rows(jnp.exp(logits - shift), jnp.add)
            sums_ref[step * subs + sub, :, columns(t)] = total
            shift_ref[step * subs + sub, :, columns(t)] = shift

    worst = jnp.max(sums_ref[pl.ds(step * subs, subs), :, :])

    @pl.when(jnp.logical_not(worst < safe_sum))
    def _():
        @pl.loop(0, col_blocks)
        def _(t):
            worst_t = jnp.max(sums_ref[pl.ds(step * subs, subs), :, columns(t)])

            @pl.when(jnp.logical_not(worst_t < safe_sum))
            def _():
                @pl.loop(0, subs)
                def _(sub):
                    worst_s = jnp.max(sums_ref[step * subs + sub, :, columns(t)])

                    @pl.when(jnp.logical_not(worst_s < safe_sum))
                    def _():
                        rhs = scaled_tokens(t)
                        lowest = base_ref[:, columns(t)]

                        def logits_of(k):
                            first = pl.multiple_of(sub * sub_rows + k * tile, tile)
                            return dot_nt(cent_ref[pl.ds(first, tile), :], rhs)

                        def raise_top(k, top):
                            return jnp.maximum(top, fold_rows(logits_of(k), jnp.maximum))

                        top = lax.fori_loop(
                            0, sub_rows // tile, raise_top, jnp.broadcast_to(lowest, (8, tok_cols))
                        )
                        top = jnp.max(top, axis=0, keepdims=True)

                        def add_up(k, total):
                            return total + fold_rows(jnp.exp(logits_of(k) - top), jnp.add)

                        total = lax.fori_loop(
                            0, sub_rows // tile, add_up, jnp.zeros((8, tok_cols), jnp.float32)
                        )
                        sums_ref[step * subs + sub, :, columns(t)] = total
                        shift_ref[step * subs + sub, :, columns(t)] = top

    @pl.when(step == pl.num_programs(0) - 1)
    def _():
        @pl.loop(0, col_blocks)
        def _(t):
            shifts = shift_ref[:, :, columns(t)]
            top = jnp.max(shifts, axis=0)
            scale = jnp.exp(shifts - top[None])
            total = jnp.sum(sums_ref[:, :, columns(t)] * scale, axis=0)
            total = jnp.sum(total, axis=0, keepdims=True)
            out_ref[:, columns(t)] = top + jnp.log(total)


def local_lse(tokens, centroids):
    tok_count, width = tokens.shape
    cent_count = centroids.shape[0]
    block_rows = divisor(cent_count, 4096)
    sub_rows = divisor(block_rows, 1024)
    tok_cols = divisor(tok_count, 512)
    blocks = cent_count // block_rows
    subs = cent_count // sub_rows
    return pl.pallas_call(
        functools.partial(stats_kernel, sub_rows, tok_cols),
        grid=(blocks,),
        in_specs=[
            pl.BlockSpec((tok_count, width), lambda j: (0, 0)),
            pl.BlockSpec((block_rows, width), lambda j: (j, 0)),
        ],
        out_specs=pl.BlockSpec((1, tok_count), lambda j: (0, 0)),
        out_shape=jax.ShapeDtypeStruct((1, tok_count), jnp.float32),
        scratch_shapes=[
            pltpu.VMEM((1, tok_count), jnp.float32),
            pltpu.VMEM((subs, 1, tok_count), jnp.float32),
            pltpu.VMEM((subs, 8, tok_count), jnp.float32),
        ],
        compiler_params=pltpu.CompilerParams(vmem_limit_bytes=vmem_bytes),
        cost_estimate=pl.CostEstimate(
            flops=2 * tok_count * cent_count * width,
            bytes_accessed=(tok_count + cent_count) * width * 2,
            transcendentals=tok_count * cent_count,
        ),
        name="row_stats",
    )(tokens, centroids)


def update_kernel(shards, place_ref, *refs):
    tok_refs, lse_refs = refs[:shards], refs[shards : 2 * shards]
    cent_ref, new_ref, mass_ref, weights_ref, total_ref = refs[2 * shards :]
    rows = cent_ref.shape[0]
    depth, width = tok_refs[0].shape
    tile = divisor(rows, 256)
    piece = divisor(depth, 512)

    def weigh(first, stage):
        cents = cent_ref[pl.ds(first, tile), :] * jnp.bfloat16(inverse_temp)
        for k in range(depth // piece):
            span = pl.ds(k * piece, piece)
            logits = dot_nt(cents, tok_refs[stage][span, :])
            weights = jnp.exp(logits - lse_refs[stage][:, span])
            weights_ref[stage % 2, :, span] = weights.astype(jnp.bfloat16)

    def gather_up(stage):
        toks = tok_refs[stage][...]
        rhs = jnp.concatenate([toks, jnp.ones_like(toks)], axis=1)
        part = jnp.dot(weights_ref[stage % 2], rhs, preferred_element_type=jnp.float32)
        if stage == 0:
            total_ref[...] = part
        else:
            total_ref[...] += part

    diagonal = lax.broadcasted_iota(jnp.int32, (128, 128), 0) == lax.broadcasted_iota(
        jnp.int32, (128, 128), 1
    )

    @pl.loop(0, rows // tile)
    def _(r):
        first = pl.multiple_of(r * tile, tile)
        weigh(first, 0)
        for stage in range(1, shards):
            weigh(first, stage)
            gather_up(stage - 1)
        gather_up(shards - 1)
        sums = total_ref[:, 0:width]
        mass = total_ref[:, width : 2 * width]
        cents = cent_ref[pl.ds(first, tile), :].astype(jnp.float32)
        new = (sums + prior_weight * cents) / (mass + prior_weight)
        new_ref[pl.ds(first, tile), :] = new.astype(new_ref.dtype)
        for k in range(tile // 128):
            square = jnp.where(diagonal, mass[k * 128 : (k + 1) * 128, :], 0.0)
            mass_ref[r * (tile // 128) + k] = jnp.sum(square, axis=0, keepdims=True)


def updated_chunk(place, toks, lses, centroids, rows):
    shards = len(toks)
    depth, width = toks[0].shape
    block_rows = divisor(rows, 1024)
    tile = divisor(block_rows, 256)
    per_chunk = rows // block_rows
    all_count = shards * depth
    whole = lambda j, place: (0, 0)
    return pl.pallas_call(
        functools.partial(update_kernel, shards),
        grid_spec=pltpu.PrefetchScalarGridSpec(
            num_scalar_prefetch=1,
            grid=(per_chunk,),
            in_specs=[pl.BlockSpec((depth, width), whole)] * shards
            + [pl.BlockSpec((1, depth), whole)] * shards
            + [pl.BlockSpec((block_rows, width), lambda j, place: (place[0] * per_chunk + j, 0))],
            out_specs=[
                pl.BlockSpec((block_rows, width), lambda j, place: (j, 0)),
                pl.BlockSpec((block_rows // 128, 1, 128), lambda j, place: (j, 0, 0)),
            ],
            scratch_shapes=[
                pltpu.VMEM((2, tile, depth), jnp.bfloat16),
                pltpu.VMEM((tile, 2 * width), jnp.float32),
            ],
        ),
        out_shape=[
            jax.ShapeDtypeStruct((rows, width), jnp.float32),
            jax.ShapeDtypeStruct((rows // 128, 1, 128), jnp.float32),
        ],
        compiler_params=pltpu.CompilerParams(vmem_limit_bytes=vmem_bytes),
        cost_estimate=pl.CostEstimate(
            flops=6 * all_count * rows * width,
            bytes_accessed=(2 * all_count + 4 * rows) * width,
            transcendentals=all_count * rows,
        ),
        name="new_rows",
    )(place, *toks, *lses, centroids)


def combine_kernel(*refs):
    parts, out_ref = [ref[...] for ref in refs[:-1]], refs[-1]
    top = functools.reduce(jnp.maximum, parts)
    out_ref[...] = top + jnp.log(sum(jnp.exp(part - top) for part in parts))


def combined_lse(parts):
    return pl.pallas_call(
        combine_kernel, out_shape=jax.ShapeDtypeStruct(parts[0].shape, jnp.float32), name="join_stats"
    )(*parts)


def blank(shape):
    return pl.pallas_call(
        lambda out_ref: None,
        out_specs=pl.BlockSpec(memory_space=pl.ANY),
        out_shape=jax.ShapeDtypeStruct(shape, jnp.float32),
        name="blank",
    )()


def from_others(value, axis):
    size = lax.axis_size(axis)
    found = [value]
    for shift in range(1, size):
        found.append(lax.ppermute(value, axis, [(k, (k + shift) % size) for k in range(size)]))
    return found


def spread(value, me, size):
    if size != 4:
        others = from_others(value, "tok")
        return [((me - s) % size, 0, part) for s, part in enumerate(others)]

    def swap(part, mask):
        return lax.ppermute(part, "tok", [(k, k ^ mask) for k in range(4)])

    half = value.shape[0] // 2
    upper, lower = value[:half], value[half:]
    upper1, lower1 = swap(upper, 1), swap(lower, 1)
    upper2, lower2 = swap(upper, 2), swap(lower, 2)
    upper3, lower3 = swap(upper1, 2), swap(lower2, 1)
    return [
        (me, 0, value),
        (me ^ 1, 0, upper1),
        (me ^ 1, half, lower1),
        (me ^ 2, 0, upper2),
        (me ^ 2, half, lower2),
        (me ^ 3, 0, upper3),
        (me ^ 3, half, lower3),
    ]


def local(tokens, centroids):
    tok_size = lax.axis_size("tok")
    me = lax.axis_index("tok")
    cent_count, width = centroids.shape
    share_rows = cent_count // tok_size

    toks = from_others(tokens, "tok")
    own_lse = combined_lse(from_others(local_lse(tokens, centroids), "cent"))
    lses = from_others(own_lse, "tok")

    chunks = 4
    while share_rows % (chunks * 256):
        chunks //= 2
    rows = share_rows // chunks
    updated = blank((cent_count, width))
    masses = []
    for k in range(chunks):
        place = (k * tok_size + me).reshape(1)
        new, mass = updated_chunk(place, toks, lses, centroids, rows)
        for shift, first, part in spread(new.astype(jnp.float16), me, tok_size):
            start = (k * tok_size + shift) * rows + first
            updated = lax.dynamic_update_slice(updated, part.astype(jnp.float32), (start, 0))
        masses.append(mass.reshape(1, 1, rows // 128, 128))
    found = from_others(jnp.concatenate(masses), "tok")
    index = lax.broadcasted_iota(jnp.int32, (1, tok_size, 1, 1), 1)
    source = (me - index) % tok_size
    all_masses = found[0]
    for s in range(1, tok_size):
        all_masses = jnp.where(source == s, found[s], all_masses)
    return updated, all_masses.reshape(cent_count)


def solution(mesh):
    placed = (P("tok", None), P("cent", None))
    return jax.shard_map(
        local, mesh=mesh, in_specs=placed, out_specs=(P("cent", None), P("cent")), check_vma=False
    )
```

```python
import functools

import jax
import jax.numpy as jnp
from jax import lax
from jax.experimental import pallas as pl
from jax.experimental.pallas import tpu as pltpu
from jax.sharding import PartitionSpec as P

inverse_temp = 2.0
prior_weight = 0.05
safe_sum = 1e30
code_scale = 2.0**18
vmem_bytes = 56 * 1024 * 1024


def divisor(count, most):
    size = min(count, most)
    while count % size:
        size //= 2
    return size


def dot_nt(a, b):
    return lax.dot_general(a, b, (((1,), (1,)), ((), ())), preferred_element_type=jnp.float32)


def fold_rows(x, combine):
    parts = [x[k * 8 : (k + 1) * 8, :] for k in range(x.shape[0] // 8)]
    while len(parts) > 1:
        half = len(parts) // 2
        parts = [combine(parts[2 * k], parts[2 * k + 1]) for k in range(half)] + parts[2 * half :]
    return parts[0]


def stats_kernel(sub_rows, tok_cols, tok_ref, cent_ref, out_ref, flip_ref, base_ref, shift_ref, sums_ref):
    step = pl.program_id(0)
    tok_count = tok_ref.shape[0]
    tile = divisor(sub_rows, 1024)
    subs = cent_ref.shape[0] // sub_rows
    col_blocks = tok_count // tok_cols

    def columns(t):
        return pl.ds(pl.multiple_of(t * tok_cols, tok_cols), tok_cols)

    def dot(a, b):
        return jnp.dot(a, b, preferred_element_type=jnp.float32)

    @pl.when(step == 0)
    def _():
        @pl.loop(0, col_blocks)
        def _(t):
            flipped = (tok_ref[columns(t), :] * jnp.bfloat16(inverse_temp)).T
            flip_ref[:, columns(t)] = flipped
            logits = dot(cent_ref[0:128, :], flipped)
            top = jnp.max(fold_rows(logits, jnp.maximum), axis=0, keepdims=True)
            base_ref[:, columns(t)] = top

    @pl.loop(0, col_blocks)
    def _(t):
        rhs = flip_ref[:, columns(t)]
        shift = base_ref[:, columns(t)]
        for sub in range(subs):
            total = jnp.zeros((8, tok_cols), jnp.float32)
            for k in range(sub_rows // tile):
                logits = dot(cent_ref[pl.ds(sub * sub_rows + k * tile, tile), :], rhs)
                total = total + fold_rows(jnp.exp(logits - shift), jnp.add)
            sums_ref[step * subs + sub, :, columns(t)] = total
            shift_ref[step * subs + sub, :, columns(t)] = shift

    worst = jnp.max(sums_ref[pl.ds(step * subs, subs), :, :])

    @pl.when(jnp.logical_not(worst < safe_sum))
    def _():
        @pl.loop(0, col_blocks)
        def _(t):
            worst_t = jnp.max(sums_ref[pl.ds(step * subs, subs), :, columns(t)])

            @pl.when(jnp.logical_not(worst_t < safe_sum))
            def _():
                @pl.loop(0, subs)
                def _(sub):
                    worst_s = jnp.max(sums_ref[step * subs + sub, :, columns(t)])

                    @pl.when(jnp.logical_not(worst_s < safe_sum))
                    def _():
                        rhs = flip_ref[:, columns(t)]
                        lowest = base_ref[:, columns(t)]

                        def logits_of(k):
                            first = pl.multiple_of(sub * sub_rows + k * tile, tile)
                            return dot(cent_ref[pl.ds(first, tile), :], rhs)

                        def raise_top(k, top):
                            return jnp.maximum(top, fold_rows(logits_of(k), jnp.maximum))

                        top = lax.fori_loop(
                            0, sub_rows // tile, raise_top, jnp.broadcast_to(lowest, (8, tok_cols))
                        )
                        top = jnp.max(top, axis=0, keepdims=True)

                        def add_up(k, total):
                            return total + fold_rows(jnp.exp(logits_of(k) - top), jnp.add)

                        total = lax.fori_loop(
                            0, sub_rows // tile, add_up, jnp.zeros((8, tok_cols), jnp.float32)
                        )
                        sums_ref[step * subs + sub, :, columns(t)] = total
                        shift_ref[step * subs + sub, :, columns(t)] = top

    @pl.when(step == pl.num_programs(0) - 1)
    def _():
        @pl.loop(0, col_blocks)
        def _(t):
            shifts = shift_ref[:, :, columns(t)]
            top = jnp.max(shifts, axis=0)
            scale = jnp.exp(shifts - top[None])
            total = jnp.sum(sums_ref[:, :, columns(t)] * scale, axis=0)
            total = jnp.sum(total, axis=0, keepdims=True)
            out_ref[:, columns(t)] = top + jnp.log(total)


def local_lse(tokens, centroids):
    tok_count, width = tokens.shape
    cent_count = centroids.shape[0]
    block_rows = divisor(cent_count, 4096)
    sub_rows = divisor(block_rows, 1024)
    tok_cols = divisor(tok_count, 512)
    blocks = cent_count // block_rows
    subs = cent_count // sub_rows
    return pl.pallas_call(
        functools.partial(stats_kernel, sub_rows, tok_cols),
        grid=(blocks,),
        in_specs=[
            pl.BlockSpec((tok_count, width), lambda j: (0, 0)),
            pl.BlockSpec((block_rows, width), lambda j: (j, 0)),
        ],
        out_specs=pl.BlockSpec((1, tok_count), lambda j: (0, 0)),
        out_shape=jax.ShapeDtypeStruct((1, tok_count), jnp.float32),
        scratch_shapes=[
            pltpu.VMEM((width, tok_count), jnp.bfloat16),
            pltpu.VMEM((1, tok_count), jnp.float32),
            pltpu.VMEM((subs, 1, tok_count), jnp.float32),
            pltpu.VMEM((subs, 8, tok_count), jnp.float32),
        ],
        compiler_params=pltpu.CompilerParams(vmem_limit_bytes=vmem_bytes),
        cost_estimate=pl.CostEstimate(
            flops=2 * tok_count * cent_count * width,
            bytes_accessed=(tok_count + cent_count) * width * 2,
            transcendentals=tok_count * cent_count,
        ),
        name="row_stats",
    )(tokens, centroids)


def encoded(x):
    x = x * code_scale
    square = x * x
    return (square * square * x).astype(jnp.bfloat16)


def decoded(code):
    code = code.astype(jnp.float32)
    size = jnp.exp2(jnp.log2(jnp.abs(code)) * 0.2) * (1.0 / code_scale)
    return jnp.where(code < 0, -size, size)


def update_kernel(shards, place_ref, *refs):
    tok_refs, lse_refs = refs[:shards], refs[shards : 2 * shards]
    cent_ref, new_ref, mass_ref, toks_ref, lses_ref, weights_ref, total_ref, sems = refs[2 * shards :]
    rows, width = cent_ref.shape
    shard_rows = tok_refs[0].shape[0]
    depth = weights_ref.shape[2]
    pieces = shards * shard_rows // depth
    piece = divisor(depth, 512)

    @pl.when(pl.program_id(0) == 0)
    def _():
        copies = []
        for s in range(shards):
            span = pl.ds(s * shard_rows, shard_rows)
            copies.append(pltpu.make_async_copy(tok_refs[s], toks_ref.at[span, :], sems.at[2 * s]))
            copies.append(pltpu.make_async_copy(lse_refs[s], lses_ref.at[:, span], sems.at[2 * s + 1]))
        for copy in copies:
            copy.start()
        for copy in copies:
            copy.wait()

    cents = cent_ref[...] * jnp.bfloat16(inverse_temp)

    def weigh(n):
        for k in range(depth // piece):
            span = pl.ds(pl.multiple_of(n * depth + k * piece, piece), piece)
            logits = dot_nt(cents, toks_ref[span, :])
            weights = jnp.exp(logits - lses_ref[:, span])
            weights_ref[lax.rem(n, 2), :, pl.ds(k * piece, piece)] = weights.astype(jnp.bfloat16)

    def gather_up(n):
        toks = toks_ref[pl.ds(pl.multiple_of(n * depth, depth), depth), :]
        rhs = jnp.concatenate([toks, jnp.ones_like(toks)], axis=1)
        return jnp.dot(weights_ref[lax.rem(n, 2)], rhs, preferred_element_type=jnp.float32)

    weigh(0)
    total_ref[...] = jnp.zeros_like(total_ref)

    @pl.loop(1, pieces)
    def _(n):
        weigh(n)
        total_ref[...] += gather_up(n - 1)

    total = total_ref[...] + gather_up(pieces - 1)
    mass = total[:, width:]
    prior = prior_weight * cent_ref[...].astype(jnp.float32)
    new_ref[...] = encoded((total[:, :width] + prior) / (mass + prior_weight))
    diagonal = lax.broadcasted_iota(jnp.int32, (128, 128), 0) == lax.broadcasted_iota(
        jnp.int32, (128, 128), 1
    )
    for k in range(rows // 128):
        square = jnp.where(diagonal, mass[k * 128 : (k + 1) * 128, :], 0.0)
        mass_ref[k] = jnp.sum(square, axis=0, keepdims=True)


def updated_chunk(block, toks, lses, centroids, rows, block_rows):
    shards = len(toks)
    shard_rows, width = toks[0].shape
    all_count = shards * shard_rows
    depth = divisor(all_count, 1024)
    anywhere = pl.BlockSpec(memory_space=pl.ANY)
    return pl.pallas_call(
        functools.partial(update_kernel, shards),
        grid_spec=pltpu.PrefetchScalarGridSpec(
            num_scalar_prefetch=1,
            grid=(rows // block_rows,),
            in_specs=[anywhere] * (2 * shards)
            + [pl.BlockSpec((block_rows, width), lambda j, place: (place[0] + j, 0))],
            out_specs=[
                pl.BlockSpec((block_rows, width), lambda j, place: (j, 0)),
                pl.BlockSpec((block_rows // 128, 1, 128), lambda j, place: (j, 0, 0)),
            ],
            scratch_shapes=[
                pltpu.VMEM((all_count, width), jnp.bfloat16),
                pltpu.VMEM((1, all_count), jnp.float32),
                pltpu.VMEM((2, block_rows, depth), jnp.bfloat16),
                pltpu.VMEM((block_rows, 2 * width), jnp.float32),
                pltpu.SemaphoreType.DMA((2 * shards,)),
            ],
        ),
        out_shape=[
            jax.ShapeDtypeStruct((rows, width), jnp.bfloat16),
            jax.ShapeDtypeStruct((rows // 128, 1, 128), jnp.float32),
        ],
        compiler_params=pltpu.CompilerParams(vmem_limit_bytes=vmem_bytes),
        cost_estimate=pl.CostEstimate(
            flops=6 * all_count * rows * width,
            bytes_accessed=(2 * all_count + 4 * rows) * width,
            transcendentals=all_count * rows,
        ),
        name="new_rows",
    )(block, *toks, *lses, centroids)


def place_kernel(code_ref, base_ref, out_ref):
    out_ref[...] = decoded(code_ref[...])


def placed_rows(base, codes, first):
    rows, width = codes.shape
    block_rows = divisor(rows, 2048)
    while first % block_rows:
        block_rows //= 2
    offset = first // block_rows
    return pl.pallas_call(
        place_kernel,
        grid=(rows // block_rows,),
        in_specs=[
            pl.BlockSpec((block_rows, width), lambda j: (j, 0)),
            pl.BlockSpec(memory_space=pl.ANY),
        ],
        out_specs=pl.BlockSpec((block_rows, width), lambda j: (offset + j, 0)),
        out_shape=jax.ShapeDtypeStruct(base.shape, base.dtype),
        input_output_aliases={1: 0},
        compiler_params=pltpu.CompilerParams(vmem_limit_bytes=vmem_bytes),
        cost_estimate=pl.CostEstimate(
            flops=10 * rows * width, bytes_accessed=6 * rows * width, transcendentals=2 * rows * width
        ),
        name="placed_rows",
    )(codes, base)


def combine_kernel(*refs):
    parts, out_ref = [ref[...] for ref in refs[:-1]], refs[-1]
    top = functools.reduce(jnp.maximum, parts)
    out_ref[...] = top + jnp.log(sum(jnp.exp(part - top) for part in parts))


def combined_lse(parts):
    return pl.pallas_call(
        combine_kernel, out_shape=jax.ShapeDtypeStruct(parts[0].shape, jnp.float32), name="join_stats"
    )(*parts)


def blank(shape):
    return pl.pallas_call(
        lambda out_ref: None,
        out_specs=pl.BlockSpec(memory_space=pl.ANY),
        out_shape=jax.ShapeDtypeStruct(shape, jnp.float32),
        name="blank",
    )()


def from_others(value, axis):
    size = lax.axis_size(axis)
    found = [value]
    for shift in range(1, size):
        found.append(lax.ppermute(value, axis, [(k, (k + shift) % size) for k in range(size)]))
    return found


def chunk_plan(share_rows, block_rows):
    blocks = share_rows // block_rows
    plan = []
    while blocks > 2:
        plan.append(2)
        blocks -= 2
    return plan + [1] * blocks


def local(tokens, centroids):
    tok_size = lax.axis_size("tok")
    me = lax.axis_index("tok")
    cent_count, width = centroids.shape
    share_rows = cent_count // tok_size

    toks = from_others(tokens, "tok")
    own_lse = combined_lse(from_others(local_lse(tokens, centroids), "cent"))
    lses = from_others(own_lse, "tok")

    block_rows = divisor(share_rows, 1024)
    updated = blank((cent_count, width))
    masses, first = [], 0
    for blocks in chunk_plan(share_rows, block_rows):
        block = first * tok_size + me * blocks
        rows = blocks * block_rows
        codes, mass = updated_chunk(block.reshape(1), toks, lses, centroids, rows, block_rows)
        codes = lax.all_gather(codes, "tok", axis=0, tiled=True)
        updated = placed_rows(updated, codes, first * tok_size * block_rows)
        masses.append(mass.reshape(rows // 128, 128))
        first += blocks
    found = from_others(jnp.concatenate(masses), "tok")
    parts, done = [], 0
    for mass in masses:
        count = mass.shape[0]
        index = lax.broadcasted_iota(jnp.int32, (tok_size, 1, 1), 0)
        source = (me - index) % tok_size
        part = found[0][None, done : done + count]
        for s in range(1, tok_size):
            part = jnp.where(source == s, found[s][None, done : done + count], part)
        parts.append(part.reshape(tok_size * count, 128))
        done += count
    return updated, jnp.concatenate(parts).reshape(cent_count)


def solution(mesh):
    placed = (P("tok", None), P("cent", None))
    return jax.shard_map(
        local, mesh=mesh, in_specs=placed, out_specs=(P("cent", None), P("cent")), check_vma=False
    )
```

```python
import functools

import jax
import jax.numpy as jnp
from jax import lax
from jax.experimental import pallas as pl
from jax.experimental.pallas import tpu as pltpu
from jax.sharding import PartitionSpec as P

inverse_temp = 2.0
prior_weight = 0.05
safe_sum = 1e30
code_scale = 2.0**24
group_rows = 128
unit_size = 256
vmem_bytes = 56 * 1024 * 1024


def divisor(count, most):
    size = min(count, most)
    while count % size:
        size //= 2
    return size


def widened(x):
    return jnp.concatenate([x, jnp.zeros_like(x)], axis=1)


def fold_rows(x, combine):
    parts = [x[k * 8 : (k + 1) * 8, :] for k in range(x.shape[0] // 8)]
    while len(parts) > 1:
        half = len(parts) // 2
        parts = [combine(parts[2 * k], parts[2 * k + 1]) for k in range(half)] + parts[2 * half :]
    return parts[0]


def stats_kernel(sub_rows, tok_cols, tok_ref, cent_ref, out_ref, base_ref, shift_ref, sums_ref):
    step = pl.program_id(0)
    tok_count = tok_ref.shape[0]
    subs = cent_ref.shape[0] // sub_rows
    groups = sub_rows // group_rows
    col_blocks = tok_count // tok_cols
    units = tok_cols // unit_size

    def columns(t):
        return pl.ds(pl.multiple_of(t * tok_cols, tok_cols), tok_cols)

    def unit_columns(t, unit):
        return pl.ds(pl.multiple_of(t * tok_cols + unit * unit_size, unit_size), unit_size)

    def main(*accs):
        accs = [accs[unit * groups : (unit + 1) * groups] for unit in range(units)]

        def load_tokens(t):
            for unit in range(units):
                toks = tok_ref[unit_columns(t, unit), :] * jnp.bfloat16(inverse_temp)
                pltpu.matmul_push_rhs(widened(toks), 0, unit, transpose=True)

        def product(first, g, load):
            lhs = widened(cent_ref[pl.ds(first, group_rows), :])
            for unit in range(units):
                pltpu.matmul_acc_lhs(accs[unit][g], lhs, 0 if load else None)

        def logits_at(t, first):
            load_tokens(t)
            product(first, 0, True)
            return [pltpu.matmul_pop(accs[unit][0]) for unit in range(units)]

        @pl.when(step == 0)
        def _():
            @pl.loop(0, col_blocks)
            def _(t):
                for unit, logits in enumerate(logits_at(t, 0)):
                    top = jnp.max(fold_rows(logits, jnp.maximum), axis=0, keepdims=True)
                    base_ref[:, unit_columns(t, unit)] = top

        @pl.loop(0, col_blocks)
        def _(t):
            load_tokens(t)
            shifts = [base_ref[:, unit_columns(t, unit)] for unit in range(units)]
            for g in range(groups):
                product(g * group_rows, g, g == 0)
            for sub in range(subs):
                totals = [jnp.zeros((8, unit_size), jnp.float32)] * units
                for g in range(groups):
                    logits = [pltpu.matmul_pop(accs[unit][g]) for unit in range(units)]
                    if sub + 1 < subs:
                        product((sub + 1) * sub_rows + g * group_rows, g, False)
                    for unit in range(units):
                        scaled = jnp.exp(logits[unit] - shifts[unit])
                        totals[unit] = totals[unit] + fold_rows(scaled, jnp.add)
                for unit in range(units):
                    sums_ref[step * subs + sub, :, unit_columns(t, unit)] = totals[unit]
                    shift_ref[step * subs + sub, :, unit_columns(t, unit)] = shifts[unit]

        def redo(t, sub):
            def first_row(k):
                return pl.multiple_of(sub * sub_rows + k * group_rows, group_rows)

            def raise_tops(k, tops):
                parts = logits_at(t, first_row(k))
                return [jnp.maximum(top, fold_rows(part, jnp.maximum)) for top, part in zip(tops, parts)]

            lowest = [base_ref[:, unit_columns(t, unit)] for unit in range(units)]
            tops = [jnp.broadcast_to(low, (8, unit_size)) for low in lowest]
            tops = lax.fori_loop(0, groups, raise_tops, tops)
            tops = [jnp.max(top, axis=0, keepdims=True) for top in tops]

            def add_up(k, totals):
                parts = logits_at(t, first_row(k))
                return [
                    total + fold_rows(jnp.exp(part - top), jnp.add)
                    for total, part, top in zip(totals, parts, tops)
                ]

            totals = [jnp.zeros((8, unit_size), jnp.float32)] * units
            totals = lax.fori_loop(0, groups, add_up, totals)
            for unit in range(units):
                sums_ref[step * subs + sub, :, unit_columns(t, unit)] = totals[unit]
                shift_ref[step * subs + sub, :, unit_columns(t, unit)] = tops[unit]

        worst = jnp.max(sums_ref[pl.ds(step * subs, subs), :, :])

        @pl.when(jnp.logical_not(worst < safe_sum))
        def _():
            @pl.loop(0, col_blocks)
            def _(t):
                worst_t = jnp.max(sums_ref[pl.ds(step * subs, subs), :, columns(t)])

                @pl.when(jnp.logical_not(worst_t < safe_sum))
                def _():
                    @pl.loop(0, subs)
                    def _(sub):
                        worst_s = jnp.max(sums_ref[step * subs + sub, :, columns(t)])

                        @pl.when(jnp.logical_not(worst_s < safe_sum))
                        def _():
                            redo(t, sub)

    accs = [
        pltpu.ACC(unit)((group_rows, unit_size), jnp.float32) for unit in range(units) for _ in range(groups)
    ]
    pl.run_scoped(main, *accs)

    @pl.when(step == pl.num_programs(0) - 1)
    def _():
        @pl.loop(0, col_blocks)
        def _(t):
            shifts = shift_ref[:, :, columns(t)]
            top = jnp.max(shifts, axis=0)
            scale = jnp.exp(shifts - top[None])
            total = jnp.sum(sums_ref[:, :, columns(t)] * scale, axis=0)
            total = jnp.sum(total, axis=0, keepdims=True)
            out_ref[:, columns(t)] = top + jnp.log(total)


def local_lse(tokens, centroids):
    tok_count, width = tokens.shape
    cent_count = centroids.shape[0]
    block_rows = divisor(cent_count, 4096)
    sub_rows = divisor(block_rows, 1024)
    tok_cols = divisor(tok_count, 512)
    blocks = cent_count // block_rows
    subs = cent_count // sub_rows
    return pl.pallas_call(
        functools.partial(stats_kernel, sub_rows, tok_cols),
        grid=(blocks,),
        in_specs=[
            pl.BlockSpec((tok_count, width), lambda j: (0, 0)),
            pl.BlockSpec((block_rows, width), lambda j: (j, 0)),
        ],
        out_specs=pl.BlockSpec((1, tok_count), lambda j: (0, 0)),
        out_shape=jax.ShapeDtypeStruct((1, tok_count), jnp.float32),
        scratch_shapes=[
            pltpu.VMEM((1, tok_count), jnp.float32),
            pltpu.VMEM((subs, 1, tok_count), jnp.float32),
            pltpu.VMEM((subs, 8, tok_count), jnp.float32),
        ],
        compiler_params=pltpu.CompilerParams(vmem_limit_bytes=vmem_bytes),
        cost_estimate=pl.CostEstimate(
            flops=2 * tok_count * cent_count * width,
            bytes_accessed=(tok_count + cent_count) * width * 2,
            transcendentals=tok_count * cent_count,
        ),
        name="row_stats",
    )(tokens, centroids)


def encoded(x):
    x = x * code_scale
    return (x * jnp.abs(x) * (x * x)).astype(jnp.bfloat16)


def decoded(code):
    code = code.astype(jnp.float32)
    size = lax.rsqrt(lax.rsqrt(jnp.maximum(jnp.abs(code), 1e-37))) * (1.0 / code_scale)
    return jnp.where(code < 0, -size, jnp.where(code > 0, size, 0.0))


def update_kernel(shards, place_ref, *refs):
    tok_refs, lse_refs = refs[:shards], refs[shards : 2 * shards]
    cent_ref, new_ref, mass_ref, toks_ref, lses_ref, sems = refs[2 * shards :]
    rows, width = cent_ref.shape
    shard_rows = tok_refs[0].shape[0]
    groups = rows // group_rows
    pieces = shards * shard_rows // unit_size
    run = divisor(pieces, 4)

    @pl.when(pl.program_id(0) == 0)
    def _():
        copies = []
        for s in range(shards):
            span = pl.ds(s * shard_rows, shard_rows)
            copies.append(pltpu.make_async_copy(tok_refs[s], toks_ref.at[span, :], sems.at[2 * s]))
            copies.append(pltpu.make_async_copy(lse_refs[s], lses_ref.at[:, span], sems.at[2 * s + 1]))
        for copy in copies:
            copy.start()
        for copy in copies:
            copy.wait()

    def rows_of(g):
        return pl.ds(g * group_rows, group_rows)

    def tokens_of(n):
        return toks_ref[pl.ds(pl.multiple_of(n * unit_size, unit_size), unit_size), :]

    def main(*accs):
        logit_accs, sum_accs = accs[:groups], accs[groups:]

        def product(g):
            lhs = widened(cent_ref[rows_of(g), :] * jnp.bfloat16(inverse_temp))
            pltpu.matmul_acc_lhs(logit_accs[g], lhs, 0 if g == 0 else None)

        def load_logit_tokens(n):
            pltpu.matmul_push_rhs(widened(tokens_of(n)), 0, 0, transpose=True)

        def step(n, last):
            toks = tokens_of(n)
            pltpu.matmul_push_rhs(jnp.concatenate([toks, jnp.ones_like(toks)], axis=1), 0, 1)
            if not last:
                load_logit_tokens(n + 1)
            lse = lses_ref[:, pl.ds(pl.multiple_of(n * unit_size, unit_size), unit_size)]
            for g in range(groups):
                logits = pltpu.matmul_pop(logit_accs[g])
                if not last:
                    product(g)
                weights = jnp.exp(logits - lse).astype(jnp.bfloat16)
                pltpu.matmul_acc_lhs(sum_accs[g], weights, 0 if g == 0 else None)

        load_logit_tokens(0)
        for g in range(groups):
            product(g)

        @pl.loop(0, pieces // run - 1)
        def _(n):
            for k in range(run):
                step(n * run + k, False)

        for k in range(run):
            step(pieces - run + k, k == run - 1)

        diagonal = lax.broadcasted_iota(jnp.int32, (128, 128), 0) == lax.broadcasted_iota(
            jnp.int32, (128, 128), 1
        )
        for g in range(groups):
            total = pltpu.matmul_pop(sum_accs[g])
            mass = total[:, width:]
            prior = prior_weight * cent_ref[rows_of(g), :].astype(jnp.float32)
            new_ref[rows_of(g), :] = encoded((total[:, :width] + prior) / (mass + prior_weight))
            mass_ref[g] = jnp.sum(jnp.where(diagonal, mass, 0.0), axis=0, keepdims=True)

    accs = [pltpu.ACC(unit)((group_rows, 2 * width), jnp.float32) for unit in range(2) for _ in range(groups)]
    pl.run_scoped(main, *accs)


def updated_chunk(block, toks, lses, centroids, rows, block_rows):
    shards = len(toks)
    shard_rows, width = toks[0].shape
    all_count = shards * shard_rows
    anywhere = pl.BlockSpec(memory_space=pl.ANY)
    return pl.pallas_call(
        functools.partial(update_kernel, shards),
        grid_spec=pltpu.PrefetchScalarGridSpec(
            num_scalar_prefetch=1,
            grid=(rows // block_rows,),
            in_specs=[anywhere] * (2 * shards)
            + [pl.BlockSpec((block_rows, width), lambda j, place: (place[0] + j, 0))],
            out_specs=[
                pl.BlockSpec((block_rows, width), lambda j, place: (j, 0)),
                pl.BlockSpec((block_rows // 128, 1, 128), lambda j, place: (j, 0, 0)),
            ],
            scratch_shapes=[
                pltpu.VMEM((all_count, width), jnp.bfloat16),
                pltpu.VMEM((1, all_count), jnp.float32),
                pltpu.SemaphoreType.DMA((2 * shards,)),
            ],
        ),
        out_shape=[
            jax.ShapeDtypeStruct((rows, width), jnp.bfloat16),
            jax.ShapeDtypeStruct((rows // 128, 1, 128), jnp.float32),
        ],
        compiler_params=pltpu.CompilerParams(vmem_limit_bytes=vmem_bytes),
        cost_estimate=pl.CostEstimate(
            flops=6 * all_count * rows * width,
            bytes_accessed=(2 * all_count + 4 * rows) * width,
            transcendentals=all_count * rows,
        ),
        name="new_rows",
    )(block, *toks, *lses, centroids)


def place_kernel(place_ref, *refs):
    code_refs, out_ref = refs[:-2], refs[-1]
    for s, code_ref in enumerate(code_refs):

        @pl.when(pl.program_id(0) == s)
        def _():
            out_ref[...] = decoded(code_ref[...])


def placed_rows(base, codes, places, block_rows):
    rows, width = codes[0].shape
    blocks = rows // block_rows

    def spec(s):
        def index(q, j, place):
            return jnp.where(q == s, j, jnp.where(q < s, 0, blocks - 1)), 0

        return pl.BlockSpec((block_rows, width), index)

    return pl.pallas_call(
        place_kernel,
        grid_spec=pltpu.PrefetchScalarGridSpec(
            num_scalar_prefetch=1,
            grid=(len(codes), blocks),
            in_specs=[spec(s) for s in range(len(codes))] + [pl.BlockSpec(memory_space=pl.ANY)],
            out_specs=pl.BlockSpec((block_rows, width), lambda q, j, place: (place[q] + j, 0)),
        ),
        out_shape=jax.ShapeDtypeStruct(base.shape, base.dtype),
        input_output_aliases={1 + len(codes): 0},
        compiler_params=pltpu.CompilerParams(vmem_limit_bytes=vmem_bytes),
        cost_estimate=pl.CostEstimate(
            flops=10 * rows * width, bytes_accessed=6 * rows * width, transcendentals=2 * rows * width
        ),
        name="placed_rows",
    )(places, *codes, base)


def combine_kernel(*refs):
    parts, out_ref = [ref[...] for ref in refs[:-1]], refs[-1]
    top = functools.reduce(jnp.maximum, parts)
    out_ref[...] = top + jnp.log(sum(jnp.exp(part - top) for part in parts))


def combined_lse(parts):
    return pl.pallas_call(
        combine_kernel, out_shape=jax.ShapeDtypeStruct(parts[0].shape, jnp.float32), name="join_stats"
    )(*parts)


def blank(shape):
    return pl.pallas_call(
        lambda out_ref: None,
        out_specs=pl.BlockSpec(memory_space=pl.ANY),
        out_shape=jax.ShapeDtypeStruct(shape, jnp.float32),
        name="blank",
    )()


def from_others(value, axis):
    size = lax.axis_size(axis)
    found = [value]
    for s in range(1, size):
        pairs = [(partner(k, s, size), k) for k in range(size)]
        found.append(lax.ppermute(value, axis, pairs))
    return found


def partner(me, s, size):
    return me ^ s if size & (size - 1) == 0 else (me - s) % size


def chunk_plan(blocks):
    plan = []
    while blocks:
        plan.append(max(1, (3 * blocks + 3) // 8))
        blocks -= plan[-1]
    return plan


def local(tokens, centroids):
    tok_size = lax.axis_size("tok")
    me = lax.axis_index("tok")
    cent_count, width = centroids.shape
    share_rows = cent_count // tok_size

    toks = from_others(tokens, "tok")
    own_lse = combined_lse(from_others(local_lse(tokens, centroids), "cent"))
    lses = from_others(own_lse, "tok")

    block_rows = divisor(share_rows, 1024)
    updated = blank((cent_count, width))
    masses, first = [], 0
    sources = jnp.stack([partner(me, s, tok_size) for s in range(tok_size)]).astype(jnp.int32)
    for blocks in chunk_plan(share_rows // block_rows):
        block = first * tok_size + me * blocks
        rows = blocks * block_rows
        codes, mass = updated_chunk(block.reshape(1), toks, lses, centroids, rows, block_rows)
        starts = first * tok_size + sources * blocks
        updated = placed_rows(updated, from_others(codes, "tok"), starts, block_rows)
        masses.append(mass.reshape(rows // 128, 128))
        first += blocks
    found = from_others(jnp.concatenate(masses), "tok")
    parts, done = [], 0
    for mass in masses:
        count = mass.shape[0]
        index = lax.broadcasted_iota(jnp.int32, (tok_size, 1, 1), 0)
        source = partner(me, index, tok_size)
        part = found[0][None, done : done + count]
        for s in range(1, tok_size):
            part = jnp.where(source == s, found[s][None, done : done + count], part)
        parts.append(part.reshape(tok_size * count, 128))
        done += count
    return updated, jnp.concatenate(parts).reshape(cent_count)


def solution(mesh):
    placed = (P("tok", None), P("cent", None))
    return jax.shard_map(
        local, mesh=mesh, in_specs=placed, out_specs=(P("cent", None), P("cent")), check_vma=False
    )
```

```python
import functools

import jax
import jax.numpy as jnp
from jax import lax
from jax.experimental import pallas as pl
from jax.experimental.pallas import tpu as pltpu
from jax.sharding import PartitionSpec as P

inverse_temp = 2.0
prior_weight = 0.05
safe_sum = 1e30
code_scale = 2.0**24
slice_rows = 64
vmem_bytes = 56 * 1024 * 1024


def divisor(count, most):
    size = min(count, most)
    while count % size:
        size //= 2
    return size


def dot_nt(a, b):
    return lax.dot_general(a, b, (((1,), (1,)), ((), ())), preferred_element_type=jnp.float32)


def fold_rows(x, combine):
    parts = [x[k * 8 : (k + 1) * 8, :] for k in range(x.shape[0] // 8)]
    while len(parts) > 1:
        half = len(parts) // 2
        parts = [combine(parts[2 * k], parts[2 * k + 1]) for k in range(half)] + parts[2 * half :]
    return parts[0]


def stats_kernel(sub_rows, tok_cols, tok_ref, cent_ref, out_ref, flip_ref, base_ref, shift_ref, sums_ref):
    step = pl.program_id(0)
    tok_count = tok_ref.shape[0]
    tile = divisor(sub_rows, 1024)
    subs = cent_ref.shape[0] // sub_rows
    col_blocks = tok_count // tok_cols

    def columns(t):
        return pl.ds(pl.multiple_of(t * tok_cols, tok_cols), tok_cols)

    def dot(a, b):
        return jnp.dot(a, b, preferred_element_type=jnp.float32)

    @pl.when(step == 0)
    def _():
        @pl.loop(0, col_blocks)
        def _(t):
            flipped = (tok_ref[columns(t), :] * jnp.bfloat16(inverse_temp)).T
            flip_ref[:, columns(t)] = flipped
            logits = dot(cent_ref[0:128, :], flipped)
            top = jnp.max(fold_rows(logits, jnp.maximum), axis=0, keepdims=True)
            base_ref[:, columns(t)] = top

    @pl.loop(0, col_blocks)
    def _(t):
        rhs = flip_ref[:, columns(t)]
        shift = base_ref[:, columns(t)]
        for sub in range(subs):
            total = jnp.zeros((8, tok_cols), jnp.float32)
            for k in range(sub_rows // tile):
                logits = dot(cent_ref[pl.ds(sub * sub_rows + k * tile, tile), :], rhs)
                for first in range(0, tile, slice_rows):
                    scaled = jnp.exp(logits[first : first + slice_rows] - shift)
                    total = total + fold_rows(scaled, jnp.add)
            sums_ref[step * subs + sub, :, columns(t)] = total
            shift_ref[step * subs + sub, :, columns(t)] = shift

    worst = jnp.max(sums_ref[pl.ds(step * subs, subs), :, :])

    @pl.when(jnp.logical_not(worst < safe_sum))
    def _():
        @pl.loop(0, col_blocks)
        def _(t):
            worst_t = jnp.max(sums_ref[pl.ds(step * subs, subs), :, columns(t)])

            @pl.when(jnp.logical_not(worst_t < safe_sum))
            def _():
                @pl.loop(0, subs)
                def _(sub):
                    worst_s = jnp.max(sums_ref[step * subs + sub, :, columns(t)])

                    @pl.when(jnp.logical_not(worst_s < safe_sum))
                    def _():
                        rhs = flip_ref[:, columns(t)]
                        lowest = base_ref[:, columns(t)]

                        def logits_of(k):
                            first = pl.multiple_of(sub * sub_rows + k * tile, tile)
                            return dot(cent_ref[pl.ds(first, tile), :], rhs)

                        def raise_top(k, top):
                            return jnp.maximum(top, fold_rows(logits_of(k), jnp.maximum))

                        top = lax.fori_loop(
                            0, sub_rows // tile, raise_top, jnp.broadcast_to(lowest, (8, tok_cols))
                        )
                        top = jnp.max(top, axis=0, keepdims=True)

                        def add_up(k, total):
                            return total + fold_rows(jnp.exp(logits_of(k) - top), jnp.add)

                        total = lax.fori_loop(
                            0, sub_rows // tile, add_up, jnp.zeros((8, tok_cols), jnp.float32)
                        )
                        sums_ref[step * subs + sub, :, columns(t)] = total
                        shift_ref[step * subs + sub, :, columns(t)] = top

    @pl.when(step == pl.num_programs(0) - 1)
    def _():
        @pl.loop(0, col_blocks)
        def _(t):
            shifts = shift_ref[:, :, columns(t)]
            top = jnp.max(shifts, axis=0)
            scale = jnp.exp(shifts - top[None])
            total = jnp.sum(sums_ref[:, :, columns(t)] * scale, axis=0)
            total = jnp.sum(total, axis=0, keepdims=True)
            out_ref[:, columns(t)] = top + jnp.log(total)


def local_lse(tokens, centroids):
    tok_count, width = tokens.shape
    cent_count = centroids.shape[0]
    block_rows = divisor(cent_count, 4096)
    sub_rows = divisor(block_rows, 1024)
    tok_cols = divisor(tok_count, 512)
    blocks = cent_count // block_rows
    subs = cent_count // sub_rows
    return pl.pallas_call(
        functools.partial(stats_kernel, sub_rows, tok_cols),
        grid=(blocks,),
        in_specs=[
            pl.BlockSpec((tok_count, width), lambda j: (0, 0)),
            pl.BlockSpec((block_rows, width), lambda j: (j, 0)),
        ],
        out_specs=pl.BlockSpec((1, tok_count), lambda j: (0, 0)),
        out_shape=jax.ShapeDtypeStruct((1, tok_count), jnp.float32),
        scratch_shapes=[
            pltpu.VMEM((width, tok_count), jnp.bfloat16),
            pltpu.VMEM((1, tok_count), jnp.float32),
            pltpu.VMEM((subs, 1, tok_count), jnp.float32),
            pltpu.VMEM((subs, 8, tok_count), jnp.float32),
        ],
        compiler_params=pltpu.CompilerParams(vmem_limit_bytes=vmem_bytes),
        cost_estimate=pl.CostEstimate(
            flops=2 * tok_count * cent_count * width,
            bytes_accessed=(tok_count + cent_count) * width * 2,
            transcendentals=tok_count * cent_count,
        ),
        name="row_stats",
    )(tokens, centroids)


def encoded(x):
    x = x * code_scale
    return (x * jnp.abs(x) * (x * x)).astype(jnp.bfloat16)


def decoded(code):
    code = code.astype(jnp.float32)
    size = lax.rsqrt(lax.rsqrt(jnp.maximum(jnp.abs(code), 1e-37))) * (1.0 / code_scale)
    return jnp.where(code < 0, -size, jnp.where(code > 0, size, 0.0))


def split_exactly(x):
    high = x.astype(jnp.bfloat16).astype(jnp.float32)
    middle = (x - high).astype(jnp.bfloat16).astype(jnp.float32)
    return high, middle, x - high - middle


class Placing:
    def __init__(self, block_rows, starts_ref, code_refs, outs, scratch):
        self.block_rows, self.starts_ref, self.code_refs = block_rows, starts_ref, code_refs
        self.updated_ref, self.masses_ref = outs
        self.codes, self.values, self.masses, self.sems = scratch

    @staticmethod
    def scratch(sources, blocks, block_rows, width):
        return [
            pltpu.VMEM((sources, blocks * coded_rows(block_rows), width), jnp.bfloat16),
            pltpu.VMEM((sources, blocks * block_rows, width), jnp.float32),
            pltpu.VMEM((sources, blocks * block_rows // 128, 128), jnp.float32),
            pltpu.SemaphoreType.DMA((3, sources)),
        ]

    def copies_in(self):
        return [
            pltpu.make_async_copy(ref, self.codes.at[s], self.sems.at[0, s])
            for s, ref in enumerate(self.code_refs)
        ]

    def copies_out(self):
        found = []
        for s in range(len(self.code_refs)):
            rows, mass_rows = self.values.shape[1], self.masses.shape[1]
            start = self.starts_ref[s]
            span = pl.ds(pl.multiple_of(start * self.block_rows, self.block_rows), rows)
            found.append(
                pltpu.make_async_copy(self.values.at[s], self.updated_ref.at[span, :], self.sems.at[1, s])
            )
            per_block = self.block_rows // 128
            span = pl.ds(pl.multiple_of(start * per_block, per_block), mass_rows)
            found.append(
                pltpu.make_async_copy(self.masses.at[s], self.masses_ref.at[span, :], self.sems.at[2, s])
            )
        return found

    def fetch(self):
        for copy in self.copies_in():
            copy.start()

    def place(self):
        block_rows, per_block = self.block_rows, self.block_rows // 128
        full = coded_rows(block_rows)
        tile = divisor(block_rows, 256)
        for copy in self.copies_in():
            copy.wait()

        @pl.loop(0, len(self.code_refs))
        def _(s):
            for b in range(self.values.shape[1] // block_rows):

                @pl.loop(0, block_rows // tile)
                def _(k):
                    source = pl.ds(pl.multiple_of(b * full + k * tile, 16), tile)
                    target = pl.ds(pl.multiple_of(b * block_rows + k * tile, tile), tile)
                    self.values[s, target, :] = decoded(self.codes[s, source, :])

                terms = self.codes[s, b * full + block_rows : (b + 1) * full, :].astype(jnp.float32)
                mass = terms[:per_block] + terms[per_block : 2 * per_block]
                mass = mass + terms[2 * per_block : 3 * per_block]
                self.masses[s, b * per_block : (b + 1) * per_block, :] = mass

        for copy in self.copies_out():
            copy.start()

    def finish(self):
        for copy in self.copies_out():
            copy.wait()


def coded_rows(block_rows):
    return block_rows + block_rows // 32


def update_kernel(sources, block_rows, *refs):
    place_ref, tok_ref, lse_ref, cent_ref = refs[:4]
    code_refs, refs = refs[4 : 4 + sources], refs[4 + sources :]
    if sources:
        code_ref, updated_ref, masses_ref = refs[2:5]
        scratch = refs[5:]
        placing = Placing(block_rows, place_ref.at[pl.ds(1, sources)], code_refs, (updated_ref, masses_ref), scratch[3:])
    else:
        code_ref, scratch, placing = refs[0], refs[1:], None
    weights_ref, total_ref, mass_ref = scratch[:3]
    step, steps = pl.program_id(0), pl.num_programs(0)
    width = tok_ref.shape[1]
    _, tile, depth = weights_ref.shape
    piece = divisor(depth, 512)
    stages = tok_ref.shape[0] // depth
    tiles = block_rows // tile

    if placing:
        pl.when(step == 0)(placing.fetch)

    def weigh(first, stage):
        cents = cent_ref[pl.ds(first, tile), :] * jnp.bfloat16(inverse_temp)
        for k in range(depth // piece):
            span = pl.ds(stage * depth + k * piece, piece)
            logits = dot_nt(cents, tok_ref[span, :])
            lse = lse_ref[:, span]
            for r in range(0, tile, slice_rows):
                weights = jnp.exp(logits[r : r + slice_rows] - lse).astype(jnp.bfloat16)
                weights_ref[stage % 2, r : r + slice_rows, pl.ds(k * piece, piece)] = weights

    def gather_up(stage):
        toks = tok_ref[pl.ds(stage * depth, depth), :]
        rhs = jnp.concatenate([toks, jnp.ones_like(toks)], axis=1)
        part = jnp.dot(weights_ref[stage % 2], rhs, preferred_element_type=jnp.float32)
        if stage == 0:
            total_ref[...] = part
        else:
            total_ref[...] += part

    diagonal = lax.broadcasted_iota(jnp.int32, (128, 128), 0) == lax.broadcasted_iota(
        jnp.int32, (128, 128), 1
    )

    def run(r):
        first = pl.multiple_of(r * tile, tile)
        weigh(first, 0)
        for stage in range(1, stages):
            weigh(first, stage)
            gather_up(stage - 1)
        gather_up(stages - 1)
        mass = total_ref[:, width : 2 * width]
        prior = prior_weight * cent_ref[pl.ds(first, tile), :].astype(jnp.float32)
        new = (total_ref[:, 0:width] + prior) / (mass + prior_weight)
        code_ref[pl.ds(first, tile), :] = encoded(new)
        for k in range(tile // 128):
            square = jnp.where(diagonal, mass[k * 128 : (k + 1) * 128, :], 0.0)
            mass_ref[pl.ds(r * (tile // 128) + k, 1), :] = jnp.sum(square, axis=0, keepdims=True)

    pl.loop(0, tiles // 2)(run)
    if placing:
        pl.when(step == 0)(placing.place)
    pl.loop(tiles // 2, tiles)(run)

    terms = split_exactly(mass_ref[...])
    terms = jnp.concatenate([*terms, jnp.zeros_like(terms[0])], axis=0)
    code_ref[block_rows : block_rows + terms.shape[0], :] = terms.astype(jnp.bfloat16)
    if placing:
        pl.when(step == steps - 1)(placing.finish)


def updated_chunk(block, every_tok, lse, centroids, blocks, block_rows, received=None):
    all_count, width = every_tok.shape
    depth = divisor(all_count, 2048)
    tile = divisor(block_rows, 512)
    rows = blocks * block_rows
    full = coded_rows(block_rows)
    anywhere = pl.BlockSpec(memory_space=pl.ANY)
    whole = lambda j, place: (0, 0)
    place, operands = block.reshape(1), [every_tok, lse, centroids]
    in_specs = [
        pl.BlockSpec((all_count, width), whole),
        pl.BlockSpec((1, all_count), whole),
        pl.BlockSpec((block_rows, width), lambda j, place: (place[0] + j, 0)),
    ]
    out_specs = [pl.BlockSpec((full, width), lambda j, place: (j, 0))]
    out_shape = [jax.ShapeDtypeStruct((blocks * full, width), jnp.bfloat16)]
    scratch_shapes = [
        pltpu.VMEM((2, tile, depth), jnp.bfloat16),
        pltpu.VMEM((tile, 2 * width), jnp.float32),
        pltpu.VMEM((block_rows // 128, 128), jnp.float32),
    ]
    aliases, sources = {}, 0
    if received:
        codes, starts, outs = received
        sources = len(codes)
        place = jnp.concatenate([place, starts])
        operands += [*codes, *outs]
        in_specs += [anywhere] * (sources + 2)
        out_specs += [anywhere] * 2
        out_shape += [jax.ShapeDtypeStruct(out.shape, out.dtype) for out in outs]
        aliases = {4 + sources: 1, 5 + sources: 2}
        scratch_shapes += Placing.scratch(sources, codes[0].shape[0] // full, block_rows, width)
    return pl.pallas_call(
        functools.partial(update_kernel, sources, block_rows),
        grid_spec=pltpu.PrefetchScalarGridSpec(
            num_scalar_prefetch=1,
            grid=(blocks,),
            in_specs=in_specs,
            out_specs=out_specs,
            scratch_shapes=scratch_shapes,
        ),
        out_shape=out_shape,
        input_output_aliases=aliases,
        compiler_params=pltpu.CompilerParams(vmem_limit_bytes=vmem_bytes),
        cost_estimate=pl.CostEstimate(
            flops=6 * all_count * rows * width,
            bytes_accessed=(2 * all_count + 4 * rows) * width,
            transcendentals=all_count * rows,
        ),
        name="new_rows",
    )(place.astype(jnp.int32), *operands)


def place_kernel(sources, block_rows, starts_ref, *refs):
    code_refs, outs, scratch = refs[:sources], refs[sources + 2 : sources + 4], refs[sources + 4 :]
    placing = Placing(block_rows, starts_ref, code_refs, outs, scratch)
    placing.fetch()
    placing.place()
    placing.finish()


def placed(received, block_rows):
    codes, starts, outs = received
    sources, width = len(codes), codes[0].shape[1]
    anywhere = pl.BlockSpec(memory_space=pl.ANY)
    return pl.pallas_call(
        functools.partial(place_kernel, sources, block_rows),
        grid_spec=pltpu.PrefetchScalarGridSpec(
            num_scalar_prefetch=1,
            grid=(1,),
            in_specs=[anywhere] * (sources + 2),
            out_specs=[anywhere] * 2,
            scratch_shapes=Placing.scratch(
                sources, codes[0].shape[0] // coded_rows(block_rows), block_rows, width
            ),
        ),
        out_shape=[jax.ShapeDtypeStruct(out.shape, out.dtype) for out in outs],
        input_output_aliases={1 + sources: 0, 2 + sources: 1},
        compiler_params=pltpu.CompilerParams(vmem_limit_bytes=vmem_bytes),
        name="placed_rows",
    )(starts.astype(jnp.int32), *codes, *outs)


def combine_kernel(groups, parts_ref, out_ref):
    per_group = parts_ref.shape[0] // groups
    count = parts_ref.shape[2]
    for t in range(groups):
        parts = [parts_ref[t * per_group + k] for k in range(per_group)]
        top = functools.reduce(jnp.maximum, parts)
        total = functools.reduce(jnp.add, [jnp.exp(part - top) for part in parts])
        out_ref[:, t * count : (t + 1) * count] = top + jnp.log(total)


def combined_lse(parts, groups):
    return pl.pallas_call(
        functools.partial(combine_kernel, groups),
        out_shape=jax.ShapeDtypeStruct((1, groups * parts.shape[2]), jnp.float32),
        name="join_stats",
    )(parts)


def blank(shape):
    return pl.pallas_call(
        lambda out_ref: None,
        out_specs=pl.BlockSpec(memory_space=pl.ANY),
        out_shape=jax.ShapeDtypeStruct(shape, jnp.float32),
        name="blank",
    )()


def from_others(value, axis):
    size = lax.axis_size(axis)
    found = [value]
    for s in range(1, size):
        pairs = [(partner(k, s, size), k) for k in range(size)]
        found.append(lax.ppermute(value, axis, pairs))
    return found


def partner(me, s, size):
    return me ^ s if size & (size - 1) == 0 else (me - s) % size


def chunk_plan(blocks):
    plan = []
    while blocks:
        plan.append(max(1, (3 * blocks + 4) // 8))
        blocks -= plan[-1]
    return plan


def local(tokens, centroids):
    tok_size, cent_size = lax.axis_size("tok"), lax.axis_size("cent")
    me = lax.axis_index("tok")
    cent_count, width = centroids.shape
    share_rows = cent_count // tok_size

    every_tok = lax.all_gather(tokens, "tok", axis=0, tiled=True)
    own_lse = local_lse(tokens, centroids)
    copies = jnp.broadcast_to(own_lse[None], (tok_size * cent_size, *own_lse.shape))
    parts = lax.all_to_all(copies, ("tok", "cent"), 0, 0, tiled=True)
    lse = combined_lse(parts, tok_size)

    block_rows = divisor(share_rows, 1024)
    sources = jnp.stack([partner(me, s, tok_size) for s in range(tok_size)])
    outs = blank((cent_count, width)), blank((cent_count // 128, 128))
    waiting, first = [], 0
    for blocks in chunk_plan(share_rows // block_rows):
        block = first * tok_size + me * blocks
        if len(waiting) == 2:
            codes, *outs = updated_chunk(
                block, every_tok, lse, centroids, blocks, block_rows, (*waiting.pop(0), outs)
            )
        else:
            (codes,) = updated_chunk(block, every_tok, lse, centroids, blocks, block_rows)
        waiting.append((from_others(codes, "tok"), first * tok_size + sources * blocks))
        first += blocks
    for received in waiting:
        outs = placed((*received, outs), block_rows)
    return outs[0], outs[1].reshape(cent_count)


def solution(mesh):
    placed_as = (P("tok", None), P("cent", None))
    return jax.shard_map(
        local, mesh=mesh, in_specs=placed_as, out_specs=(P("cent", None), P("cent")), check_vma=False
    )
```

```python
import functools

import jax
import jax.numpy as jnp
from jax import lax
from jax.experimental import pallas as pl
from jax.experimental.pallas import tpu as pltpu
from jax.sharding import PartitionSpec as P

inverse_temp = 2.0
prior_weight = 0.05
safe_sum = 1e30
headroom = 60.0
code_scale = 2.0**24
slice_rows = 64
vmem_bytes = 56 * 1024 * 1024


def divisor(count, most):
    size = min(count, most)
    while count % size:
        size //= 2
    return size


def dot_nt(a, b):
    return lax.dot_general(a, b, (((1,), (1,)), ((), ())), preferred_element_type=jnp.float32)


def fold_rows(x, combine):
    parts = [x[k * 8 : (k + 1) * 8, :] for k in range(x.shape[0] // 8)]
    while len(parts) > 1:
        half = len(parts) // 2
        parts = [combine(parts[2 * k], parts[2 * k + 1]) for k in range(half)] + parts[2 * half :]
    return parts[0]


def stats_kernel(sub_rows, tok_cols, tok_ref, cent_ref, out_ref, flip_ref, base_ref, shift_ref, sums_ref):
    step = pl.program_id(0)
    tok_count = tok_ref.shape[0]
    tile = divisor(sub_rows, 1024)
    subs = cent_ref.shape[0] // sub_rows
    col_blocks = tok_count // tok_cols

    def columns(t):
        return pl.ds(pl.multiple_of(t * tok_cols, tok_cols), tok_cols)

    def dot(a, b):
        return jnp.dot(a, b, preferred_element_type=jnp.float32)

    @pl.when(step == 0)
    def _():
        @pl.loop(0, col_blocks)
        def _(t):
            flipped = (tok_ref[columns(t), :] * jnp.bfloat16(inverse_temp)).T
            flip_ref[:, columns(t)] = flipped
            logits = dot(cent_ref[0:128, :], flipped)
            top = jnp.max(fold_rows(logits, jnp.maximum), axis=0, keepdims=True)
            base_ref[:, columns(t)] = top + headroom

    @pl.loop(0, col_blocks)
    def _(t):
        rhs = flip_ref[:, columns(t)]
        shift = base_ref[:, columns(t)]
        for sub in range(subs):
            total = jnp.zeros((8, tok_cols), jnp.float32)
            for k in range(sub_rows // tile):
                logits = dot(cent_ref[pl.ds(sub * sub_rows + k * tile, tile), :], rhs)
                for first in range(0, tile, slice_rows):
                    scaled = jnp.exp(logits[first : first + slice_rows] - shift)
                    total = total + fold_rows(scaled, jnp.add)
            sums_ref[step * subs + sub, :, columns(t)] = total
            shift_ref[step * subs + sub, :, columns(t)] = shift

    worst = jnp.max(sums_ref[pl.ds(step * subs, subs), :, :])

    @pl.when(jnp.logical_not(worst < safe_sum))
    def _():
        @pl.loop(0, col_blocks)
        def _(t):
            worst_t = jnp.max(sums_ref[pl.ds(step * subs, subs), :, columns(t)])

            @pl.when(jnp.logical_not(worst_t < safe_sum))
            def _():
                @pl.loop(0, subs)
                def _(sub):
                    worst_s = jnp.max(sums_ref[step * subs + sub, :, columns(t)])

                    @pl.when(jnp.logical_not(worst_s < safe_sum))
                    def _():
                        first = pl.multiple_of(sub * sub_rows, sub_rows)
                        logits = dot(cent_ref[pl.ds(first, sub_rows), :], flip_ref[:, columns(t)])
                        top = jnp.max(fold_rows(logits, jnp.maximum), axis=0, keepdims=True)
                        total = fold_rows(jnp.exp(logits - top), jnp.add)
                        sums_ref[step * subs + sub, :, columns(t)] = total
                        shift_ref[step * subs + sub, :, columns(t)] = top

    @pl.when(step == pl.num_programs(0) - 1)
    def _():
        @pl.loop(0, col_blocks)
        def _(t):
            shifts = shift_ref[:, :, columns(t)]
            top = jnp.max(shifts, axis=0)
            scale = jnp.exp(shifts - top[None])
            total = jnp.sum(sums_ref[:, :, columns(t)] * scale, axis=0)
            total = jnp.sum(total, axis=0, keepdims=True)
            out_ref[:, columns(t)] = top + jnp.log(total)


def local_lse(tokens, centroids):
    tok_count, width = tokens.shape
    cent_count = centroids.shape[0]
    block_rows = divisor(cent_count, 4096)
    sub_rows = divisor(block_rows, 1024)
    tok_cols = divisor(tok_count, 512)
    blocks = cent_count // block_rows
    subs = cent_count // sub_rows
    return pl.pallas_call(
        functools.partial(stats_kernel, sub_rows, tok_cols),
        grid=(blocks,),
        in_specs=[
            pl.BlockSpec((tok_count, width), lambda j: (0, 0)),
            pl.BlockSpec((block_rows, width), lambda j: (j, 0)),
        ],
        out_specs=pl.BlockSpec((1, tok_count), lambda j: (0, 0)),
        out_shape=jax.ShapeDtypeStruct((1, tok_count), jnp.float32),
        scratch_shapes=[
            pltpu.VMEM((width, tok_count), jnp.bfloat16),
            pltpu.VMEM((1, tok_count), jnp.float32),
            pltpu.VMEM((subs, 1, tok_count), jnp.float32),
            pltpu.VMEM((subs, 8, tok_count), jnp.float32),
        ],
        compiler_params=pltpu.CompilerParams(vmem_limit_bytes=vmem_bytes),
        cost_estimate=pl.CostEstimate(
            flops=2 * tok_count * cent_count * width,
            bytes_accessed=(tok_count + cent_count) * width * 2,
            transcendentals=tok_count * cent_count,
        ),
        name="row_stats",
    )(tokens, centroids)


def encoded(x):
    x = x * code_scale
    return (x * jnp.abs(x) * (x * x)).astype(jnp.bfloat16)


def decoded(code):
    code = code.astype(jnp.float32)
    size = lax.rsqrt(lax.rsqrt(jnp.maximum(jnp.abs(code), 1e-37))) * (1.0 / code_scale)
    return jnp.where(code < 0, -size, jnp.where(code > 0, size, 0.0))


def split_exactly(x):
    high = x.astype(jnp.bfloat16).astype(jnp.float32)
    middle = (x - high).astype(jnp.bfloat16).astype(jnp.float32)
    return high, middle, x - high - middle


class Placing:
    def __init__(self, block_rows, starts_ref, pieces, code_refs, outs, scratch):
        self.block_rows, self.starts_ref = block_rows, starts_ref
        self.pieces, self.code_refs = pieces, code_refs
        self.updated_ref, self.masses_ref = outs
        self.codes, self.values, self.masses, self.sems = scratch

    @staticmethod
    def scratch(sources, blocks, block_rows, width):
        return [
            pltpu.VMEM((sources, blocks * coded_rows(block_rows), width), jnp.bfloat16),
            pltpu.VMEM((sources, blocks * block_rows, width), jnp.float32),
            pltpu.VMEM((sources, blocks * block_rows // 128, 128), jnp.float32),
            pltpu.SemaphoreType.DMA((4, sources)),
        ]

    def copies_in(self):
        found, refs = [], list(self.code_refs)
        for s, count in enumerate(self.pieces):
            first = 0
            for k in range(count):
                ref = refs.pop(0)
                target = self.codes.at[s, pl.ds(first, ref.shape[0]), :]
                found.append(pltpu.make_async_copy(ref, target, self.sems.at[3 * k, s]))
                first += ref.shape[0]
        return found

    def copies_out(self):
        found = []
        for s in range(len(self.pieces)):
            rows, mass_rows = self.values.shape[1], self.masses.shape[1]
            start = self.starts_ref[s]
            span = pl.ds(pl.multiple_of(start * self.block_rows, self.block_rows), rows)
            found.append(
                pltpu.make_async_copy(self.values.at[s], self.updated_ref.at[span, :], self.sems.at[1, s])
            )
            per_block = self.block_rows // 128
            span = pl.ds(pl.multiple_of(start * per_block, per_block), mass_rows)
            found.append(
                pltpu.make_async_copy(self.masses.at[s], self.masses_ref.at[span, :], self.sems.at[2, s])
            )
        return found

    def fetch(self):
        for copy in self.copies_in():
            copy.start()

    def place(self):
        block_rows, per_block = self.block_rows, self.block_rows // 128
        full = coded_rows(block_rows)
        tile = divisor(block_rows, 256)
        for copy in self.copies_in():
            copy.wait()

        @pl.loop(0, len(self.pieces))
        def _(s):
            for b in range(self.values.shape[1] // block_rows):

                @pl.loop(0, block_rows // tile)
                def _(k):
                    source = pl.ds(pl.multiple_of(b * full + k * tile, 16), tile)
                    target = pl.ds(pl.multiple_of(b * block_rows + k * tile, tile), tile)
                    self.values[s, target, :] = decoded(self.codes[s, source, :])

                terms = self.codes[s, b * full + block_rows : (b + 1) * full, :].astype(jnp.float32)
                mass = terms[:per_block] + terms[per_block : 2 * per_block]
                mass = mass + terms[2 * per_block : 3 * per_block]
                self.masses[s, b * per_block : (b + 1) * per_block, :] = mass

        for copy in self.copies_out():
            copy.start()

    def finish(self):
        for copy in self.copies_out():
            copy.wait()


def coded_rows(block_rows):
    return block_rows + block_rows // 32


def update_kernel(pieces, block_rows, *refs):
    place_ref, tok_ref, lse_ref, cent_ref = refs[:4]
    code_refs, refs = refs[4 : 4 + sum(pieces)], refs[4 + sum(pieces) :]
    if pieces:
        code_ref, updated_ref, masses_ref = refs[2:5]
        scratch = refs[5:]
        starts_ref = place_ref.at[pl.ds(1, len(pieces))]
        placing = Placing(
            block_rows, starts_ref, pieces, code_refs, (updated_ref, masses_ref), scratch[3:]
        )
    else:
        code_ref, scratch, placing = refs[0], refs[1:], None
    weights_ref, total_ref, mass_ref = scratch[:3]
    step, steps = pl.program_id(0), pl.num_programs(0)
    width = cent_ref.shape[1]
    _, tile, depth = weights_ref.shape
    piece = divisor(depth, 512)
    stages = tok_ref.shape[1] // depth
    tiles = block_rows // tile

    if placing:
        pl.when(step == 0)(placing.fetch)

    def weigh(first, stage):
        cents = cent_ref[pl.ds(first, tile), :] * jnp.bfloat16(inverse_temp)
        for k in range(depth // piece):
            span = pl.ds(stage * depth + k * piece, piece)
            logits = jnp.dot(cents, tok_ref[0:width, span], preferred_element_type=jnp.float32)
            lse = lse_ref[:, span]
            for r in range(0, tile, slice_rows):
                weights = jnp.exp(logits[r : r + slice_rows] - lse).astype(jnp.bfloat16)
                weights_ref[stage % 2, r : r + slice_rows, pl.ds(k * piece, piece)] = weights

    def gather_up(stage):
        toks = tok_ref[:, pl.ds(stage * depth, depth)]
        part = dot_nt(toks, weights_ref[stage % 2])
        if stage == 0:
            total_ref[...] = part
        else:
            total_ref[...] += part

    def run(r):
        first = pl.multiple_of(r * tile, tile)
        weigh(first, 0)
        for stage in range(1, stages):
            weigh(first, stage)
            gather_up(stage - 1)
        gather_up(stages - 1)
        mass = total_ref[width : width + 1, :]
        prior = prior_weight * cent_ref[pl.ds(first, tile), :].astype(jnp.float32).T
        new = (total_ref[0:width, :] + prior) / (mass + prior_weight)
        code_ref[pl.ds(first, tile), :] = encoded(new.T)
        for k in range(tile // 128):
            mass_ref[pl.ds(r * (tile // 128) + k, 1), :] = mass[:, k * 128 : (k + 1) * 128]

    pl.loop(0, tiles // 2)(run)
    if placing:
        pl.when(step == 0)(placing.place)
    pl.loop(tiles // 2, tiles)(run)

    terms = split_exactly(mass_ref[...])
    terms = jnp.concatenate([*terms, jnp.zeros_like(terms[0])], axis=0)
    code_ref[block_rows : block_rows + terms.shape[0], :] = terms.astype(jnp.bfloat16)
    if placing:
        pl.when(step == steps - 1)(placing.finish)


def turned_kernel(tok_ref, out_ref):
    rows = divisor(tok_ref.shape[0], 512)
    width = tok_ref.shape[1]

    @pl.loop(0, tok_ref.shape[0] // rows)
    def _(k):
        span = pl.ds(pl.multiple_of(k * rows, rows), rows)
        out_ref[0:width, span] = tok_ref[span, :].T
        out_ref[width:, span] = jnp.ones((16, rows), jnp.bfloat16)


def turned(tokens):
    count, width = tokens.shape
    return pl.pallas_call(
        turned_kernel,
        out_shape=jax.ShapeDtypeStruct((width + 16, count), jnp.bfloat16),
        compiler_params=pltpu.CompilerParams(vmem_limit_bytes=vmem_bytes),
        name="turned_tokens",
    )(tokens)


def updated_chunk(block, toks, lse, centroids, blocks, block_rows, received=None):
    all_count, width = toks.shape[1], centroids.shape[1]
    depth = divisor(all_count, 2048)
    tile = divisor(block_rows, 512)
    rows = blocks * block_rows
    full = coded_rows(block_rows)
    anywhere = pl.BlockSpec(memory_space=pl.ANY)
    whole = lambda j, place: (0, 0)
    place, operands = block.reshape(1), [toks, lse, centroids]
    in_specs = [
        pl.BlockSpec(toks.shape, whole),
        pl.BlockSpec((1, all_count), whole),
        pl.BlockSpec((block_rows, width), lambda j, place: (place[0] + j, 0)),
    ]
    out_specs = [pl.BlockSpec((full, width), lambda j, place: (j, 0))]
    out_shape = [jax.ShapeDtypeStruct((blocks * full, width), jnp.bfloat16)]
    scratch_shapes = [
        pltpu.VMEM((2, tile, depth), jnp.bfloat16),
        pltpu.VMEM((toks.shape[0], tile), jnp.float32),
        pltpu.VMEM((block_rows // 128, 128), jnp.float32),
    ]
    aliases, pieces = {}, []
    if received:
        codes, starts, outs = received
        pieces = [len(parts) for parts in codes]
        place = jnp.concatenate([place, starts])
        operands += [*sum(codes, []), *outs]
        in_specs += [anywhere] * (sum(pieces) + 2)
        out_specs += [anywhere] * 2
        out_shape += [jax.ShapeDtypeStruct(out.shape, out.dtype) for out in outs]
        aliases = {4 + sum(pieces): 1, 5 + sum(pieces): 2}
        scratch_shapes += Placing.scratch(len(codes), codes[0][0].shape[0] // full, block_rows, width)
    return pl.pallas_call(
        functools.partial(update_kernel, pieces, block_rows),
        grid_spec=pltpu.PrefetchScalarGridSpec(
            num_scalar_prefetch=1,
            grid=(blocks,),
            in_specs=in_specs,
            out_specs=out_specs,
            scratch_shapes=scratch_shapes,
        ),
        out_shape=out_shape,
        input_output_aliases=aliases,
        compiler_params=pltpu.CompilerParams(vmem_limit_bytes=vmem_bytes),
        cost_estimate=pl.CostEstimate(
            flops=6 * all_count * rows * width,
            bytes_accessed=(2 * all_count + 4 * rows) * width,
            transcendentals=all_count * rows,
        ),
        name="new_rows",
    )(place.astype(jnp.int32), *operands)


def place_kernel(pieces, block_rows, starts_ref, *refs):
    count = sum(pieces)
    code_refs, outs, scratch = refs[:count], refs[count + 2 : count + 4], refs[count + 4 :]
    placing = Placing(block_rows, starts_ref, pieces, code_refs, outs, scratch)
    placing.fetch()
    placing.place()
    placing.finish()


def placed(received, block_rows):
    codes, starts, outs = received
    pieces = [len(parts) for parts in codes]
    rows, width = codes[0][0].shape
    anywhere = pl.BlockSpec(memory_space=pl.ANY)
    return pl.pallas_call(
        functools.partial(place_kernel, pieces, block_rows),
        grid_spec=pltpu.PrefetchScalarGridSpec(
            num_scalar_prefetch=1,
            grid=(1,),
            in_specs=[anywhere] * (sum(pieces) + 2),
            out_specs=[anywhere] * 2,
            scratch_shapes=Placing.scratch(len(codes), rows // coded_rows(block_rows), block_rows, width),
        ),
        out_shape=[jax.ShapeDtypeStruct(out.shape, out.dtype) for out in outs],
        input_output_aliases={1 + sum(pieces): 0, 2 + sum(pieces): 1},
        compiler_params=pltpu.CompilerParams(vmem_limit_bytes=vmem_bytes),
        name="placed_rows",
    )(starts.astype(jnp.int32), *sum(codes, []), *outs)


def combine_kernel(groups, parts_ref, out_ref):
    per_group = parts_ref.shape[0] // groups
    count = parts_ref.shape[2]
    for t in range(groups):
        parts = [parts_ref[t * per_group + k] for k in range(per_group)]
        top = functools.reduce(jnp.maximum, parts)
        total = functools.reduce(jnp.add, [jnp.exp(part - top) for part in parts])
        out_ref[:, t * count : (t + 1) * count] = top + jnp.log(total)


def combined_lse(parts, groups):
    return pl.pallas_call(
        functools.partial(combine_kernel, groups),
        out_shape=jax.ShapeDtypeStruct((1, groups * parts.shape[2]), jnp.float32),
        name="join_stats",
    )(parts)


def blank(shape):
    return pl.pallas_call(
        lambda out_ref: None,
        out_specs=pl.BlockSpec(memory_space=pl.ANY),
        out_shape=jax.ShapeDtypeStruct(shape, jnp.float32),
        name="blank",
    )()


def from_others(value, axis):
    size = lax.axis_size(axis)
    found = [value]
    for s in range(1, size):
        pairs = [(partner(k, s, size), k) for k in range(size)]
        found.append(lax.ppermute(value, axis, pairs))
    return found


def partner(me, s, size):
    return me ^ s if size & (size - 1) == 0 else (me - s) % size


def spread(codes):
    size = lax.axis_size("tok")
    if size != 4:
        return [[found] for found in from_others(codes, "tok")]

    def swap(part, mask):
        return lax.ppermute(part, "tok", [(k, k ^ mask) for k in range(4)])

    half = codes.shape[0] // 2
    one, two = swap(codes, 1), swap(codes, 2)
    return [[codes], [one], [two], [swap(one[:half], 2), swap(two[half:], 1)]]


def chunk_plan(blocks):
    plan = []
    while blocks > 2:
        plan.append(2)
        blocks -= 2
    return plan + [1] * blocks


def local(tokens, centroids):
    tok_size, cent_size = lax.axis_size("tok"), lax.axis_size("cent")
    me = lax.axis_index("tok")
    cent_count, width = centroids.shape
    share_rows = cent_count // tok_size

    toks = turned(lax.all_gather(tokens, "tok", axis=0, tiled=True))
    own_lse = local_lse(tokens, centroids)
    copies = jnp.broadcast_to(own_lse[None], (tok_size * cent_size, *own_lse.shape))
    parts = lax.all_to_all(copies, ("tok", "cent"), 0, 0, tiled=True)
    lse = combined_lse(parts, tok_size)

    block_rows = divisor(share_rows, 1024)
    sources = jnp.stack([partner(me, s, tok_size) for s in range(tok_size)])
    outs = blank((cent_count, width)), blank((cent_count // 128, 128))
    waiting, first = [], 0
    for blocks in chunk_plan(share_rows // block_rows):
        block = first * tok_size + me * blocks
        if len(waiting) == 3:
            codes, *outs = updated_chunk(
                block, toks, lse, centroids, blocks, block_rows, (*waiting.pop(0), outs)
            )
        else:
            (codes,) = updated_chunk(block, toks, lse, centroids, blocks, block_rows)
        waiting.append((spread(codes), first * tok_size + sources * blocks))
        first += blocks
    for received in waiting:
        outs = placed((*received, outs), block_rows)
    return outs[0], outs[1].reshape(cent_count)


def solution(mesh):
    placed_as = (P("tok", None), P("cent", None))
    return jax.shard_map(
        local, mesh=mesh, in_specs=placed_as, out_specs=(P("cent", None), P("cent")), check_vma=False
    )
```

```python
import functools

import jax
import jax.numpy as jnp
from jax import lax
from jax.experimental import pallas as pl
from jax.experimental.pallas import tpu as pltpu
from jax.sharding import PartitionSpec as P

inverse_temp = 2.0
prior_weight = 0.05
safe_sum = 1e30
headroom = 60.0
code_scale = 2.0**24
slice_rows = 64
vmem_bytes = 56 * 1024 * 1024


def divisor(count, most):
    size = min(count, most)
    while count % size:
        size //= 2
    return size


def dot_nt(a, b):
    return lax.dot_general(a, b, (((1,), (1,)), ((), ())), preferred_element_type=jnp.float32)


def fold_rows(x, combine):
    parts = [x[k * 8 : (k + 1) * 8, :] for k in range(x.shape[0] // 8)]
    while len(parts) > 1:
        half = len(parts) // 2
        parts = [combine(parts[2 * k], parts[2 * k + 1]) for k in range(half)] + parts[2 * half :]
    return parts[0]


def stats_kernel(
    sub_rows, tok_cols, tok_ref, cent_ref, out_ref, flip_ref, base_ref, shift_ref, sums_ref, worst_ref
):
    step = pl.program_id(0)
    tok_count = tok_ref.shape[0]
    subs = cent_ref.shape[0] // sub_rows
    col_blocks = tok_count // tok_cols
    redo_cols = divisor(tok_cols, 256)
    redo_blocks = tok_count // redo_cols

    def columns(t, size=tok_cols):
        return pl.ds(pl.multiple_of(t * size, size), size)

    def dot(a, b):
        return jnp.dot(a, b, preferred_element_type=jnp.float32)

    @pl.when(step == 0)
    def _():
        @pl.loop(0, col_blocks)
        def _(t):
            flipped = (tok_ref[columns(t), :] * jnp.bfloat16(inverse_temp)).T
            flip_ref[:, columns(t)] = flipped
            logits = dot(cent_ref[0:128, :], flipped)
            top = jnp.max(fold_rows(logits, jnp.maximum), axis=0, keepdims=True)
            base_ref[:, columns(t)] = top + headroom

    @pl.loop(0, col_blocks)
    def _(t):
        rhs = flip_ref[:, columns(t)]
        shift = base_ref[:, columns(t)]
        for sub in range(subs):
            total = jnp.zeros((8, tok_cols), jnp.float32)
            logits = dot(cent_ref[pl.ds(sub * sub_rows, sub_rows), :], rhs)
            for first in range(0, sub_rows, slice_rows):
                scaled = jnp.exp(logits[first : first + slice_rows] - shift)
                total = total + fold_rows(scaled, jnp.add)
            sums_ref[step * subs + sub, :, columns(t)] = total
            shift_ref[step * subs + sub, :, columns(t)] = shift

    worst = jnp.float32(0.0)
    for sub in range(subs):
        for t in range(redo_blocks):
            block = jnp.max(sums_ref[step * subs + sub, :, t * redo_cols : (t + 1) * redo_cols])
            worst_ref[sub * redo_blocks + t] = block
            worst = jnp.maximum(worst, block)

    @pl.when(jnp.logical_not(worst < safe_sum))
    def _():
        @pl.loop(0, subs * redo_blocks)
        def _(k):
            @pl.when(jnp.logical_not(worst_ref[k] < safe_sum))
            def _():
                sub, t = k // redo_blocks, lax.rem(k, redo_blocks)
                first = pl.multiple_of(sub * sub_rows, sub_rows)
                logits = dot(cent_ref[pl.ds(first, sub_rows), :], flip_ref[:, columns(t, redo_cols)])
                top = jnp.max(fold_rows(logits, jnp.maximum), axis=0, keepdims=True)
                total = fold_rows(jnp.exp(logits - top), jnp.add)
                sums_ref[step * subs + sub, :, columns(t, redo_cols)] = total
                shift_ref[step * subs + sub, :, columns(t, redo_cols)] = top

    @pl.when(step == pl.num_programs(0) - 1)
    def _():
        @pl.loop(0, col_blocks)
        def _(t):
            shifts = shift_ref[:, :, columns(t)]
            top = jnp.max(shifts, axis=0)
            scale = jnp.exp(shifts - top[None])
            total = jnp.sum(sums_ref[:, :, columns(t)] * scale, axis=0)
            total = jnp.sum(total, axis=0, keepdims=True)
            out_ref[:, :, columns(t)] = jnp.broadcast_to(
                (top + jnp.log(total))[None], (out_ref.shape[0], 1, tok_cols)
            )


def local_lse(tokens, centroids, copies):
    tok_count, width = tokens.shape
    cent_count = centroids.shape[0]
    block_rows = divisor(cent_count, 4096)
    sub_rows = divisor(block_rows, 1024)
    tok_cols = divisor(tok_count, 512)
    blocks = cent_count // block_rows
    subs = cent_count // sub_rows
    flags = block_rows // sub_rows * (tok_count // divisor(tok_cols, 256))
    return pl.pallas_call(
        functools.partial(stats_kernel, sub_rows, tok_cols),
        grid=(blocks,),
        in_specs=[
            pl.BlockSpec((tok_count, width), lambda j: (0, 0)),
            pl.BlockSpec((block_rows, width), lambda j: (j, 0)),
        ],
        out_specs=pl.BlockSpec((copies, 1, tok_count), lambda j: (0, 0, 0)),
        out_shape=jax.ShapeDtypeStruct((copies, 1, tok_count), jnp.float32),
        scratch_shapes=[
            pltpu.VMEM((width, tok_count), jnp.bfloat16),
            pltpu.VMEM((1, tok_count), jnp.float32),
            pltpu.VMEM((subs, 1, tok_count), jnp.float32),
            pltpu.VMEM((subs, 8, tok_count), jnp.float32),
            pltpu.SMEM((flags,), jnp.float32),
        ],
        compiler_params=pltpu.CompilerParams(vmem_limit_bytes=vmem_bytes),
        cost_estimate=pl.CostEstimate(
            flops=2 * tok_count * cent_count * width,
            bytes_accessed=(tok_count + cent_count) * width * 2,
            transcendentals=tok_count * cent_count,
        ),
        name="row_stats",
    )(tokens, centroids)


def encoded(x):
    x = x * code_scale
    return (x * jnp.abs(x) * (x * x)).astype(jnp.bfloat16)


def decoded(code):
    code = code.astype(jnp.float32)
    size = lax.rsqrt(lax.rsqrt(jnp.maximum(jnp.abs(code), 1e-37))) * (1.0 / code_scale)
    return jnp.where(code < 0, -size, jnp.where(code > 0, size, 0.0))


def split_exactly(x):
    high = x.astype(jnp.bfloat16).astype(jnp.float32)
    middle = (x - high).astype(jnp.bfloat16).astype(jnp.float32)
    return high, middle, x - high - middle


class Placing:
    def __init__(self, block_rows, starts_ref, pieces, code_refs, outs, scratch):
        self.block_rows, self.starts_ref = block_rows, starts_ref
        self.pieces, self.code_refs = pieces, code_refs
        self.updated_ref, self.masses_ref = outs
        self.codes, self.values, self.masses, self.sems = scratch

    @staticmethod
    def scratch(sources, blocks, block_rows, width):
        return [
            pltpu.VMEM((sources, blocks * coded_rows(block_rows), width), jnp.bfloat16),
            pltpu.VMEM((sources, blocks * block_rows, width), jnp.float32),
            pltpu.VMEM((sources, blocks * block_rows // 128, 128), jnp.float32),
            pltpu.SemaphoreType.DMA((4, sources)),
        ]

    def copies_in(self):
        found, refs = [], list(self.code_refs)
        for s, count in enumerate(self.pieces):
            found.append([])
            first = 0
            for k in range(count):
                ref = refs.pop(0)
                target = self.codes.at[s, pl.ds(first, ref.shape[0]), :]
                found[s].append(pltpu.make_async_copy(ref, target, self.sems.at[3 * k, s]))
                first += ref.shape[0]
        return found

    def copies_out(self, s):
        rows, mass_rows = self.values.shape[1], self.masses.shape[1]
        start = self.starts_ref[s]
        span = pl.ds(pl.multiple_of(start * self.block_rows, self.block_rows), rows)
        per_block = self.block_rows // 128
        mass_span = pl.ds(pl.multiple_of(start * per_block, per_block), mass_rows)
        return [
            pltpu.make_async_copy(self.values.at[s], self.updated_ref.at[span, :], self.sems.at[1, s]),
            pltpu.make_async_copy(self.masses.at[s], self.masses_ref.at[mass_span, :], self.sems.at[2, s]),
        ]

    def fetch(self):
        for copies in self.copies_in():
            for copy in copies:
                copy.start()

    def place(self):
        block_rows, per_block = self.block_rows, self.block_rows // 128
        full = coded_rows(block_rows)
        tile = divisor(block_rows, 256)
        for s, copies in enumerate(self.copies_in()):
            for copy in copies:
                copy.wait()

            @pl.loop(0, self.values.shape[1] // block_rows)
            def _(b):
                for k in range(block_rows // tile):
                    source = pl.ds(pl.multiple_of(b * full + k * tile, 32), tile)
                    target = pl.ds(pl.multiple_of(b * block_rows + k * tile, tile), tile)
                    self.values[s, target, :] = decoded(self.codes[s, source, :])
                last = pl.ds(pl.multiple_of(b * full + block_rows, 32), full - block_rows)
                terms = self.codes[s, last, :].astype(jnp.float32)
                mass = terms[:per_block] + terms[per_block : 2 * per_block]
                mass = mass + terms[2 * per_block : 3 * per_block]
                self.masses[s, pl.ds(pl.multiple_of(b * per_block, per_block), per_block), :] = mass

            for copy in self.copies_out(s):
                copy.start()

    def finish(self):
        for s in range(len(self.pieces)):
            for copy in self.copies_out(s):
                copy.wait()


def coded_rows(block_rows):
    return block_rows + block_rows // 32


def update_kernel(unread, pieces, block_rows, *refs):
    place_ref, tok_ref, lse_ref, cent_ref = refs[:4]
    refs = refs[4 + unread :]
    code_refs, refs = refs[: sum(pieces)], refs[sum(pieces) :]
    if pieces:
        code_ref, updated_ref, masses_ref = refs[2:5]
        scratch = refs[5:]
        starts_ref = place_ref.at[pl.ds(1, len(pieces))]
        placing = Placing(
            block_rows, starts_ref, pieces, code_refs, (updated_ref, masses_ref), scratch[8:]
        )
    else:
        code_ref, scratch, placing = refs[0], refs[1:], None
    toks_ref, lses_ref, cents_ref, codes_ref, weights_ref, total_ref, mass_ref, sems = scratch[:8]
    rows, width = cents_ref.shape
    _, tile, depth = weights_ref.shape
    piece = divisor(depth, 512)
    stages = toks_ref.shape[0] // depth
    full = coded_rows(block_rows)
    per_block = block_rows // tile

    first_row = pl.multiple_of(place_ref[0] * block_rows, block_rows)
    loads = [
        pltpu.make_async_copy(cent_ref.at[pl.ds(first_row, rows), :], cents_ref, sems.at[0]),
        pltpu.make_async_copy(lse_ref, lses_ref, sems.at[1]),
    ]
    for stage in range(stages):
        span = pl.ds(stage * depth, depth)
        loads.append(pltpu.make_async_copy(tok_ref.at[span, :], toks_ref.at[span, :], sems.at[2 + stage]))
    for load in loads:
        load.start()
    if placing:
        placing.fetch()

    def weigh(first, stage):
        cents = cents_ref[pl.ds(first, tile), :] * jnp.bfloat16(inverse_temp)
        for k in range(depth // piece):
            span = pl.ds(stage * depth + k * piece, piece)
            logits = dot_nt(cents, toks_ref[span, :])
            lse = lses_ref[:, span]
            for r in range(0, tile, slice_rows):
                weights = jnp.exp(logits[r : r + slice_rows] - lse).astype(jnp.bfloat16)
                weights_ref[stage % 2, r : r + slice_rows, pl.ds(k * piece, piece)] = weights

    def gather_up(stage):
        toks = toks_ref[pl.ds(stage * depth, depth), :]
        rhs = jnp.concatenate([toks, jnp.ones_like(toks)], axis=1)
        part = jnp.dot(weights_ref[stage % 2], rhs, preferred_element_type=jnp.float32)
        if stage == 0:
            total_ref[...] = part
        else:
            total_ref[...] += part

    diagonal = lax.broadcasted_iota(jnp.int32, (128, 128), 0) == lax.broadcasted_iota(
        jnp.int32, (128, 128), 1
    )

    def run(r, waits=()):
        first = pl.multiple_of(r * tile, tile)
        for stage in range(stages):
            if waits:
                waits[stage].wait()
            weigh(first, stage)
            if stage:
                gather_up(stage - 1)
        gather_up(stages - 1)
        mass = total_ref[:, width : 2 * width]
        prior = prior_weight * cents_ref[pl.ds(first, tile), :].astype(jnp.float32)
        new = (total_ref[:, 0:width] + prior) / (mass + prior_weight)
        block = r // per_block
        coded = pl.multiple_of(first + block * (full - block_rows), 32)
        codes_ref[pl.ds(coded, tile), :] = encoded(new)
        for k in range(tile // 128):
            square = jnp.where(diagonal, mass[k * 128 : (k + 1) * 128, :], 0.0)
            mass_ref[r * (tile // 128) + k] = jnp.sum(square, axis=0, keepdims=True)

    loads[0].wait()
    loads[1].wait()
    run(0, loads[2:])
    if placing:
        placing.place()
    pl.loop(1, rows // tile)(run)

    for b in range(rows // block_rows):
        mass = mass_ref[b * block_rows // 128 : (b + 1) * block_rows // 128]
        mass = mass.reshape(block_rows // 128, 128)
        terms = split_exactly(mass)
        terms = jnp.concatenate([*terms, jnp.zeros_like(mass)], axis=0)
        codes_ref[b * full + block_rows : (b + 1) * full, :] = terms.astype(jnp.bfloat16)
    store = pltpu.make_async_copy(codes_ref, code_ref, sems.at[0])
    store.start()
    if placing:
        placing.finish()
    store.wait()


def updated_chunk(block, toks, lse, centroids, blocks, block_rows, after=(), received=None):
    all_count, width = toks.shape
    depth = divisor(all_count, 2048)
    tile = divisor(block_rows, 512)
    rows = blocks * block_rows
    full = coded_rows(block_rows)
    anywhere = pl.BlockSpec(memory_space=pl.ANY)
    place, operands = block.reshape(1), [toks, lse, centroids, *after]
    out_shape = [jax.ShapeDtypeStruct((blocks * full, width), jnp.bfloat16)]
    scratch_shapes = [
        pltpu.VMEM((all_count, width), jnp.bfloat16),
        pltpu.VMEM((1, all_count), jnp.float32),
        pltpu.VMEM((rows, width), jnp.bfloat16),
        pltpu.VMEM((blocks * full, width), jnp.bfloat16),
        pltpu.VMEM((2, tile, depth), jnp.bfloat16),
        pltpu.VMEM((tile, 2 * width), jnp.float32),
        pltpu.VMEM((rows // 128, 1, 128), jnp.float32),
        pltpu.SemaphoreType.DMA((2 + all_count // depth,)),
    ]
    aliases, pieces = {}, []
    if received:
        codes, starts, outs = received
        pieces = [len(parts) for parts in codes]
        place = jnp.concatenate([place, starts])
        operands += [*sum(codes, []), *outs]
        out_shape += [jax.ShapeDtypeStruct(out.shape, out.dtype) for out in outs]
        aliases = {len(operands) - 1: 1, len(operands): 2}
        scratch_shapes += Placing.scratch(len(codes), codes[0][0].shape[0] // full, block_rows, width)
    return pl.pallas_call(
        functools.partial(update_kernel, len(after), pieces, block_rows),
        grid_spec=pltpu.PrefetchScalarGridSpec(
            num_scalar_prefetch=1,
            grid=(1,),
            in_specs=[anywhere] * len(operands),
            out_specs=[anywhere] * len(out_shape),
            scratch_shapes=scratch_shapes,
        ),
        out_shape=out_shape,
        input_output_aliases=aliases,
        compiler_params=pltpu.CompilerParams(vmem_limit_bytes=vmem_bytes),
        cost_estimate=pl.CostEstimate(
            flops=6 * all_count * rows * width,
            bytes_accessed=(2 * all_count + 4 * rows) * width,
            transcendentals=all_count * rows,
        ),
        name="new_rows",
    )(place.astype(jnp.int32), *operands)


def place_kernel(chunks, block_rows, starts_ref, *refs):
    count = sum(map(sum, chunks))
    code_refs, outs, scratch = refs[:count], refs[count + 2 : count + 4], refs[count + 4 :]
    placings, first = [], 0
    for pieces in chunks:
        starts = starts_ref.at[pl.ds(first, len(pieces))]
        placings.append(
            Placing(block_rows, starts, pieces, code_refs[: sum(pieces)], outs, scratch[:4])
        )
        code_refs, scratch = code_refs[sum(pieces) :], scratch[4:]
        first += len(pieces)
    for placing in placings:
        placing.fetch()
    for placing in placings:
        placing.place()
    for placing in placings:
        placing.finish()


def placed(received, outs, block_rows):
    operands, starts, chunks, scratch_shapes = [], [], [], []
    for codes, start in received:
        chunks.append([len(parts) for parts in codes])
        operands += sum(codes, [])
        starts.append(start)
        rows, width = codes[0][0].shape
        blocks = rows // coded_rows(block_rows)
        scratch_shapes += Placing.scratch(len(codes), blocks, block_rows, width)
    anywhere = pl.BlockSpec(memory_space=pl.ANY)
    return pl.pallas_call(
        functools.partial(place_kernel, chunks, block_rows),
        grid_spec=pltpu.PrefetchScalarGridSpec(
            num_scalar_prefetch=1,
            grid=(1,),
            in_specs=[anywhere] * (len(operands) + 2),
            out_specs=[anywhere] * 2,
            scratch_shapes=scratch_shapes,
        ),
        out_shape=[jax.ShapeDtypeStruct(out.shape, out.dtype) for out in outs],
        input_output_aliases={1 + len(operands): 0, 2 + len(operands): 1},
        compiler_params=pltpu.CompilerParams(vmem_limit_bytes=vmem_bytes),
        name="placed_rows",
    )(jnp.concatenate(starts).astype(jnp.int32), *operands, *outs)


def combine_kernel(groups, parts_ref, out_ref):
    per_group = parts_ref.shape[0] // groups
    count = parts_ref.shape[2]
    for t in range(groups):
        parts = [parts_ref[t * per_group + k] for k in range(per_group)]
        top = functools.reduce(jnp.maximum, parts)
        total = functools.reduce(jnp.add, [jnp.exp(part - top) for part in parts])
        out_ref[:, t * count : (t + 1) * count] = top + jnp.log(total)


def combined_lse(parts, groups):
    return pl.pallas_call(
        functools.partial(combine_kernel, groups),
        out_shape=jax.ShapeDtypeStruct((1, groups * parts.shape[2]), jnp.float32),
        name="join_stats",
    )(parts)


def blank(shape):
    return pl.pallas_call(
        lambda out_ref: None,
        out_specs=pl.BlockSpec(memory_space=pl.ANY),
        out_shape=jax.ShapeDtypeStruct(shape, jnp.float32),
        name="blank",
    )()


def from_others(value, axis):
    size = lax.axis_size(axis)
    found = [value]
    for s in range(1, size):
        pairs = [(partner(k, s, size), k) for k in range(size)]
        found.append(lax.ppermute(value, axis, pairs))
    return found


def partner(me, s, size):
    return me ^ s if size & (size - 1) == 0 else (me - s) % size


def spread(codes):
    size = lax.axis_size("tok")
    if size != 4:
        return [[found] for found in from_others(codes, "tok")]

    def swap(part, mask):
        return lax.ppermute(part, "tok", [(k, k ^ mask) for k in range(4)])

    half = codes.shape[0] // 2
    one, two = swap(codes, 1), swap(codes, 2)
    return [[codes], [one], [two], [swap(one[:half], 2), swap(two[half:], 1)]]


def chunk_plan(blocks):
    plan = [1] if blocks > 1 else []
    blocks -= len(plan)
    while blocks:
        plan.insert(0, min(blocks, 2 if blocks > 3 else 3))
        blocks -= plan[0]
    return plan


def local(tokens, centroids):
    tok_size, cent_size = lax.axis_size("tok"), lax.axis_size("cent")
    me = lax.axis_index("tok")
    cent_count, width = centroids.shape
    share_rows = cent_count // tok_size

    toks = lax.all_gather(tokens, "tok", axis=0, tiled=True)
    own_lse = local_lse(tokens, centroids, tok_size * cent_size)
    parts = lax.all_to_all(own_lse, ("tok", "cent"), 0, 0, tiled=True)
    lse = combined_lse(parts, tok_size)

    block_rows = divisor(share_rows, 1024)
    sources = jnp.stack([partner(me, s, tok_size) for s in range(tok_size)])
    outs = blank((cent_count, width)), blank((cent_count // 128, 128))
    waiting, first = [], 0
    for blocks in chunk_plan(share_rows // block_rows):
        block = first * tok_size + me * blocks
        after = sum(waiting[-2][0][1:3], []) if len(waiting) > 1 else ()
        received = (*waiting.pop(0), outs) if len(waiting) == 3 else None
        codes, *placed_outs = updated_chunk(
            block, toks, lse, centroids, blocks, block_rows, after, received
        )
        outs = placed_outs or outs
        waiting.append((spread(codes), first * tok_size + sources * blocks))
        first += blocks
    if len(waiting) > 1:
        outs = placed(waiting[:-1], outs, block_rows)
    outs = placed(waiting[-1:], outs, block_rows)
    return outs[0], outs[1].reshape(cent_count)


def solution(mesh):
    placed_as = (P("tok", None), P("cent", None))
    return jax.shard_map(
        local, mesh=mesh, in_specs=placed_as, out_specs=(P("cent", None), P("cent")), check_vma=False
    )
```

```python
import functools

import jax
import jax.numpy as jnp
from jax import lax
from jax.experimental import pallas as pl
from jax.experimental.pallas import tpu as pltpu
from jax.sharding import PartitionSpec as P

inverse_temp = 2.0
prior_weight = 0.05
safe_sum = 1e30
headroom = 60.0
code_scale = 2.0**24
slice_rows = 64
vmem_bytes = 56 * 1024 * 1024


def divisor(count, most):
    size = min(count, most)
    while count % size:
        size //= 2
    return size


def dot_nt(a, b):
    return lax.dot_general(a, b, (((1,), (1,)), ((), ())), preferred_element_type=jnp.float32)


def fold_rows(x, combine):
    parts = [x[k * 8 : (k + 1) * 8, :] for k in range(x.shape[0] // 8)]
    while len(parts) > 1:
        half = len(parts) // 2
        parts = [combine(parts[2 * k], parts[2 * k + 1]) for k in range(half)] + parts[2 * half :]
    return parts[0]


def split_exactly(x):
    high = x.astype(jnp.bfloat16).astype(jnp.float32)
    middle = (x - high).astype(jnp.bfloat16).astype(jnp.float32)
    return high, middle, x - high - middle


def stats_kernel(
    sub_rows, tok_cols, tok_ref, cent_ref, out_ref, flip_ref, base_ref, shift_ref, sums_ref, worst_ref
):
    step = pl.program_id(0)
    tok_count = tok_ref.shape[0]
    subs = cent_ref.shape[0] // sub_rows
    col_blocks = tok_count // tok_cols
    redo_cols = divisor(tok_cols, 256)
    redo_blocks = tok_count // redo_cols

    def columns(t, size=tok_cols):
        return pl.ds(pl.multiple_of(t * size, size), size)

    def dot(a, b):
        return jnp.dot(a, b, preferred_element_type=jnp.float32)

    width = tok_ref.shape[1]

    @pl.when(step == 0)
    def _():
        @pl.loop(0, col_blocks)
        def _(t):
            flipped = (tok_ref[columns(t), :] * jnp.bfloat16(inverse_temp)).T
            flip_ref[0:width, columns(t)] = flipped
            logits = dot(cent_ref[0:128, :], flipped)
            top = jnp.max(fold_rows(logits, jnp.maximum), axis=0, keepdims=True)
            base = top + headroom
            base_ref[:, columns(t)] = base
            row = lax.broadcasted_iota(jnp.int32, (width, tok_cols), 0)
            terms = jnp.zeros((width, tok_cols), jnp.float32)
            for k, term in enumerate(split_exactly(-base)):
                terms = jnp.where(row == k, term, terms)
            flip_ref[width:, columns(t)] = terms.astype(jnp.bfloat16)

    lane = lax.broadcasted_iota(jnp.int32, (sub_rows, width), 1)
    ones = jnp.where(lane < 3, 1.0, 0.0).astype(jnp.bfloat16)

    @pl.loop(0, col_blocks)
    def _(t):
        rhs = flip_ref[:, columns(t)]
        shift = base_ref[:, columns(t)]
        for sub in range(subs):
            total = jnp.zeros((8, tok_cols), jnp.float32)
            lhs = jnp.concatenate([cent_ref[pl.ds(sub * sub_rows, sub_rows), :], ones], axis=1)
            logits = dot(lhs, rhs)
            for first in range(0, sub_rows, slice_rows):
                scaled = jnp.exp(logits[first : first + slice_rows])
                total = total + fold_rows(scaled, jnp.add)
            sums_ref[step * subs + sub, :, columns(t)] = total
            shift_ref[step * subs + sub, :, columns(t)] = shift

    worst = jnp.float32(0.0)
    for sub in range(subs):
        for t in range(redo_blocks):
            block = jnp.max(sums_ref[step * subs + sub, :, t * redo_cols : (t + 1) * redo_cols])
            worst_ref[sub * redo_blocks + t] = block
            worst = jnp.maximum(worst, block)

    @pl.when(jnp.logical_not(worst < safe_sum))
    def _():
        @pl.loop(0, subs * redo_blocks)
        def _(k):
            @pl.when(jnp.logical_not(worst_ref[k] < safe_sum))
            def _():
                sub, t = k // redo_blocks, lax.rem(k, redo_blocks)
                first = pl.multiple_of(sub * sub_rows, sub_rows)
                rhs = flip_ref[0:width, columns(t, redo_cols)]
                logits = dot(cent_ref[pl.ds(first, sub_rows), :], rhs)
                top = jnp.max(fold_rows(logits, jnp.maximum), axis=0, keepdims=True)
                total = fold_rows(jnp.exp(logits - top), jnp.add)
                sums_ref[step * subs + sub, :, columns(t, redo_cols)] = total
                shift_ref[step * subs + sub, :, columns(t, redo_cols)] = top

    @pl.when(step == pl.num_programs(0) - 1)
    def _():
        @pl.loop(0, col_blocks)
        def _(t):
            shifts = shift_ref[:, :, columns(t)]
            top = jnp.max(shifts, axis=0)
            scale = jnp.exp(shifts - top[None])
            total = jnp.sum(sums_ref[:, :, columns(t)] * scale, axis=0)
            total = jnp.sum(total, axis=0, keepdims=True)
            out_ref[:, :, columns(t)] = jnp.broadcast_to(
                (top + jnp.log(total))[None], (out_ref.shape[0], 1, tok_cols)
            )


def local_lse(tokens, centroids, copies):
    tok_count, width = tokens.shape
    cent_count = centroids.shape[0]
    block_rows = divisor(cent_count, 4096)
    sub_rows = divisor(block_rows, 1024)
    tok_cols = divisor(tok_count, 512)
    blocks = cent_count // block_rows
    subs = cent_count // sub_rows
    flags = block_rows // sub_rows * (tok_count // divisor(tok_cols, 256))
    return pl.pallas_call(
        functools.partial(stats_kernel, sub_rows, tok_cols),
        grid=(blocks,),
        in_specs=[
            pl.BlockSpec((tok_count, width), lambda j: (0, 0)),
            pl.BlockSpec((block_rows, width), lambda j: (j, 0)),
        ],
        out_specs=pl.BlockSpec((copies, 1, tok_count), lambda j: (0, 0, 0)),
        out_shape=jax.ShapeDtypeStruct((copies, 1, tok_count), jnp.float32),
        scratch_shapes=[
            pltpu.VMEM((2 * width, tok_count), jnp.bfloat16),
            pltpu.VMEM((1, tok_count), jnp.float32),
            pltpu.VMEM((subs, 1, tok_count), jnp.float32),
            pltpu.VMEM((subs, 8, tok_count), jnp.float32),
            pltpu.SMEM((flags,), jnp.float32),
        ],
        compiler_params=pltpu.CompilerParams(vmem_limit_bytes=vmem_bytes),
        cost_estimate=pl.CostEstimate(
            flops=2 * tok_count * cent_count * width,
            bytes_accessed=(tok_count + cent_count) * width * 2,
            transcendentals=tok_count * cent_count,
        ),
        name="row_stats",
    )(tokens, centroids)


def encoded(x):
    x = x * code_scale
    return (x * jnp.abs(x) * (x * x)).astype(jnp.bfloat16)


def decoded(code):
    code = code.astype(jnp.float32)
    size = lax.rsqrt(lax.rsqrt(jnp.maximum(jnp.abs(code), 1e-37))) * (1.0 / code_scale)
    return jnp.where(code < 0, -size, jnp.where(code > 0, size, 0.0))


class Placing:
    def __init__(self, block_rows, starts_ref, pieces, code_refs, outs, scratch):
        self.block_rows, self.starts_ref = block_rows, starts_ref
        self.pieces, self.code_refs = pieces, code_refs
        self.updated_ref, self.masses_ref = outs
        self.codes, self.values, self.masses, self.sems = scratch

    @staticmethod
    def scratch(sources, blocks, block_rows, width):
        return [
            pltpu.VMEM((sources, blocks * coded_rows(block_rows), width), jnp.bfloat16),
            pltpu.VMEM((sources, blocks * block_rows, width), jnp.float32),
            pltpu.VMEM((sources, blocks * block_rows // 128, 128), jnp.float32),
            pltpu.SemaphoreType.DMA((4, sources)),
        ]

    def copies_in(self):
        found, refs = [], list(self.code_refs)
        for s, count in enumerate(self.pieces):
            found.append([])
            first = 0
            for k in range(count):
                ref = refs.pop(0)
                target = self.codes.at[s, pl.ds(first, ref.shape[0]), :]
                found[s].append(pltpu.make_async_copy(ref, target, self.sems.at[3 * k, s]))
                first += ref.shape[0]
        return found

    def copies_out(self, s):
        rows, mass_rows = self.values.shape[1], self.masses.shape[1]
        start = self.starts_ref[s]
        span = pl.ds(pl.multiple_of(start * self.block_rows, self.block_rows), rows)
        per_block = self.block_rows // 128
        mass_span = pl.ds(pl.multiple_of(start * per_block, per_block), mass_rows)
        return [
            pltpu.make_async_copy(self.values.at[s], self.updated_ref.at[span, :], self.sems.at[1, s]),
            pltpu.make_async_copy(self.masses.at[s], self.masses_ref.at[mass_span, :], self.sems.at[2, s]),
        ]

    def fetch(self):
        for copies in self.copies_in():
            for copy in copies:
                copy.start()

    def place(self):
        block_rows, per_block = self.block_rows, self.block_rows // 128
        full = coded_rows(block_rows)
        tile = divisor(block_rows, 256)
        for s, copies in enumerate(self.copies_in()):
            for copy in copies:
                copy.wait()

            @pl.loop(0, self.values.shape[1] // block_rows)
            def _(b):
                for k in range(block_rows // tile):
                    source = pl.ds(pl.multiple_of(b * full + k * tile, 32), tile)
                    target = pl.ds(pl.multiple_of(b * block_rows + k * tile, tile), tile)
                    self.values[s, target, :] = decoded(self.codes[s, source, :])
                last = pl.ds(pl.multiple_of(b * full + block_rows, 32), full - block_rows)
                terms = self.codes[s, last, :].astype(jnp.float32)
                mass = terms[:per_block] + terms[per_block : 2 * per_block]
                mass = mass + terms[2 * per_block : 3 * per_block]
                self.masses[s, pl.ds(pl.multiple_of(b * per_block, per_block), per_block), :] = mass

            for copy in self.copies_out(s):
                copy.start()

    def finish(self):
        for s in range(len(self.pieces)):
            for copy in self.copies_out(s):
                copy.wait()


def coded_rows(block_rows):
    return block_rows + block_rows // 32


def update_kernel(unread, pieces, block_rows, *refs):
    place_ref, tok_ref, lse_ref, cent_ref = refs[:4]
    refs = refs[4 + unread :]
    code_refs, refs = refs[: sum(pieces)], refs[sum(pieces) :]
    if pieces:
        code_ref, updated_ref, masses_ref = refs[2:5]
        scratch = refs[5:]
        starts_ref = place_ref.at[pl.ds(1, len(pieces))]
        placing = Placing(
            block_rows, starts_ref, pieces, code_refs, (updated_ref, masses_ref), scratch[3:]
        )
    else:
        code_ref, scratch, placing = refs[0], refs[1:], None
    weights_ref, total_ref, mass_ref = scratch[:3]
    step, steps = pl.program_id(0), pl.num_programs(0)
    width = tok_ref.shape[1]
    _, tile, depth = weights_ref.shape
    piece = divisor(depth, 512)
    stages = tok_ref.shape[0] // depth
    tiles = block_rows // tile

    if placing:
        pl.when(step == 0)(placing.fetch)

    def weigh(first, stage):
        cents = cent_ref[pl.ds(first, tile), :] * jnp.bfloat16(inverse_temp)
        for k in range(depth // piece):
            span = pl.ds(stage * depth + k * piece, piece)
            logits = dot_nt(cents, tok_ref[span, :])
            lse = lse_ref[:, span]
            for r in range(0, tile, slice_rows):
                weights = jnp.exp(logits[r : r + slice_rows] - lse).astype(jnp.bfloat16)
                weights_ref[stage % 2, r : r + slice_rows, pl.ds(k * piece, piece)] = weights

    def gather_up(stage):
        toks = tok_ref[pl.ds(stage * depth, depth), :]
        rhs = jnp.concatenate([toks, jnp.ones_like(toks)], axis=1)
        part = jnp.dot(weights_ref[stage % 2], rhs, preferred_element_type=jnp.float32)
        if stage == 0:
            total_ref[...] = part
        else:
            total_ref[...] += part

    diagonal = lax.broadcasted_iota(jnp.int32, (128, 128), 0) == lax.broadcasted_iota(
        jnp.int32, (128, 128), 1
    )

    def run(r):
        first = pl.multiple_of(r * tile, tile)
        weigh(first, 0)
        for stage in range(1, stages):
            weigh(first, stage)
            gather_up(stage - 1)
        gather_up(stages - 1)
        mass = total_ref[:, width : 2 * width]
        prior = prior_weight * cent_ref[pl.ds(first, tile), :].astype(jnp.float32)
        new = (total_ref[:, 0:width] + prior) / (mass + prior_weight)
        code_ref[pl.ds(first, tile), :] = encoded(new)
        for k in range(tile // 128):
            square = jnp.where(diagonal, mass[k * 128 : (k + 1) * 128, :], 0.0)
            mass_ref[pl.ds(r * (tile // 128) + k, 1), :] = jnp.sum(square, axis=0, keepdims=True)

    pl.loop(0, tiles // 2)(run)
    if placing:
        pl.when(step == 0)(placing.place)
    pl.loop(tiles // 2, tiles)(run)

    terms = split_exactly(mass_ref[...])
    terms = jnp.concatenate([*terms, jnp.zeros_like(terms[0])], axis=0)
    code_ref[block_rows : block_rows + terms.shape[0], :] = terms.astype(jnp.bfloat16)
    if placing:
        pl.when(step == steps - 1)(placing.finish)


def updated_chunk(block, toks, lse, centroids, blocks, block_rows, after=(), received=None):
    all_count, width = toks.shape
    depth = divisor(all_count, 2048)
    tile = divisor(block_rows, 512)
    rows = blocks * block_rows
    full = coded_rows(block_rows)
    anywhere = pl.BlockSpec(memory_space=pl.ANY)
    whole = lambda j, place: (0, 0)
    place, operands = block.reshape(1), [toks, lse, centroids, *after]
    in_specs = [
        pl.BlockSpec((all_count, width), whole),
        pl.BlockSpec((1, all_count), whole),
        pl.BlockSpec((block_rows, width), lambda j, place: (place[0] + j, 0)),
    ] + [anywhere] * len(after)
    out_specs = [pl.BlockSpec((full, width), lambda j, place: (j, 0))]
    out_shape = [jax.ShapeDtypeStruct((blocks * full, width), jnp.bfloat16)]
    scratch_shapes = [
        pltpu.VMEM((2, tile, depth), jnp.bfloat16),
        pltpu.VMEM((tile, 2 * width), jnp.float32),
        pltpu.VMEM((block_rows // 128, 128), jnp.float32),
    ]
    aliases, pieces = {}, []
    if received:
        codes, starts, outs = received
        pieces = [len(parts) for parts in codes]
        place = jnp.concatenate([place, starts])
        operands += [*sum(codes, []), *outs]
        in_specs += [anywhere] * (sum(pieces) + 2)
        out_specs += [anywhere] * 2
        out_shape += [jax.ShapeDtypeStruct(out.shape, out.dtype) for out in outs]
        aliases = {len(operands) - 1: 1, len(operands): 2}
        scratch_shapes += Placing.scratch(len(codes), codes[0][0].shape[0] // full, block_rows, width)
    return pl.pallas_call(
        functools.partial(update_kernel, len(after), pieces, block_rows),
        grid_spec=pltpu.PrefetchScalarGridSpec(
            num_scalar_prefetch=1,
            grid=(blocks,),
            in_specs=in_specs,
            out_specs=out_specs,
            scratch_shapes=scratch_shapes,
        ),
        out_shape=out_shape,
        input_output_aliases=aliases,
        compiler_params=pltpu.CompilerParams(vmem_limit_bytes=vmem_bytes),
        cost_estimate=pl.CostEstimate(
            flops=6 * all_count * rows * width,
            bytes_accessed=(2 * all_count + 4 * rows) * width,
            transcendentals=all_count * rows,
        ),
        name="new_rows",
    )(place.astype(jnp.int32), *operands)


def place_kernel(chunks, block_rows, starts_ref, *refs):
    count = sum(map(sum, chunks))
    code_refs, outs, scratch = refs[:count], refs[count + 2 : count + 4], refs[count + 4 :]
    placings, first = [], 0
    for pieces in chunks:
        starts = starts_ref.at[pl.ds(first, len(pieces))]
        placings.append(
            Placing(block_rows, starts, pieces, code_refs[: sum(pieces)], outs, scratch[:4])
        )
        code_refs, scratch = code_refs[sum(pieces) :], scratch[4:]
        first += len(pieces)
    for placing in placings:
        placing.fetch()
    for placing in placings:
        placing.place()
    for placing in placings:
        placing.finish()


def placed(received, outs, block_rows):
    operands, starts, chunks, scratch_shapes = [], [], [], []
    for codes, start in received:
        chunks.append([len(parts) for parts in codes])
        operands += sum(codes, [])
        starts.append(start)
        rows, width = codes[0][0].shape
        blocks = rows // coded_rows(block_rows)
        scratch_shapes += Placing.scratch(len(codes), blocks, block_rows, width)
    anywhere = pl.BlockSpec(memory_space=pl.ANY)
    return pl.pallas_call(
        functools.partial(place_kernel, chunks, block_rows),
        grid_spec=pltpu.PrefetchScalarGridSpec(
            num_scalar_prefetch=1,
            grid=(1,),
            in_specs=[anywhere] * (len(operands) + 2),
            out_specs=[anywhere] * 2,
            scratch_shapes=scratch_shapes,
        ),
        out_shape=[jax.ShapeDtypeStruct(out.shape, out.dtype) for out in outs],
        input_output_aliases={1 + len(operands): 0, 2 + len(operands): 1},
        compiler_params=pltpu.CompilerParams(vmem_limit_bytes=vmem_bytes),
        name="placed_rows",
    )(jnp.concatenate(starts).astype(jnp.int32), *operands, *outs)


def combine_kernel(groups, parts_ref, out_ref):
    per_group = parts_ref.shape[0] // groups
    count = parts_ref.shape[2]
    for t in range(groups):
        parts = [parts_ref[t * per_group + k] for k in range(per_group)]
        top = functools.reduce(jnp.maximum, parts)
        total = functools.reduce(jnp.add, [jnp.exp(part - top) for part in parts])
        out_ref[:, t * count : (t + 1) * count] = top + jnp.log(total)


def combined_lse(parts, groups):
    return pl.pallas_call(
        functools.partial(combine_kernel, groups),
        out_shape=jax.ShapeDtypeStruct((1, groups * parts.shape[2]), jnp.float32),
        name="join_stats",
    )(parts)


def blank(shape):
    return pl.pallas_call(
        lambda out_ref: None,
        out_specs=pl.BlockSpec(memory_space=pl.ANY),
        out_shape=jax.ShapeDtypeStruct(shape, jnp.float32),
        name="blank",
    )()


def from_others(value, axis):
    size = lax.axis_size(axis)
    found = [value]
    for s in range(1, size):
        pairs = [(partner(k, s, size), k) for k in range(size)]
        found.append(lax.ppermute(value, axis, pairs))
    return found


def partner(me, s, size):
    return me ^ s if size & (size - 1) == 0 else (me - s) % size


def chunk_plan(blocks):
    plan = []
    while blocks > 2:
        plan.append(2)
        blocks -= 2
    return plan + [1] * blocks


def local(tokens, centroids):
    tok_size, cent_size = lax.axis_size("tok"), lax.axis_size("cent")
    me = lax.axis_index("tok")
    cent_count, width = centroids.shape
    share_rows = cent_count // tok_size

    toks = lax.all_gather(tokens, "tok", axis=0, tiled=True)
    own_lse = local_lse(tokens, centroids, tok_size * cent_size)
    parts = lax.all_to_all(own_lse, ("tok", "cent"), 0, 0, tiled=True)
    lse = combined_lse(parts, tok_size)

    block_rows = divisor(share_rows, 1024)
    sources = jnp.stack([partner(me, s, tok_size) for s in range(tok_size)])
    outs = blank((cent_count, width)), blank((cent_count // 128, 128))
    waiting, first = [], 0
    plan = chunk_plan(share_rows // block_rows)
    for k, blocks in enumerate(plan):
        block = first * tok_size + me * blocks
        after, received = (), None
        if len(waiting) == 2:
            if k + 1 < len(plan):
                received = (*waiting.pop(0), outs)
            else:
                after = sum(waiting[0][0][1:], [])
        codes, *placed_outs = updated_chunk(
            block, toks, lse, centroids, blocks, block_rows, after, received
        )
        outs = placed_outs or outs
        found = [[part] for part in from_others(codes, "tok")]
        waiting.append((found, first * tok_size + sources * blocks))
        first += blocks
    if len(waiting) > 1:
        outs = placed(waiting[:-1], outs, block_rows)
    outs = placed(waiting[-1:], outs, block_rows)
    return outs[0], outs[1].reshape(cent_count)


def solution(mesh):
    placed_as = (P("tok", None), P("cent", None))
    return jax.shard_map(
        local, mesh=mesh, in_specs=placed_as, out_specs=(P("cent", None), P("cent")), check_vma=False
    )
```

```python
import functools

import jax
import jax.numpy as jnp
from jax import lax
from jax.experimental import pallas as pl
from jax.experimental.pallas import tpu as pltpu
from jax.sharding import PartitionSpec as P

inverse_temp = 2.0
prior_weight = 0.05
safe_sum = 1e30
headroom = 60.0
code_scale = 2.0**24
slice_rows = 64
vmem_bytes = 56 * 1024 * 1024


def divisor(count, most):
    size = min(count, most)
    while count % size:
        size //= 2
    return size


def dot_nt(a, b):
    return lax.dot_general(a, b, (((1,), (1,)), ((), ())), preferred_element_type=jnp.float32)


def fold_rows(x, combine):
    parts = [x[k * 8 : (k + 1) * 8, :] for k in range(x.shape[0] // 8)]
    while len(parts) > 1:
        half = len(parts) // 2
        parts = [combine(parts[2 * k], parts[2 * k + 1]) for k in range(half)] + parts[2 * half :]
    return parts[0]


def split_exactly(x):
    high = x.astype(jnp.bfloat16).astype(jnp.float32)
    middle = (x - high).astype(jnp.bfloat16).astype(jnp.float32)
    return high, middle, x - high - middle


def stats_kernel(
    sub_rows, tok_cols, tok_ref, cent_ref, out_ref, flip_ref, base_ref, shift_ref, sums_ref, worst_ref
):
    step = pl.program_id(0)
    tok_count = tok_ref.shape[0]
    subs = cent_ref.shape[0] // sub_rows
    col_blocks = tok_count // tok_cols
    redo_cols = divisor(tok_cols, 256)
    redo_blocks = tok_count // redo_cols

    def columns(t, size=tok_cols):
        return pl.ds(pl.multiple_of(t * size, size), size)

    def dot(a, b):
        return jnp.dot(a, b, preferred_element_type=jnp.float32)

    width = tok_ref.shape[1]

    @pl.when(step == 0)
    def _():
        @pl.loop(0, col_blocks)
        def _(t):
            flipped = (tok_ref[columns(t), :] * jnp.bfloat16(inverse_temp)).T
            flip_ref[0:width, columns(t)] = flipped
            logits = dot(cent_ref[0:128, :], flipped)
            top = jnp.max(fold_rows(logits, jnp.maximum), axis=0, keepdims=True)
            base = top + headroom
            base_ref[:, columns(t)] = base
            row = lax.broadcasted_iota(jnp.int32, (width, tok_cols), 0)
            terms = jnp.zeros((width, tok_cols), jnp.float32)
            for k, term in enumerate(split_exactly(-base)):
                terms = jnp.where(row == k, term, terms)
            flip_ref[width:, columns(t)] = terms.astype(jnp.bfloat16)

    lane = lax.broadcasted_iota(jnp.int32, (sub_rows, width), 1)
    ones = jnp.where(lane < 3, 1.0, 0.0).astype(jnp.bfloat16)

    @pl.loop(0, col_blocks)
    def _(t):
        rhs = flip_ref[:, columns(t)]
        shift = base_ref[:, columns(t)]
        for sub in range(subs):
            total = jnp.zeros((8, tok_cols), jnp.float32)
            lhs = jnp.concatenate([cent_ref[pl.ds(sub * sub_rows, sub_rows), :], ones], axis=1)
            logits = dot(lhs, rhs)
            for first in range(0, sub_rows, slice_rows):
                scaled = jnp.exp(logits[first : first + slice_rows])
                total = total + fold_rows(scaled, jnp.add)
            sums_ref[step * subs + sub, :, columns(t)] = total
            shift_ref[step * subs + sub, :, columns(t)] = shift

    worst = jnp.float32(0.0)
    for sub in range(subs):
        for t in range(redo_blocks):
            block = jnp.max(sums_ref[step * subs + sub, :, t * redo_cols : (t + 1) * redo_cols])
            worst_ref[sub * redo_blocks + t] = block
            worst = jnp.maximum(worst, block)

    @pl.when(jnp.logical_not(worst < safe_sum))
    def _():
        @pl.loop(0, subs * redo_blocks)
        def _(k):
            @pl.when(jnp.logical_not(worst_ref[k] < safe_sum))
            def _():
                sub, t = k // redo_blocks, lax.rem(k, redo_blocks)
                first = pl.multiple_of(sub * sub_rows, sub_rows)
                rhs = flip_ref[0:width, columns(t, redo_cols)]
                logits = dot(cent_ref[pl.ds(first, sub_rows), :], rhs)
                top = jnp.max(fold_rows(logits, jnp.maximum), axis=0, keepdims=True)
                total = fold_rows(jnp.exp(logits - top), jnp.add)
                sums_ref[step * subs + sub, :, columns(t, redo_cols)] = total
                shift_ref[step * subs + sub, :, columns(t, redo_cols)] = top

    @pl.when(step == pl.num_programs(0) - 1)
    def _():
        @pl.loop(0, col_blocks)
        def _(t):
            shifts = shift_ref[:, :, columns(t)]
            top = jnp.max(shifts, axis=0)
            scale = jnp.exp(shifts - top[None])
            total = jnp.sum(sums_ref[:, :, columns(t)] * scale, axis=0)
            total = jnp.sum(total, axis=0, keepdims=True)
            out_ref[:, :, columns(t)] = jnp.broadcast_to(
                (top + jnp.log(total))[None], (out_ref.shape[0], 1, tok_cols)
            )


def local_lse(tokens, centroids, copies):
    tok_count, width = tokens.shape
    cent_count = centroids.shape[0]
    block_rows = divisor(cent_count, 4096)
    sub_rows = divisor(block_rows, 1024)
    tok_cols = divisor(tok_count, 512)
    blocks = cent_count // block_rows
    subs = cent_count // sub_rows
    flags = block_rows // sub_rows * (tok_count // divisor(tok_cols, 256))
    return pl.pallas_call(
        functools.partial(stats_kernel, sub_rows, tok_cols),
        grid=(blocks,),
        in_specs=[
            pl.BlockSpec((tok_count, width), lambda j: (0, 0)),
            pl.BlockSpec((block_rows, width), lambda j: (j, 0)),
        ],
        out_specs=pl.BlockSpec((copies, 1, tok_count), lambda j: (0, 0, 0)),
        out_shape=jax.ShapeDtypeStruct((copies, 1, tok_count), jnp.float32),
        scratch_shapes=[
            pltpu.VMEM((2 * width, tok_count), jnp.bfloat16),
            pltpu.VMEM((1, tok_count), jnp.float32),
            pltpu.VMEM((subs, 1, tok_count), jnp.float32),
            pltpu.VMEM((subs, 8, tok_count), jnp.float32),
            pltpu.SMEM((flags,), jnp.float32),
        ],
        compiler_params=pltpu.CompilerParams(vmem_limit_bytes=vmem_bytes),
        cost_estimate=pl.CostEstimate(
            flops=2 * tok_count * cent_count * width,
            bytes_accessed=(tok_count + cent_count) * width * 2,
            transcendentals=tok_count * cent_count,
        ),
        name="row_stats",
    )(tokens, centroids)


def encoded(x):
    x = x * code_scale
    return (x * jnp.abs(x) * (x * x)).astype(jnp.bfloat16)


def decoded(code):
    code = code.astype(jnp.float32)
    size = lax.rsqrt(lax.rsqrt(jnp.maximum(jnp.abs(code), 1e-37))) * (1.0 / code_scale)
    return jnp.where(code < 0, -size, jnp.where(code > 0, size, 0.0))


class Placing:
    def __init__(self, block_rows, starts_ref, pieces, code_refs, outs, scratch):
        self.block_rows, self.starts_ref = block_rows, starts_ref
        self.pieces, self.code_refs = pieces, code_refs
        self.updated_ref, self.masses_ref = outs
        self.codes, self.values, self.masses, self.sems = scratch

    @staticmethod
    def scratch(sources, blocks, block_rows, width):
        return [
            pltpu.VMEM((sources, blocks * coded_rows(block_rows), width), jnp.bfloat16),
            pltpu.VMEM((sources, blocks * block_rows, width), jnp.float32),
            pltpu.VMEM((sources, blocks * block_rows // 128, 128), jnp.float32),
            pltpu.SemaphoreType.DMA((4, sources)),
        ]

    def copies_in(self):
        found, refs = [], list(self.code_refs)
        for s, count in enumerate(self.pieces):
            found.append([])
            first = 0
            for k in range(count):
                ref = refs.pop(0)
                target = self.codes.at[s, pl.ds(first, ref.shape[0]), :]
                found[s].append(pltpu.make_async_copy(ref, target, self.sems.at[3 * k, s]))
                first += ref.shape[0]
        return found

    def copies_out(self, s):
        rows, mass_rows = self.values.shape[1], self.masses.shape[1]
        start = self.starts_ref[s]
        span = pl.ds(pl.multiple_of(start * self.block_rows, self.block_rows), rows)
        per_block = self.block_rows // 128
        mass_span = pl.ds(pl.multiple_of(start * per_block, per_block), mass_rows)
        return [
            pltpu.make_async_copy(self.values.at[s], self.updated_ref.at[span, :], self.sems.at[1, s]),
            pltpu.make_async_copy(self.masses.at[s], self.masses_ref.at[mass_span, :], self.sems.at[2, s]),
        ]

    def fetch(self):
        for copies in self.copies_in():
            for copy in copies:
                copy.start()

    def place(self):
        block_rows, per_block = self.block_rows, self.block_rows // 128
        full = coded_rows(block_rows)
        tile = divisor(block_rows, 256)
        for s, copies in enumerate(self.copies_in()):
            for copy in copies:
                copy.wait()

            @pl.loop(0, self.values.shape[1] // block_rows)
            def _(b):
                for k in range(block_rows // tile):
                    source = pl.ds(pl.multiple_of(b * full + k * tile, 32), tile)
                    target = pl.ds(pl.multiple_of(b * block_rows + k * tile, tile), tile)
                    self.values[s, target, :] = decoded(self.codes[s, source, :])
                last = pl.ds(pl.multiple_of(b * full + block_rows, 32), full - block_rows)
                terms = self.codes[s, last, :].astype(jnp.float32)
                mass = terms[:per_block] + terms[per_block : 2 * per_block]
                mass = mass + terms[2 * per_block : 3 * per_block]
                self.masses[s, pl.ds(pl.multiple_of(b * per_block, per_block), per_block), :] = mass

            for copy in self.copies_out(s):
                copy.start()

    def finish(self):
        for s in range(len(self.pieces)):
            for copy in self.copies_out(s):
                copy.wait()


def coded_rows(block_rows):
    return block_rows + block_rows // 32


def combine(groups, parts_ref, out_ref):
    per_group = parts_ref.shape[0] // groups
    count = parts_ref.shape[2]
    for t in range(groups):
        parts = [parts_ref[t * per_group + k] for k in range(per_group)]
        top = functools.reduce(jnp.maximum, parts)
        total = functools.reduce(jnp.add, [jnp.exp(part - top) for part in parts])
        out_ref[:, t * count : (t + 1) * count] = top + jnp.log(total)


def update_kernel(joins, unread, pieces, block_rows, *refs):
    place_ref, tok_ref, lse_ref, cent_ref = refs[:4]
    refs = refs[4 + unread :]
    code_refs, refs = refs[: sum(pieces)], refs[sum(pieces) :]
    if pieces:
        code_ref, updated_ref, masses_ref = refs[2:5]
        scratch = refs[5:]
        starts_ref = place_ref.at[pl.ds(1, len(pieces))]
        placing = Placing(
            block_rows, starts_ref, pieces, code_refs, (updated_ref, masses_ref), scratch[3:]
        )
    else:
        code_ref, scratch, placing = refs[0], refs[1:], None
    if joins:
        parts_ref, lse_ref, scratch = lse_ref, scratch[0], scratch[1:]
        pl.when(pl.program_id(0) == 0)(lambda: combine(joins, parts_ref, lse_ref))
    weights_ref, total_ref, mass_ref = scratch[:3]
    step, steps = pl.program_id(0), pl.num_programs(0)
    width = tok_ref.shape[1]
    _, tile, depth = weights_ref.shape
    piece = divisor(depth, 512)
    stages = tok_ref.shape[0] // depth
    tiles = block_rows // tile

    if placing:
        pl.when(step == 0)(placing.fetch)

    def weigh(first, stage):
        cents = cent_ref[pl.ds(first, tile), :] * jnp.bfloat16(inverse_temp)
        for k in range(depth // piece):
            span = pl.ds(stage * depth + k * piece, piece)
            logits = dot_nt(cents, tok_ref[span, :])
            lse = lse_ref[:, span]
            for r in range(0, tile, slice_rows):
                weights = jnp.exp(logits[r : r + slice_rows] - lse).astype(jnp.bfloat16)
                weights_ref[stage % 2, r : r + slice_rows, pl.ds(k * piece, piece)] = weights

    def gather_up(stage):
        toks = tok_ref[pl.ds(stage * depth, depth), :]
        rhs = jnp.concatenate([toks, jnp.ones_like(toks)], axis=1)
        part = jnp.dot(weights_ref[stage % 2], rhs, preferred_element_type=jnp.float32)
        if stage == 0:
            total_ref[...] = part
        else:
            total_ref[...] += part

    diagonal = lax.broadcasted_iota(jnp.int32, (128, 128), 0) == lax.broadcasted_iota(
        jnp.int32, (128, 128), 1
    )

    def run(r):
        first = pl.multiple_of(r * tile, tile)
        weigh(first, 0)
        for stage in range(1, stages):
            weigh(first, stage)
            gather_up(stage - 1)
        gather_up(stages - 1)
        mass = total_ref[:, width : 2 * width]
        prior = prior_weight * cent_ref[pl.ds(first, tile), :].astype(jnp.float32)
        new = (total_ref[:, 0:width] + prior) / (mass + prior_weight)
        code_ref[pl.ds(first, tile), :] = encoded(new)
        for k in range(tile // 128):
            square = jnp.where(diagonal, mass[k * 128 : (k + 1) * 128, :], 0.0)
            mass_ref[pl.ds(r * (tile // 128) + k, 1), :] = jnp.sum(square, axis=0, keepdims=True)

    pl.loop(0, tiles // 2)(run)
    if placing:
        pl.when(step == 0)(placing.place)
    pl.loop(tiles // 2, tiles)(run)

    terms = split_exactly(mass_ref[...])
    terms = jnp.concatenate([*terms, jnp.zeros_like(terms[0])], axis=0)
    code_ref[block_rows : block_rows + terms.shape[0], :] = terms.astype(jnp.bfloat16)
    if placing:
        pl.when(step == steps - 1)(placing.finish)


def updated_chunk(block, toks, lse, centroids, blocks, block_rows, after=(), received=None, joins=0):
    all_count, width = toks.shape
    depth = divisor(all_count, 2048)
    tile = divisor(block_rows, 1024)
    rows = blocks * block_rows
    full = coded_rows(block_rows)
    anywhere = pl.BlockSpec(memory_space=pl.ANY)
    whole = lambda j, place: (0, 0)
    place, operands = block.reshape(1), [toks, lse, centroids, *after]
    in_specs = [
        pl.BlockSpec((all_count, width), whole),
        pl.BlockSpec(lse.shape, (lambda j, place: (0, 0, 0)) if joins else whole),
        pl.BlockSpec((block_rows, width), lambda j, place: (place[0] + j, 0)),
    ] + [anywhere] * len(after)
    out_specs = [pl.BlockSpec((full, width), lambda j, place: (j, 0))]
    out_shape = [jax.ShapeDtypeStruct((blocks * full, width), jnp.bfloat16)]
    scratch_shapes = [
        pltpu.VMEM((2, tile, depth), jnp.bfloat16),
        pltpu.VMEM((tile, 2 * width), jnp.float32),
        pltpu.VMEM((block_rows // 128, 128), jnp.float32),
    ]
    aliases, pieces = {}, []
    if joins:
        out_specs.append(pl.BlockSpec((1, all_count), whole))
        out_shape.append(jax.ShapeDtypeStruct((1, all_count), jnp.float32))
    if received:
        codes, starts, outs = received
        pieces = [len(parts) for parts in codes]
        place = jnp.concatenate([place, starts])
        operands += [*sum(codes, []), *outs]
        in_specs += [anywhere] * (sum(pieces) + 2)
        out_specs += [anywhere] * 2
        out_shape += [jax.ShapeDtypeStruct(out.shape, out.dtype) for out in outs]
        aliases = {len(operands) - 1: 1, len(operands): 2}
        scratch_shapes += Placing.scratch(len(codes), codes[0][0].shape[0] // full, block_rows, width)
    return pl.pallas_call(
        functools.partial(update_kernel, joins, len(after), pieces, block_rows),
        grid_spec=pltpu.PrefetchScalarGridSpec(
            num_scalar_prefetch=1,
            grid=(blocks,),
            in_specs=in_specs,
            out_specs=out_specs,
            scratch_shapes=scratch_shapes,
        ),
        out_shape=out_shape,
        input_output_aliases=aliases,
        compiler_params=pltpu.CompilerParams(vmem_limit_bytes=vmem_bytes * 3 // 4),
        cost_estimate=pl.CostEstimate(
            flops=6 * all_count * rows * width,
            bytes_accessed=(2 * all_count + 4 * rows) * width,
            transcendentals=all_count * rows,
        ),
        name="new_rows",
    )(place.astype(jnp.int32), *operands)


def place_kernel(chunks, block_rows, starts_ref, *refs):
    count = sum(map(sum, chunks))
    code_refs, outs, scratch = refs[:count], refs[count + 2 : count + 4], refs[count + 4 :]
    placings, first = [], 0
    for pieces in chunks:
        starts = starts_ref.at[pl.ds(first, len(pieces))]
        placings.append(
            Placing(block_rows, starts, pieces, code_refs[: sum(pieces)], outs, scratch[:4])
        )
        code_refs, scratch = code_refs[sum(pieces) :], scratch[4:]
        first += len(pieces)
    for placing in placings:
        placing.fetch()
    for placing in placings:
        placing.place()
    for placing in placings:
        placing.finish()


def placed(received, outs, block_rows):
    operands, starts, chunks, scratch_shapes = [], [], [], []
    for codes, start in received:
        chunks.append([len(parts) for parts in codes])
        operands += sum(codes, [])
        starts.append(start)
        rows, width = codes[0][0].shape
        blocks = rows // coded_rows(block_rows)
        scratch_shapes += Placing.scratch(len(codes), blocks, block_rows, width)
    anywhere = pl.BlockSpec(memory_space=pl.ANY)
    return pl.pallas_call(
        functools.partial(place_kernel, chunks, block_rows),
        grid_spec=pltpu.PrefetchScalarGridSpec(
            num_scalar_prefetch=1,
            grid=(1,),
            in_specs=[anywhere] * (len(operands) + 2),
            out_specs=[anywhere] * 2,
            scratch_shapes=scratch_shapes,
        ),
        out_shape=[jax.ShapeDtypeStruct(out.shape, out.dtype) for out in outs],
        input_output_aliases={1 + len(operands): 0, 2 + len(operands): 1},
        compiler_params=pltpu.CompilerParams(vmem_limit_bytes=vmem_bytes // 2),
        name="placed_rows",
    )(jnp.concatenate(starts).astype(jnp.int32), *operands, *outs)


def blank(shape):
    return pl.pallas_call(
        lambda out_ref: None,
        out_specs=pl.BlockSpec(memory_space=pl.ANY),
        out_shape=jax.ShapeDtypeStruct(shape, jnp.float32),
        name="blank",
    )()


def from_others(value, axis):
    size = lax.axis_size(axis)
    found = [value]
    for s in range(1, size):
        pairs = [(partner(k, s, size), k) for k in range(size)]
        found.append(lax.ppermute(value, axis, pairs))
    return found


def partner(me, s, size):
    return me ^ s if size & (size - 1) == 0 else (me - s) % size


def chunk_plan(blocks):
    plan = []
    while blocks > 2:
        plan.append(2)
        blocks -= 2
    return plan + [1] * blocks


def local(tokens, centroids):
    tok_size, cent_size = lax.axis_size("tok"), lax.axis_size("cent")
    me = lax.axis_index("tok")
    cent_count, width = centroids.shape
    share_rows = cent_count // tok_size

    toks = lax.all_gather(tokens, "tok", axis=0, tiled=True)
    own_lse = local_lse(tokens, centroids, tok_size * cent_size)
    parts = lax.all_to_all(own_lse, ("tok", "cent"), 0, 0, tiled=True)

    block_rows = divisor(share_rows, 1024)
    sources = jnp.stack([partner(me, s, tok_size) for s in range(tok_size)])
    outs = blank((cent_count, width)), blank((cent_count // 128, 128))
    waiting, first = [], 0
    plan = chunk_plan(share_rows // block_rows)
    for k, blocks in enumerate(plan):
        block = first * tok_size + me * blocks
        arrived, received = [], None
        if len(waiting) > 1:
            arrived = sum(waiting[-2][0][1:], [])
            if blocks == 1:
                received = (*waiting.pop(0), outs)
                arrived = arrived if waiting[1:] else []
        operands = toks, lse if k else parts, centroids, blocks, block_rows, arrived, received
        codes, *rest = updated_chunk(block, *operands, joins=0 if k else tok_size)
        if not k:
            (lse,) = rest
        elif received:
            outs = rest
        found = [[part] for part in from_others(codes, "tok")]
        waiting.append((found, first * tok_size + sources * blocks))
        first += blocks
    if len(waiting) > 1:
        outs = placed(waiting[:-1], outs, block_rows)
    outs = placed(waiting[-1:], outs, block_rows)
    return outs[0], outs[1].reshape(cent_count)


def solution(mesh):
    placed_as = (P("tok", None), P("cent", None))
    return jax.shard_map(
        local, mesh=mesh, in_specs=placed_as, out_specs=(P("cent", None), P("cent")), check_vma=False
    )
```

```python
import functools

import jax
import jax.numpy as jnp
from jax import lax
from jax.experimental import pallas as pl
from jax.experimental.pallas import tpu as pltpu
from jax.sharding import PartitionSpec as P

inverse_temp = 2.0
prior_weight = 0.05
safe_sum = 1e30
headroom = 60.0
code_scale = 2.0**24
slice_rows = 64
vmem_bytes = 56 * 1024 * 1024


def divisor(count, most):
    size = min(count, most)
    while count % size:
        size //= 2
    return size


def dot_nt(a, b):
    return lax.dot_general(a, b, (((1,), (1,)), ((), ())), preferred_element_type=jnp.float32)


def fold_rows(x, combine):
    parts = [x[k * 8 : (k + 1) * 8, :] for k in range(x.shape[0] // 8)]
    while len(parts) > 1:
        half = len(parts) // 2
        parts = [combine(parts[2 * k], parts[2 * k + 1]) for k in range(half)] + parts[2 * half :]
    return parts[0]


def split_exactly(x):
    high = x.astype(jnp.bfloat16).astype(jnp.float32)
    middle = (x - high).astype(jnp.bfloat16).astype(jnp.float32)
    return high, middle, x - high - middle


def stats_kernel(
    sub_rows, tok_cols, tok_ref, cent_ref, out_ref, flip_ref, base_ref, shift_ref, sums_ref, worst_ref
):
    step = pl.program_id(0)
    tok_count = tok_ref.shape[0]
    subs = cent_ref.shape[0] // sub_rows
    col_blocks = tok_count // tok_cols
    redo_cols = divisor(tok_cols, 128)
    redo_blocks = tok_count // redo_cols

    def columns(t, size=tok_cols):
        return pl.ds(pl.multiple_of(t * size, size), size)

    def dot(a, b):
        return jnp.dot(a, b, preferred_element_type=jnp.float32)

    width = tok_ref.shape[1]

    @pl.when(step == 0)
    def _():
        @pl.loop(0, col_blocks)
        def _(t):
            flipped = (tok_ref[columns(t), :] * jnp.bfloat16(inverse_temp)).T
            flip_ref[0:width, columns(t)] = flipped
            logits = dot(cent_ref[0:128, :], flipped)
            top = jnp.max(fold_rows(logits, jnp.maximum), axis=0, keepdims=True)
            base = top + headroom
            base_ref[:, columns(t)] = base
            row = lax.broadcasted_iota(jnp.int32, (width, tok_cols), 0)
            terms = jnp.zeros((width, tok_cols), jnp.float32)
            for k, term in enumerate(split_exactly(-base)):
                terms = jnp.where(row == k, term, terms)
            flip_ref[width:, columns(t)] = terms.astype(jnp.bfloat16)

    lane = lax.broadcasted_iota(jnp.int32, (sub_rows, width), 1)
    ones = jnp.where(lane < 3, 1.0, 0.0).astype(jnp.bfloat16)

    @pl.loop(0, col_blocks)
    def _(t):
        rhs = flip_ref[:, columns(t)]
        shift = base_ref[:, columns(t)]
        for sub in range(subs):
            total = jnp.zeros((8, tok_cols), jnp.float32)
            lhs = jnp.concatenate([cent_ref[pl.ds(sub * sub_rows, sub_rows), :], ones], axis=1)
            logits = dot(lhs, rhs)
            for first in range(0, sub_rows, slice_rows):
                scaled = jnp.exp(logits[first : first + slice_rows])
                total = total + fold_rows(scaled, jnp.add)
            sums_ref[step * subs + sub, :, columns(t)] = total
            shift_ref[step * subs + sub, :, columns(t)] = shift

    worst = jnp.float32(0.0)
    for sub in range(subs):
        for t in range(redo_blocks):
            block = jnp.max(sums_ref[step * subs + sub, :, t * redo_cols : (t + 1) * redo_cols])
            worst_ref[sub * redo_blocks + t] = block
            worst = jnp.maximum(worst, block)

    @pl.when(jnp.logical_not(worst < safe_sum))
    def _():
        @pl.loop(0, subs * redo_blocks)
        def _(k):
            @pl.when(jnp.logical_not(worst_ref[k] < safe_sum))
            def _():
                sub, t = k // redo_blocks, lax.rem(k, redo_blocks)
                first = pl.multiple_of(sub * sub_rows, sub_rows)
                rhs = flip_ref[0:width, columns(t, redo_cols)]
                logits = dot(cent_ref[pl.ds(first, sub_rows), :], rhs)
                top = jnp.max(fold_rows(logits, jnp.maximum), axis=0, keepdims=True)
                total = fold_rows(jnp.exp(logits - top), jnp.add)
                sums_ref[step * subs + sub, :, columns(t, redo_cols)] = total
                shift_ref[step * subs + sub, :, columns(t, redo_cols)] = top

    @pl.when(step == pl.num_programs(0) - 1)
    def _():
        @pl.loop(0, col_blocks)
        def _(t):
            shifts = shift_ref[:, :, columns(t)]
            top = jnp.max(shifts, axis=0)
            scale = jnp.exp(shifts - top[None])
            total = jnp.sum(sums_ref[:, :, columns(t)] * scale, axis=0)
            total = jnp.sum(total, axis=0, keepdims=True)
            out_ref[:, :, columns(t)] = jnp.broadcast_to(
                (top + jnp.log(total))[None], (out_ref.shape[0], 1, tok_cols)
            )


def local_lse(tokens, centroids, copies):
    tok_count, width = tokens.shape
    cent_count = centroids.shape[0]
    block_rows = divisor(cent_count, 4096)
    sub_rows = divisor(block_rows, 1024)
    tok_cols = divisor(tok_count, 512)
    blocks = cent_count // block_rows
    subs = cent_count // sub_rows
    flags = block_rows // sub_rows * (tok_count // divisor(tok_cols, 128))
    return pl.pallas_call(
        functools.partial(stats_kernel, sub_rows, tok_cols),
        grid=(blocks,),
        in_specs=[
            pl.BlockSpec((tok_count, width), lambda j: (0, 0)),
            pl.BlockSpec((block_rows, width), lambda j: (j, 0)),
        ],
        out_specs=pl.BlockSpec((copies, 1, tok_count), lambda j: (0, 0, 0)),
        out_shape=jax.ShapeDtypeStruct((copies, 1, tok_count), jnp.float32),
        scratch_shapes=[
            pltpu.VMEM((2 * width, tok_count), jnp.bfloat16),
            pltpu.VMEM((1, tok_count), jnp.float32),
            pltpu.VMEM((subs, 1, tok_count), jnp.float32),
            pltpu.VMEM((subs, 8, tok_count), jnp.float32),
            pltpu.SMEM((flags,), jnp.float32),
        ],
        compiler_params=pltpu.CompilerParams(vmem_limit_bytes=vmem_bytes),
        cost_estimate=pl.CostEstimate(
            flops=2 * tok_count * cent_count * width,
            bytes_accessed=(tok_count + cent_count) * width * 2,
            transcendentals=tok_count * cent_count,
        ),
        name="row_stats",
    )(tokens, centroids)


def encoded(x):
    x = x * code_scale
    return (x * jnp.abs(x) * (x * x)).astype(jnp.bfloat16)


def decoded(code):
    code = code.astype(jnp.float32)
    size = lax.rsqrt(lax.rsqrt(jnp.maximum(jnp.abs(code), 1e-37))) * (1.0 / code_scale)
    return jnp.where(code < 0, -size, jnp.where(code > 0, size, 0.0))


class Placing:
    def __init__(self, block_rows, starts_ref, pieces, code_refs, outs, scratch):
        self.block_rows, self.starts_ref = block_rows, starts_ref
        self.pieces, self.code_refs = pieces, code_refs
        self.updated_ref, self.masses_ref = outs
        self.codes, self.values, self.masses, self.sems = scratch

    @staticmethod
    def scratch(sources, blocks, block_rows, width):
        return [
            pltpu.VMEM((sources, blocks * coded_rows(block_rows), width), jnp.bfloat16),
            pltpu.VMEM((sources, blocks * block_rows, width), jnp.float32),
            pltpu.VMEM((sources, blocks * block_rows // 128, 128), jnp.float32),
            pltpu.SemaphoreType.DMA((4, sources)),
        ]

    def copies_in(self):
        found, refs = [], list(self.code_refs)
        for s, count in enumerate(self.pieces):
            found.append([])
            first = 0
            for k in range(count):
                ref = refs.pop(0)
                target = self.codes.at[s, pl.ds(first, ref.shape[0]), :]
                found[s].append(pltpu.make_async_copy(ref, target, self.sems.at[3 * k, s]))
                first += ref.shape[0]
        return found

    def copies_out(self, s):
        rows, mass_rows = self.values.shape[1], self.masses.shape[1]
        start = self.starts_ref[s]
        span = pl.ds(pl.multiple_of(start * self.block_rows, self.block_rows), rows)
        per_block = self.block_rows // 128
        mass_span = pl.ds(pl.multiple_of(start * per_block, per_block), mass_rows)
        return [
            pltpu.make_async_copy(self.values.at[s], self.updated_ref.at[span, :], self.sems.at[1, s]),
            pltpu.make_async_copy(self.masses.at[s], self.masses_ref.at[mass_span, :], self.sems.at[2, s]),
        ]

    def fetch(self):
        for copies in self.copies_in():
            for copy in copies:
                copy.start()

    def place(self):
        block_rows, per_block = self.block_rows, self.block_rows // 128
        full = coded_rows(block_rows)
        tile = divisor(block_rows, 256)
        for s, copies in enumerate(self.copies_in()):
            for copy in copies:
                copy.wait()

            @pl.loop(0, self.values.shape[1] // block_rows)
            def _(b):
                for k in range(block_rows // tile):
                    source = pl.ds(pl.multiple_of(b * full + k * tile, 32), tile)
                    target = pl.ds(pl.multiple_of(b * block_rows + k * tile, tile), tile)
                    self.values[s, target, :] = decoded(self.codes[s, source, :])
                last = pl.ds(pl.multiple_of(b * full + block_rows, 32), full - block_rows)
                terms = self.codes[s, last, :].astype(jnp.float32)
                mass = terms[:per_block] + terms[per_block : 2 * per_block]
                mass = mass + terms[2 * per_block : 3 * per_block]
                self.masses[s, pl.ds(pl.multiple_of(b * per_block, per_block), per_block), :] = mass

            for copy in self.copies_out(s):
                copy.start()

    def finish(self):
        for s in range(len(self.pieces)):
            for copy in self.copies_out(s):
                copy.wait()


def coded_rows(block_rows):
    return block_rows + block_rows // 32


def combine(groups, parts_ref, out_ref):
    per_group = parts_ref.shape[0] // groups
    count = parts_ref.shape[2]
    for t in range(groups):
        parts = [parts_ref[t * per_group + k] for k in range(per_group)]
        top = functools.reduce(jnp.maximum, parts)
        total = functools.reduce(jnp.add, [jnp.exp(part - top) for part in parts])
        out_ref[:, t * count : (t + 1) * count] = top + jnp.log(total)


def update_kernel(joins, unread, pieces, block_rows, *refs):
    place_ref, tok_ref, lse_ref, cent_ref = refs[:4]
    refs = refs[4 + unread :]
    code_refs, refs = refs[: sum(pieces)], refs[sum(pieces) :]
    if pieces:
        code_ref, updated_ref, masses_ref = refs[2:5]
        scratch = refs[5:]
        starts_ref = place_ref.at[pl.ds(1, len(pieces))]
        placing = Placing(
            block_rows, starts_ref, pieces, code_refs, (updated_ref, masses_ref), scratch[3:]
        )
    else:
        code_ref, scratch, placing = refs[0], refs[1:], None
    if joins:
        parts_ref, lse_ref, scratch = lse_ref, scratch[0], scratch[1:]
        pl.when(pl.program_id(0) == 0)(lambda: combine(joins, parts_ref, lse_ref))
    weights_ref, total_ref, mass_ref = scratch[:3]
    step, steps = pl.program_id(0), pl.num_programs(0)
    width = tok_ref.shape[1]
    _, tile, depth = weights_ref.shape
    piece = divisor(depth, 512)
    stages = tok_ref.shape[0] // depth
    tiles = block_rows // tile

    if placing:
        pl.when(step == 0)(placing.fetch)

    def weigh(first, stage):
        cents = cent_ref[pl.ds(first, tile), :] * jnp.bfloat16(inverse_temp)
        for k in range(depth // piece):
            span = pl.ds(stage * depth + k * piece, piece)
            logits = dot_nt(cents, tok_ref[span, :])
            lse = lse_ref[:, span]
            for r in range(0, tile, slice_rows):
                weights = jnp.exp(logits[r : r + slice_rows] - lse).astype(jnp.bfloat16)
                weights_ref[stage % 2, r : r + slice_rows, pl.ds(k * piece, piece)] = weights

    def gather_up(stage):
        toks = tok_ref[pl.ds(stage * depth, depth), :]
        rhs = jnp.concatenate([toks, jnp.ones_like(toks)], axis=1)
        part = jnp.dot(weights_ref[stage % 2], rhs, preferred_element_type=jnp.float32)
        if stage == 0:
            total_ref[...] = part
        else:
            total_ref[...] += part

    diagonal = lax.broadcasted_iota(jnp.int32, (128, 128), 0) == lax.broadcasted_iota(
        jnp.int32, (128, 128), 1
    )

    def run(r):
        first = pl.multiple_of(r * tile, tile)
        weigh(first, 0)
        for stage in range(1, stages):
            weigh(first, stage)
            gather_up(stage - 1)
        gather_up(stages - 1)
        mass = total_ref[:, width : 2 * width]
        prior = prior_weight * cent_ref[pl.ds(first, tile), :].astype(jnp.float32)
        new = (total_ref[:, 0:width] + prior) / (mass + prior_weight)
        code_ref[pl.ds(first, tile), :] = encoded(new)
        for k in range(tile // 128):
            square = jnp.where(diagonal, mass[k * 128 : (k + 1) * 128, :], 0.0)
            mass_ref[pl.ds(r * (tile // 128) + k, 1), :] = jnp.sum(square, axis=0, keepdims=True)

    pl.loop(0, tiles // 2)(run)
    if placing:
        pl.when(step == 0)(placing.place)
    pl.loop(tiles // 2, tiles)(run)

    terms = split_exactly(mass_ref[...])
    terms = jnp.concatenate([*terms, jnp.zeros_like(terms[0])], axis=0)
    code_ref[block_rows : block_rows + terms.shape[0], :] = terms.astype(jnp.bfloat16)
    if placing:
        pl.when(step == steps - 1)(placing.finish)


def updated_chunk(block, toks, lse, centroids, blocks, block_rows, after=(), received=None, joins=0):
    all_count, width = toks.shape
    depth = divisor(all_count, 2048)
    tile = divisor(block_rows, 1024)
    rows = blocks * block_rows
    full = coded_rows(block_rows)
    anywhere = pl.BlockSpec(memory_space=pl.ANY)
    whole = lambda j, place: (0, 0)
    place, operands = block.reshape(1), [
        pltpu.with_memory_space_constraint(toks, pltpu.HBM),
        lse,
        pltpu.with_memory_space_constraint(centroids, pltpu.HBM),
        *after,
    ]
    in_specs = [
        pl.BlockSpec((all_count, width), whole),
        pl.BlockSpec(lse.shape, (lambda j, place: (0, 0, 0)) if joins else whole),
        pl.BlockSpec((block_rows, width), lambda j, place: (place[0] + j, 0)),
    ] + [anywhere] * len(after)
    out_specs = [pl.BlockSpec((full, width), lambda j, place: (j, 0))]
    out_shape = [jax.ShapeDtypeStruct((blocks * full, width), jnp.bfloat16)]
    scratch_shapes = [
        pltpu.VMEM((2, tile, depth), jnp.bfloat16),
        pltpu.VMEM((tile, 2 * width), jnp.float32),
        pltpu.VMEM((block_rows // 128, 128), jnp.float32),
    ]
    aliases, pieces = {}, []
    if joins:
        out_specs.append(pl.BlockSpec((1, all_count), whole))
        out_shape.append(jax.ShapeDtypeStruct((1, all_count), jnp.float32))
    if received:
        codes, starts, outs = received
        pieces = [len(parts) for parts in codes]
        place = jnp.concatenate([place, starts])
        operands += [*sum(codes, []), *outs]
        in_specs += [anywhere] * (sum(pieces) + 2)
        out_specs += [anywhere] * 2
        out_shape += [jax.ShapeDtypeStruct(out.shape, out.dtype) for out in outs]
        aliases = {len(operands) - 1: 1, len(operands): 2}
        scratch_shapes += Placing.scratch(len(codes), codes[0][0].shape[0] // full, block_rows, width)
    return pl.pallas_call(
        functools.partial(update_kernel, joins, len(after), pieces, block_rows),
        grid_spec=pltpu.PrefetchScalarGridSpec(
            num_scalar_prefetch=1,
            grid=(blocks,),
            in_specs=in_specs,
            out_specs=out_specs,
            scratch_shapes=scratch_shapes,
        ),
        out_shape=out_shape,
        input_output_aliases=aliases,
        compiler_params=pltpu.CompilerParams(vmem_limit_bytes=vmem_bytes * 3 // 4),
        cost_estimate=pl.CostEstimate(
            flops=6 * all_count * rows * width // 8,
            bytes_accessed=(2 * all_count + 4 * rows) * width // 8,
            transcendentals=all_count * rows // 8,
        ),
        name="new_rows",
    )(place.astype(jnp.int32), *operands)


def place_kernel(chunks, block_rows, starts_ref, *refs):
    count = sum(map(sum, chunks))
    code_refs, outs, scratch = refs[:count], refs[count + 2 : count + 4], refs[count + 4 :]
    placings, first = [], 0
    for pieces in chunks:
        starts = starts_ref.at[pl.ds(first, len(pieces))]
        placings.append(
            Placing(block_rows, starts, pieces, code_refs[: sum(pieces)], outs, scratch[:4])
        )
        code_refs, scratch = code_refs[sum(pieces) :], scratch[4:]
        first += len(pieces)
    for placing in placings:
        placing.fetch()
    for placing in placings:
        placing.place()
    for placing in placings:
        placing.finish()


def placed(received, outs, block_rows):
    operands, starts, chunks, scratch_shapes = [], [], [], []
    for codes, start in received:
        chunks.append([len(parts) for parts in codes])
        operands += sum(codes, [])
        starts.append(start)
        rows, width = codes[0][0].shape
        blocks = rows // coded_rows(block_rows)
        scratch_shapes += Placing.scratch(len(codes), blocks, block_rows, width)
    anywhere = pl.BlockSpec(memory_space=pl.ANY)
    return pl.pallas_call(
        functools.partial(place_kernel, chunks, block_rows),
        grid_spec=pltpu.PrefetchScalarGridSpec(
            num_scalar_prefetch=1,
            grid=(1,),
            in_specs=[anywhere] * (len(operands) + 2),
            out_specs=[anywhere] * 2,
            scratch_shapes=scratch_shapes,
        ),
        out_shape=[jax.ShapeDtypeStruct(out.shape, out.dtype) for out in outs],
        input_output_aliases={1 + len(operands): 0, 2 + len(operands): 1},
        compiler_params=pltpu.CompilerParams(vmem_limit_bytes=vmem_bytes // 2),
        name="placed_rows",
    )(jnp.concatenate(starts).astype(jnp.int32), *operands, *outs)


def blank(shape):
    return pl.pallas_call(
        lambda out_ref: None,
        out_specs=pl.BlockSpec(memory_space=pl.ANY),
        out_shape=jax.ShapeDtypeStruct(shape, jnp.float32),
        name="blank",
    )()


def from_others(value, axis):
    size = lax.axis_size(axis)
    found = [value]
    for s in range(1, size):
        pairs = [(partner(k, s, size), k) for k in range(size)]
        found.append(lax.ppermute(value, axis, pairs))
    return found


def partner(me, s, size):
    return me ^ s if size & (size - 1) == 0 else (me - s) % size


def chunk_plan(blocks):
    plan = []
    while blocks > 2:
        plan.append(2)
        blocks -= 2
    return plan + [1] * blocks


def local(tokens, centroids):
    tok_size, cent_size = lax.axis_size("tok"), lax.axis_size("cent")
    me = lax.axis_index("tok")
    cent_count, width = centroids.shape
    share_rows = cent_count // tok_size

    toks = lax.all_gather(tokens, "tok", axis=0, tiled=True)
    own_lse = local_lse(tokens, centroids, tok_size * cent_size)
    parts = lax.all_to_all(own_lse, ("tok", "cent"), 0, 0, tiled=True)

    block_rows = divisor(share_rows, 1024)
    sources = jnp.stack([partner(me, s, tok_size) for s in range(tok_size)])
    outs = blank((cent_count, width)), blank((cent_count // 128, 128))
    waiting, first = [], 0
    plan = chunk_plan(share_rows // block_rows)
    for k, blocks in enumerate(plan):
        block = first * tok_size + me * blocks
        arrived, received = [], None
        if len(waiting) > 1:
            arrived = sum(waiting[-2][0][1:], [])
            if blocks == 1:
                received = (*waiting.pop(0), outs)
                arrived = arrived[:1] if k + 1 == len(plan) else arrived
        operands = toks, lse if k else parts, centroids, blocks, block_rows, arrived, received
        codes, *rest = updated_chunk(block, *operands, joins=0 if k else tok_size)
        if not k:
            (lse,) = rest
        elif received:
            outs = rest
        found = [[part] for part in from_others(codes, "tok")]
        waiting.append((found, first * tok_size + sources * blocks))
        first += blocks
    if len(waiting) > 1:
        outs = placed(waiting[:-1], outs, block_rows)
    outs = placed(waiting[-1:], outs, block_rows)
    return outs[0], outs[1].reshape(cent_count)


def solution(mesh):
    placed_as = (P("tok", None), P("cent", None))
    return jax.shard_map(
        local, mesh=mesh, in_specs=placed_as, out_specs=(P("cent", None), P("cent")), check_vma=False
    )
```

```python
import functools

import jax
import jax.numpy as jnp
import numpy as np
from jax import lax
from jax.experimental import pallas as pl
from jax.experimental.pallas import tpu as pltpu
from jax.sharding import PartitionSpec as P

inverse_temp = 2.0
prior_weight = 0.05
safe_sum = 1e30
headroom = 60.0
code_scale = 2.0**24
slice_rows = 64
vmem_bytes = 56 * 1024 * 1024


def divisor(count, most):
    size = min(count, most)
    while count % size:
        size //= 2
    return size


def dot_nt(a, b):
    return lax.dot_general(a, b, (((1,), (1,)), ((), ())), preferred_element_type=jnp.float32)


def fold_rows(x, combine):
    parts = [x[k * 8 : (k + 1) * 8, :] for k in range(x.shape[0] // 8)]
    while len(parts) > 1:
        half = len(parts) // 2
        parts = [combine(parts[2 * k], parts[2 * k + 1]) for k in range(half)] + parts[2 * half :]
    return parts[0]


def split_exactly(x):
    high = x.astype(jnp.bfloat16).astype(jnp.float32)
    middle = (x - high).astype(jnp.bfloat16).astype(jnp.float32)
    return high, middle, x - high - middle


def stats_kernel(
    sub_rows, tok_cols, tok_ref, cent_ref, out_ref, flip_ref, base_ref, shift_ref, sums_ref, worst_ref
):
    step = pl.program_id(0)
    tok_count = tok_ref.shape[0]
    subs = cent_ref.shape[0] // sub_rows
    col_blocks = tok_count // tok_cols
    redo_cols = divisor(tok_cols, 256)
    redo_blocks = tok_count // redo_cols

    def columns(t, size=tok_cols):
        return pl.ds(pl.multiple_of(t * size, size), size)

    def dot(a, b):
        return jnp.dot(a, b, preferred_element_type=jnp.float32)

    width = tok_ref.shape[1]

    @pl.when(step == 0)
    def _():
        @pl.loop(0, col_blocks)
        def _(t):
            flipped = (tok_ref[columns(t), :] * jnp.bfloat16(inverse_temp)).T
            flip_ref[0:width, columns(t)] = flipped
            logits = dot(cent_ref[0:128, :], flipped)
            top = jnp.max(fold_rows(logits, jnp.maximum), axis=0, keepdims=True)
            base = top + headroom
            base_ref[:, columns(t)] = base
            row = lax.broadcasted_iota(jnp.int32, (width, tok_cols), 0)
            terms = jnp.zeros((width, tok_cols), jnp.float32)
            for k, term in enumerate(split_exactly(-base)):
                terms = jnp.where(row == k, term, terms)
            flip_ref[width:, columns(t)] = terms.astype(jnp.bfloat16)

    lane = lax.broadcasted_iota(jnp.int32, (sub_rows, width), 1)
    ones = jnp.where(lane < 3, 1.0, 0.0).astype(jnp.bfloat16)

    @pl.loop(0, col_blocks)
    def _(t):
        rhs = flip_ref[:, columns(t)]
        shift = base_ref[:, columns(t)]
        for sub in range(subs):
            total = jnp.zeros((8, tok_cols), jnp.float32)
            lhs = jnp.concatenate([cent_ref[pl.ds(sub * sub_rows, sub_rows), :], ones], axis=1)
            logits = dot(lhs, rhs)
            for first in range(0, sub_rows, slice_rows):
                scaled = jnp.exp(logits[first : first + slice_rows])
                total = total + fold_rows(scaled, jnp.add)
            sums_ref[step * subs + sub, :, columns(t)] = total
            shift_ref[step * subs + sub, :, columns(t)] = shift

    worst = jnp.float32(0.0)
    for sub in range(subs):
        for t in range(redo_blocks):
            block = jnp.max(sums_ref[step * subs + sub, :, t * redo_cols : (t + 1) * redo_cols])
            worst_ref[sub * redo_blocks + t] = block
            worst = jnp.maximum(worst, block)

    @pl.when(jnp.logical_not(worst < safe_sum))
    def _():
        @pl.loop(0, subs * redo_blocks)
        def _(k):
            @pl.when(jnp.logical_not(worst_ref[k] < safe_sum))
            def _():
                sub, t = k // redo_blocks, lax.rem(k, redo_blocks)
                first = pl.multiple_of(sub * sub_rows, sub_rows)
                rhs = flip_ref[0:width, columns(t, redo_cols)]
                logits = dot(cent_ref[pl.ds(first, sub_rows), :], rhs)
                top = jnp.max(fold_rows(logits, jnp.maximum), axis=0, keepdims=True)
                total = fold_rows(jnp.exp(logits - top), jnp.add)
                sums_ref[step * subs + sub, :, columns(t, redo_cols)] = total
                shift_ref[step * subs + sub, :, columns(t, redo_cols)] = top

    @pl.when(step == pl.num_programs(0) - 1)
    def _():
        @pl.loop(0, col_blocks)
        def _(t):
            shifts = shift_ref[:, :, columns(t)]
            top = jnp.max(shifts, axis=0)
            scale = jnp.exp(shifts - top[None])
            total = jnp.sum(sums_ref[:, :, columns(t)] * scale, axis=0)
            total = jnp.sum(total, axis=0, keepdims=True)
            out_ref[:, :, columns(t)] = jnp.broadcast_to(
                (top + jnp.log(total))[None], (out_ref.shape[0], 1, tok_cols)
            )


def local_lse(tokens, centroids, copies):
    tok_count, width = tokens.shape
    cent_count = centroids.shape[0]
    block_rows = divisor(cent_count, 4096)
    sub_rows = divisor(block_rows, 1024)
    tok_cols = divisor(tok_count, 512)
    blocks = cent_count // block_rows
    subs = cent_count // sub_rows
    flags = block_rows // sub_rows * (tok_count // divisor(tok_cols, 256))
    return pl.pallas_call(
        functools.partial(stats_kernel, sub_rows, tok_cols),
        grid=(blocks,),
        in_specs=[
            pl.BlockSpec((tok_count, width), lambda j: (0, 0)),
            pl.BlockSpec((block_rows, width), lambda j: (j, 0)),
        ],
        out_specs=pl.BlockSpec((copies, 1, tok_count), lambda j: (0, 0, 0)),
        out_shape=jax.ShapeDtypeStruct((copies, 1, tok_count), jnp.float32),
        scratch_shapes=[
            pltpu.VMEM((2 * width, tok_count), jnp.bfloat16),
            pltpu.VMEM((1, tok_count), jnp.float32),
            pltpu.VMEM((subs, 1, tok_count), jnp.float32),
            pltpu.VMEM((subs, 8, tok_count), jnp.float32),
            pltpu.SMEM((flags,), jnp.float32),
        ],
        compiler_params=pltpu.CompilerParams(vmem_limit_bytes=vmem_bytes),
        cost_estimate=pl.CostEstimate(
            flops=2 * tok_count * cent_count * width,
            bytes_accessed=(tok_count + cent_count) * width * 2,
            transcendentals=tok_count * cent_count,
        ),
        name="row_stats",
    )(tokens, centroids)


def encoded(x):
    x = x * code_scale
    return (x * jnp.abs(x) * (x * x)).astype(jnp.bfloat16)


def decoded(code):
    code = code.astype(jnp.float32)
    size = lax.rsqrt(lax.rsqrt(jnp.maximum(jnp.abs(code), 1e-37))) * (1.0 / code_scale)
    return jnp.where(code < 0, -size, jnp.where(code > 0, size, 0.0))


class Placing:
    def __init__(self, block_rows, table_ref, chunk, pieces, code_refs, outs, scratch):
        self.block_rows, self.table_ref, self.chunk = block_rows, table_ref, chunk
        self.pieces, self.code_refs = pieces, code_refs
        self.updated_ref, self.masses_ref = outs
        self.codes, self.values, self.masses, self.sems = scratch

    @staticmethod
    def scratch(sources, blocks, block_rows, width):
        return [
            pltpu.VMEM((sources, blocks * coded_rows(block_rows), width), jnp.bfloat16),
            pltpu.VMEM((sources, blocks * block_rows, width), jnp.float32),
            pltpu.VMEM((sources, blocks * block_rows // 128, 128), jnp.float32),
            pltpu.SemaphoreType.DMA((4, sources)),
        ]

    def copies_in(self):
        found, refs = [], list(self.code_refs)
        for s, count in enumerate(self.pieces):
            found.append([])
            first = 0
            for k in range(count):
                ref = refs.pop(0)
                target = self.codes.at[s, pl.ds(first, ref.shape[0]), :]
                found[s].append(pltpu.make_async_copy(ref, target, self.sems.at[3 * k, s]))
                first += ref.shape[0]
        return found

    def copies_out(self, s):
        rows, mass_rows = self.values.shape[1], self.masses.shape[1]
        start = self.table_ref[self.chunk, s]
        span = pl.ds(pl.multiple_of(start * self.block_rows, self.block_rows), rows)
        per_block = self.block_rows // 128
        mass_span = pl.ds(pl.multiple_of(start * per_block, per_block), mass_rows)
        return [
            pltpu.make_async_copy(self.values.at[s], self.updated_ref.at[span, :], self.sems.at[1, s]),
            pltpu.make_async_copy(self.masses.at[s], self.masses_ref.at[mass_span, :], self.sems.at[2, s]),
        ]

    def fetch(self):
        for copies in self.copies_in():
            for copy in copies:
                copy.start()

    def place(self):
        block_rows, per_block = self.block_rows, self.block_rows // 128
        full = coded_rows(block_rows)
        tile = divisor(block_rows, 256)
        for s, copies in enumerate(self.copies_in()):
            for copy in copies:
                copy.wait()

            @pl.loop(0, self.values.shape[1] // block_rows)
            def _(b):
                for k in range(block_rows // tile):
                    source = pl.ds(pl.multiple_of(b * full + k * tile, 32), tile)
                    target = pl.ds(pl.multiple_of(b * block_rows + k * tile, tile), tile)
                    self.values[s, target, :] = decoded(self.codes[s, source, :])
                last = pl.ds(pl.multiple_of(b * full + block_rows, 32), full - block_rows)
                terms = self.codes[s, last, :].astype(jnp.float32)
                mass = terms[:per_block] + terms[per_block : 2 * per_block]
                mass = mass + terms[2 * per_block : 3 * per_block]
                self.masses[s, pl.ds(pl.multiple_of(b * per_block, per_block), per_block), :] = mass

            for copy in self.copies_out(s):
                copy.start()

    def finish(self):
        for s in range(len(self.pieces)):
            for copy in self.copies_out(s):
                copy.wait()


def coded_rows(block_rows):
    return block_rows + block_rows // 32


def combine(groups, parts_ref, out_ref):
    per_group = parts_ref.shape[0] // groups
    count = parts_ref.shape[2]
    for t in range(groups):
        parts = [parts_ref[t * per_group + k] for k in range(per_group)]
        top = functools.reduce(jnp.maximum, parts)
        total = functools.reduce(jnp.add, [jnp.exp(part - top) for part in parts])
        out_ref[:, t * count : (t + 1) * count] = top + jnp.log(total)


def update_kernel(joins, unread, placed_chunk, pieces, block_rows, *refs):
    table_ref, tok_ref, lse_ref, cent_ref = refs[:4]
    refs = refs[4 + unread :]
    code_refs, refs = refs[: sum(pieces)], refs[sum(pieces) :]
    if pieces:
        code_ref, updated_ref, masses_ref = refs[2:5]
        scratch = refs[5:]
        outs = updated_ref, masses_ref
        placing = Placing(block_rows, table_ref, placed_chunk, pieces, code_refs, outs, scratch[3:])
    else:
        code_ref, scratch, placing = refs[0], refs[1:], None
    if joins:
        parts_ref, lse_ref, scratch = lse_ref, scratch[0], scratch[1:]
        pl.when(pl.program_id(0) == 0)(lambda: combine(joins, parts_ref, lse_ref))
    weights_ref, total_ref, mass_ref = scratch[:3]
    step, steps = pl.program_id(0), pl.num_programs(0)
    width = tok_ref.shape[1]
    _, tile, depth = weights_ref.shape
    piece = divisor(depth, 512)
    stages = tok_ref.shape[0] // depth
    tiles = block_rows // tile

    if placing:
        pl.when(step == 0)(placing.fetch)

    def weigh(first, stage):
        cents = cent_ref[pl.ds(first, tile), :] * jnp.bfloat16(inverse_temp)
        for k in range(depth // piece):
            span = pl.ds(stage * depth + k * piece, piece)
            logits = dot_nt(cents, tok_ref[span, :])
            lse = lse_ref[:, span]
            for r in range(0, tile, slice_rows):
                weights = jnp.exp(logits[r : r + slice_rows] - lse).astype(jnp.bfloat16)
                weights_ref[stage % 2, r : r + slice_rows, pl.ds(k * piece, piece)] = weights

    def gather_up(stage):
        toks = tok_ref[pl.ds(stage * depth, depth), :]
        rhs = jnp.concatenate([toks, jnp.ones_like(toks)], axis=1)
        part = jnp.dot(weights_ref[stage % 2], rhs, preferred_element_type=jnp.float32)
        if stage == 0:
            total_ref[...] = part
        else:
            total_ref[...] += part

    diagonal = lax.broadcasted_iota(jnp.int32, (128, 128), 0) == lax.broadcasted_iota(
        jnp.int32, (128, 128), 1
    )

    def run(r):
        first = pl.multiple_of(r * tile, tile)
        weigh(first, 0)
        for stage in range(1, stages):
            weigh(first, stage)
            gather_up(stage - 1)
        gather_up(stages - 1)
        mass = total_ref[:, width : 2 * width]
        prior = prior_weight * cent_ref[pl.ds(first, tile), :].astype(jnp.float32)
        new = (total_ref[:, 0:width] + prior) / (mass + prior_weight)
        code_ref[pl.ds(first, tile), :] = encoded(new)
        for k in range(tile // 128):
            square = jnp.where(diagonal, mass[k * 128 : (k + 1) * 128, :], 0.0)
            mass_ref[pl.ds(r * (tile // 128) + k, 1), :] = jnp.sum(square, axis=0, keepdims=True)

    pl.loop(0, tiles // 2)(run)
    if placing:
        pl.when(step == 0)(placing.place)
    pl.loop(tiles // 2, tiles)(run)

    terms = split_exactly(mass_ref[...])
    terms = jnp.concatenate([*terms, jnp.zeros_like(terms[0])], axis=0)
    code_ref[block_rows : block_rows + terms.shape[0], :] = terms.astype(jnp.bfloat16)
    if placing:
        pl.when(step == steps - 1)(placing.finish)


def updated_chunk(
    table, chunk, toks, lse, centroids, blocks, block_rows, after=(), received=None, joins=0
):
    all_count, width = toks.shape
    depth = divisor(all_count, 2048)
    tile = divisor(block_rows, 1024)
    rows = blocks * block_rows
    full = coded_rows(block_rows)
    anywhere = pl.BlockSpec(memory_space=pl.ANY)
    whole = lambda j, place: (0, 0)
    operands = [
        toks,
        lse,
        pltpu.with_memory_space_constraint(centroids, pltpu.HBM),
        *after,
    ]
    in_specs = [
        pl.BlockSpec((all_count, width), whole),
        pl.BlockSpec(lse.shape, (lambda j, place: (0, 0, 0)) if joins else whole),
        pl.BlockSpec((block_rows, width), lambda j, table: (table[chunk, 0] + j, 0)),
    ] + [anywhere] * len(after)
    out_specs = [pl.BlockSpec((full, width), lambda j, place: (j, 0))]
    out_shape = [jax.ShapeDtypeStruct((blocks * full, width), jnp.bfloat16)]
    scratch_shapes = [
        pltpu.VMEM((2, tile, depth), jnp.bfloat16),
        pltpu.VMEM((tile, 2 * width), jnp.float32),
        pltpu.VMEM((block_rows // 128, 128), jnp.float32),
    ]
    aliases, pieces, placed_chunk = {}, [], None
    if joins:
        out_specs.append(pl.BlockSpec((1, all_count), whole))
        out_shape.append(jax.ShapeDtypeStruct((1, all_count), jnp.float32))
    if received:
        placed_chunk, codes, outs = received
        pieces = [len(parts) for parts in codes]
        operands += [*sum(codes, []), *outs]
        in_specs += [anywhere] * (sum(pieces) + 2)
        out_specs += [anywhere] * 2
        out_shape += [jax.ShapeDtypeStruct(out.shape, out.dtype) for out in outs]
        aliases = {len(operands) - 1: 1, len(operands): 2}
        scratch_shapes += Placing.scratch(len(codes), codes[0][0].shape[0] // full, block_rows, width)
    return pl.pallas_call(
        functools.partial(update_kernel, joins, len(after), placed_chunk, pieces, block_rows),
        grid_spec=pltpu.PrefetchScalarGridSpec(
            num_scalar_prefetch=1,
            grid=(blocks,),
            in_specs=in_specs,
            out_specs=out_specs,
            scratch_shapes=scratch_shapes,
        ),
        out_shape=out_shape,
        input_output_aliases=aliases,
        compiler_params=pltpu.CompilerParams(vmem_limit_bytes=vmem_bytes * 3 // 4),
        cost_estimate=pl.CostEstimate(
            flops=6 * all_count * rows * width // 8,
            bytes_accessed=(2 * all_count + 4 * rows) * width // 8,
            transcendentals=all_count * rows // 8,
        ),
        name="new_rows",
    )(table, *operands)


def place_kernel(chunks, block_rows, table_ref, *refs):
    count = sum(sum(pieces) for _, pieces in chunks)
    code_refs, outs, scratch = refs[:count], refs[count + 2 : count + 4], refs[count + 4 :]
    placings = []
    for chunk, pieces in chunks:
        used = code_refs[: sum(pieces)]
        placings.append(Placing(block_rows, table_ref, chunk, pieces, used, outs, scratch[:4]))
        code_refs, scratch = code_refs[sum(pieces) :], scratch[4:]
    for placing in placings:
        placing.fetch()
    for placing in placings:
        placing.place()
    for placing in placings:
        placing.finish()


def placed(table, received, outs, block_rows):
    operands, chunks, scratch_shapes = [], [], []
    for chunk, codes in received:
        chunks.append((chunk, [len(parts) for parts in codes]))
        operands += sum(codes, [])
        rows, width = codes[0][0].shape
        blocks = rows // coded_rows(block_rows)
        scratch_shapes += Placing.scratch(len(codes), blocks, block_rows, width)
    anywhere = pl.BlockSpec(memory_space=pl.ANY)
    return pl.pallas_call(
        functools.partial(place_kernel, chunks, block_rows),
        grid_spec=pltpu.PrefetchScalarGridSpec(
            num_scalar_prefetch=1,
            grid=(1,),
            in_specs=[anywhere] * (len(operands) + 2),
            out_specs=[anywhere] * 2,
            scratch_shapes=scratch_shapes,
        ),
        out_shape=[jax.ShapeDtypeStruct(out.shape, out.dtype) for out in outs],
        input_output_aliases={1 + len(operands): 0, 2 + len(operands): 1},
        compiler_params=pltpu.CompilerParams(vmem_limit_bytes=vmem_bytes // 2),
        name="placed_rows",
    )(table, *operands, *outs)


def blank(shape):
    return pl.pallas_call(
        lambda out_ref: None,
        out_specs=pl.BlockSpec(memory_space=pl.ANY),
        out_shape=jax.ShapeDtypeStruct(shape, jnp.float32),
        name="blank",
    )()


def from_others(value, axis):
    size = lax.axis_size(axis)
    found = [value]
    for s in range(1, size):
        pairs = [(partner(k, s, size), k) for k in range(size)]
        found.append(lax.ppermute(value, axis, pairs))
    return found


def partner(me, s, size):
    return me ^ s if size & (size - 1) == 0 else (me - s) % size


def chunk_plan(blocks):
    plan = []
    while blocks > 2:
        plan.append(2)
        blocks -= 2
    return plan + [1] * blocks


def local(tokens, centroids):
    tok_size, cent_size = lax.axis_size("tok"), lax.axis_size("cent")
    me = lax.axis_index("tok")
    cent_count, width = centroids.shape
    share_rows = cent_count // tok_size

    toks = lax.all_gather(tokens, "tok", axis=0, tiled=True)
    own_lse = local_lse(tokens, centroids, tok_size * cent_size)
    parts = lax.all_to_all(own_lse, ("tok", "cent"), 0, 0, tiled=True)

    block_rows = divisor(share_rows, 1024)
    plan = chunk_plan(share_rows // block_rows)
    sources = jnp.stack([partner(me, s, tok_size) for s in range(tok_size)])[None, :]
    starts = np.cumsum([0] + plan[:-1])[:, None] * tok_size
    table = (starts + sources * np.array(plan)[:, None]).astype(jnp.int32)
    outs = blank((cent_count, width)), blank((cent_count // 128, 128))
    waiting = []
    for k, blocks in enumerate(plan):
        arrived, received = [], None
        if len(waiting) > 1:
            arrived = sum(waiting[-2][1][1:], [])
            if blocks == 1:
                received = (*waiting.pop(0), outs)
                arrived = arrived[:1] if k + 1 == len(plan) else arrived
        operands = toks, lse if k else parts, centroids, blocks, block_rows, arrived, received
        codes, *rest = updated_chunk(table, k, *operands, joins=0 if k else tok_size)
        if not k:
            (lse,) = rest
        elif received:
            outs = rest
        waiting.append((k, [[part] for part in from_others(codes, "tok")]))
    if len(waiting) > 1:
        outs = placed(table, waiting[:-1], outs, block_rows)
    outs = placed(table, waiting[-1:], outs, block_rows)
    return outs[0], outs[1].reshape(cent_count)


def solution(mesh):
    placed_as = (P("tok", None), P("cent", None))
    return jax.shard_map(
        local, mesh=mesh, in_specs=placed_as, out_specs=(P("cent", None), P("cent")), check_vma=False
    )
```

```python
import functools

import jax
import jax.numpy as jnp
import numpy as np
from jax import lax
from jax.experimental import pallas as pl
from jax.experimental.pallas import tpu as pltpu
from jax.sharding import PartitionSpec as P

inverse_temp = 2.0
prior_weight = 0.05
safe_sum = 1e30
headroom = 60.0
code_scale = 2.0**24
slice_rows = 64
vmem_bytes = 56 * 1024 * 1024


def divisor(count, most):
    size = min(count, most)
    while count % size:
        size //= 2
    return size


def dot_nt(a, b):
    return lax.dot_general(a, b, (((1,), (1,)), ((), ())), preferred_element_type=jnp.float32)


def fold_rows(x, combine):
    parts = [x[k * 8 : (k + 1) * 8, :] for k in range(x.shape[0] // 8)]
    while len(parts) > 1:
        half = len(parts) // 2
        parts = [combine(parts[2 * k], parts[2 * k + 1]) for k in range(half)] + parts[2 * half :]
    return parts[0]


def split_exactly(x):
    high = x.astype(jnp.bfloat16).astype(jnp.float32)
    middle = (x - high).astype(jnp.bfloat16).astype(jnp.float32)
    return high, middle, x - high - middle


def stats_kernel(
    sub_rows, tok_cols, tok_ref, cent_ref, out_ref, flip_ref, base_ref, shift_ref, sums_ref, worst_ref
):
    step = pl.program_id(0)
    tok_count = tok_ref.shape[0]
    subs = cent_ref.shape[0] // sub_rows
    col_blocks = tok_count // tok_cols
    redo_cols = divisor(tok_cols, 256)
    redo_blocks = tok_count // redo_cols

    def columns(t, size=tok_cols):
        return pl.ds(pl.multiple_of(t * size, size), size)

    def dot(a, b):
        return jnp.dot(a, b, preferred_element_type=jnp.float32)

    width = tok_ref.shape[1]

    @pl.when(step == 0)
    def _():
        @pl.loop(0, col_blocks)
        def _(t):
            flipped = (tok_ref[columns(t), :] * jnp.bfloat16(inverse_temp)).T
            flip_ref[0:width, columns(t)] = flipped
            logits = dot(cent_ref[0:128, :], flipped)
            top = jnp.max(fold_rows(logits, jnp.maximum), axis=0, keepdims=True)
            base = top + headroom
            base_ref[:, columns(t)] = base
            row = lax.broadcasted_iota(jnp.int32, (width, tok_cols), 0)
            terms = jnp.zeros((width, tok_cols), jnp.float32)
            for k, term in enumerate(split_exactly(-base)):
                terms = jnp.where(row == k, term, terms)
            flip_ref[width:, columns(t)] = terms.astype(jnp.bfloat16)

    lane = lax.broadcasted_iota(jnp.int32, (sub_rows, width), 1)
    ones = jnp.where(lane < 3, 1.0, 0.0).astype(jnp.bfloat16)

    @pl.loop(0, col_blocks)
    def _(t):
        rhs = flip_ref[:, columns(t)]
        shift = base_ref[:, columns(t)]
        for sub in range(subs):
            total = jnp.zeros((8, tok_cols), jnp.float32)
            lhs = jnp.concatenate([cent_ref[pl.ds(sub * sub_rows, sub_rows), :], ones], axis=1)
            logits = dot(lhs, rhs)
            for first in range(0, sub_rows, slice_rows):
                scaled = jnp.exp(logits[first : first + slice_rows])
                total = total + fold_rows(scaled, jnp.add)
            sums_ref[step * subs + sub, :, columns(t)] = total
            shift_ref[step * subs + sub, :, columns(t)] = shift

    worst = jnp.float32(0.0)
    for sub in range(subs):
        for t in range(redo_blocks):
            block = jnp.max(sums_ref[step * subs + sub, :, t * redo_cols : (t + 1) * redo_cols])
            worst_ref[sub * redo_blocks + t] = block
            worst = jnp.maximum(worst, block)

    @pl.when(jnp.logical_not(worst < safe_sum))
    def _():
        @pl.loop(0, subs * redo_blocks)
        def _(k):
            @pl.when(jnp.logical_not(worst_ref[k] < safe_sum))
            def _():
                sub, t = k // redo_blocks, lax.rem(k, redo_blocks)
                first = pl.multiple_of(sub * sub_rows, sub_rows)
                rhs = flip_ref[0:width, columns(t, redo_cols)]
                logits = dot(cent_ref[pl.ds(first, sub_rows), :], rhs)
                top = jnp.max(fold_rows(logits, jnp.maximum), axis=0, keepdims=True)
                total = fold_rows(jnp.exp(logits - top), jnp.add)
                sums_ref[step * subs + sub, :, columns(t, redo_cols)] = total
                shift_ref[step * subs + sub, :, columns(t, redo_cols)] = top

    @pl.when(step == pl.num_programs(0) - 1)
    def _():
        @pl.loop(0, col_blocks)
        def _(t):
            shifts = shift_ref[:, :, columns(t)]
            top = jnp.max(shifts, axis=0)
            scale = jnp.exp(shifts - top[None])
            total = jnp.sum(sums_ref[:, :, columns(t)] * scale, axis=0)
            total = jnp.sum(total, axis=0, keepdims=True)
            out_ref[:, :, columns(t)] = jnp.broadcast_to(
                (top + jnp.log(total))[None], (out_ref.shape[0], 1, tok_cols)
            )


def local_lse(tokens, centroids, copies):
    tok_count, width = tokens.shape
    cent_count = centroids.shape[0]
    block_rows = divisor(cent_count, 4096)
    sub_rows = divisor(block_rows, 1024)
    tok_cols = divisor(tok_count, 512)
    blocks = cent_count // block_rows
    subs = cent_count // sub_rows
    flags = block_rows // sub_rows * (tok_count // divisor(tok_cols, 256))
    return pl.pallas_call(
        functools.partial(stats_kernel, sub_rows, tok_cols),
        grid=(blocks,),
        in_specs=[
            pl.BlockSpec((tok_count, width), lambda j: (0, 0)),
            pl.BlockSpec((block_rows, width), lambda j: (j, 0)),
        ],
        out_specs=pl.BlockSpec((copies, 1, tok_count), lambda j: (0, 0, 0)),
        out_shape=jax.ShapeDtypeStruct((copies, 1, tok_count), jnp.float32),
        scratch_shapes=[
            pltpu.VMEM((2 * width, tok_count), jnp.bfloat16),
            pltpu.VMEM((1, tok_count), jnp.float32),
            pltpu.VMEM((subs, 1, tok_count), jnp.float32),
            pltpu.VMEM((subs, 8, tok_count), jnp.float32),
            pltpu.SMEM((flags,), jnp.float32),
        ],
        compiler_params=pltpu.CompilerParams(vmem_limit_bytes=vmem_bytes * 4 // 7),
        cost_estimate=pl.CostEstimate(
            flops=2 * tok_count * cent_count * width,
            bytes_accessed=(tok_count + cent_count) * width * 2,
            transcendentals=tok_count * cent_count,
        ),
        name="row_stats",
    )(*(pltpu.with_memory_space_constraint(x, pltpu.HBM) for x in (tokens, centroids)))


def encoded(x):
    x = x * code_scale
    return (x * jnp.abs(x) * (x * x)).astype(jnp.bfloat16)


def decoded(code):
    code = code.astype(jnp.float32)
    size = lax.rsqrt(lax.rsqrt(jnp.maximum(jnp.abs(code), 1e-37))) * (1.0 / code_scale)
    return jnp.where(code < 0, -size, jnp.where(code > 0, size, 0.0))


class Placing:
    def __init__(self, block_rows, table_ref, chunk, pieces, code_refs, outs, scratch):
        self.block_rows, self.table_ref, self.chunk = block_rows, table_ref, chunk
        self.pieces, self.code_refs = pieces, code_refs
        self.updated_ref, self.masses_ref = outs
        self.codes, self.values, self.masses, self.sems = scratch

    @staticmethod
    def scratch(sources, blocks, block_rows, width):
        return [
            pltpu.VMEM((sources, blocks * coded_rows(block_rows), width), jnp.bfloat16),
            pltpu.VMEM((sources, blocks * block_rows, width), jnp.float32),
            pltpu.VMEM((sources, blocks * block_rows // 128, 128), jnp.float32),
            pltpu.SemaphoreType.DMA((4, sources)),
        ]

    def copies_in(self):
        found, refs = [], list(self.code_refs)
        for s, count in enumerate(self.pieces):
            found.append([])
            first = 0
            for k in range(count):
                ref = refs.pop(0)
                target = self.codes.at[s, pl.ds(first, ref.shape[0]), :]
                found[s].append(pltpu.make_async_copy(ref, target, self.sems.at[3 * k, s]))
                first += ref.shape[0]
        return found

    def copies_out(self, s):
        rows, mass_rows = self.values.shape[1], self.masses.shape[1]
        start = self.table_ref[self.chunk, s]
        span = pl.ds(pl.multiple_of(start * self.block_rows, self.block_rows), rows)
        per_block = self.block_rows // 128
        mass_span = pl.ds(pl.multiple_of(start * per_block, per_block), mass_rows)
        return [
            pltpu.make_async_copy(self.values.at[s], self.updated_ref.at[span, :], self.sems.at[1, s]),
            pltpu.make_async_copy(self.masses.at[s], self.masses_ref.at[mass_span, :], self.sems.at[2, s]),
        ]

    def fetch(self):
        for copies in self.copies_in():
            for copy in copies:
                copy.start()

    def place(self):
        block_rows, per_block = self.block_rows, self.block_rows // 128
        full = coded_rows(block_rows)
        tile = divisor(block_rows, 256)
        for s, copies in enumerate(self.copies_in()):
            for copy in copies:
                copy.wait()

            @pl.loop(0, self.values.shape[1] // block_rows)
            def _(b):
                for k in range(block_rows // tile):
                    source = pl.ds(pl.multiple_of(b * full + k * tile, 32), tile)
                    target = pl.ds(pl.multiple_of(b * block_rows + k * tile, tile), tile)
                    self.values[s, target, :] = decoded(self.codes[s, source, :])
                last = pl.ds(pl.multiple_of(b * full + block_rows, 32), full - block_rows)
                terms = self.codes[s, last, :].astype(jnp.float32)
                mass = terms[:per_block] + terms[per_block : 2 * per_block]
                mass = mass + terms[2 * per_block : 3 * per_block]
                self.masses[s, pl.ds(pl.multiple_of(b * per_block, per_block), per_block), :] = mass

            for copy in self.copies_out(s):
                copy.start()

    def finish(self):
        for s in range(len(self.pieces)):
            for copy in self.copies_out(s):
                copy.wait()


def coded_rows(block_rows):
    return block_rows + block_rows // 32


def combine(groups, parts_ref, out_ref):
    per_group = parts_ref.shape[0] // groups
    count = parts_ref.shape[2]
    for t in range(groups):
        parts = [parts_ref[t * per_group + k] for k in range(per_group)]
        top = functools.reduce(jnp.maximum, parts)
        total = functools.reduce(jnp.add, [jnp.exp(part - top) for part in parts])
        out_ref[:, t * count : (t + 1) * count] = top + jnp.log(total)


def update_kernel(joins, unread, placed_chunk, pieces, block_rows, *refs):
    table_ref, tok_ref, lse_ref, cent_ref = refs[:4]
    refs = refs[4 + unread :]
    code_refs, refs = refs[: sum(pieces)], refs[sum(pieces) :]
    if pieces:
        code_ref, updated_ref, masses_ref = refs[2:5]
        scratch = refs[5:]
        outs = updated_ref, masses_ref
        placing = Placing(block_rows, table_ref, placed_chunk, pieces, code_refs, outs, scratch[3:])
    else:
        code_ref, scratch, placing = refs[0], refs[1:], None
    if joins:
        parts_ref, lse_ref, scratch = lse_ref, scratch[0], scratch[1:]
        pl.when(pl.program_id(0) == 0)(lambda: combine(joins, parts_ref, lse_ref))
    weights_ref, total_ref, mass_ref = scratch[:3]
    step, steps = pl.program_id(0), pl.num_programs(0)
    width = tok_ref.shape[1]
    _, tile, depth = weights_ref.shape
    piece = divisor(depth, 512)
    stages = tok_ref.shape[0] // depth
    tiles = block_rows // tile

    if placing:
        pl.when(step == 0)(placing.fetch)

    def weigh(first, stage):
        cents = cent_ref[pl.ds(first, tile), :] * jnp.bfloat16(inverse_temp)
        for k in range(depth // piece):
            span = pl.ds(stage * depth + k * piece, piece)
            logits = dot_nt(cents, tok_ref[span, :])
            lse = lse_ref[:, span]
            for r in range(0, tile, slice_rows):
                weights = jnp.exp(logits[r : r + slice_rows] - lse).astype(jnp.bfloat16)
                weights_ref[stage % 2, r : r + slice_rows, pl.ds(k * piece, piece)] = weights

    def gather_up(stage):
        toks = tok_ref[pl.ds(stage * depth, depth), :]
        rhs = jnp.concatenate([toks, jnp.ones_like(toks)], axis=1)
        part = jnp.dot(weights_ref[stage % 2], rhs, preferred_element_type=jnp.float32)
        if stage == 0:
            total_ref[...] = part
        else:
            total_ref[...] += part

    diagonal = lax.broadcasted_iota(jnp.int32, (128, 128), 0) == lax.broadcasted_iota(
        jnp.int32, (128, 128), 1
    )

    def run(r):
        first = pl.multiple_of(r * tile, tile)
        weigh(first, 0)
        for stage in range(1, stages):
            weigh(first, stage)
            gather_up(stage - 1)
        gather_up(stages - 1)
        mass = total_ref[:, width : 2 * width]
        prior = prior_weight * cent_ref[pl.ds(first, tile), :].astype(jnp.float32)
        new = (total_ref[:, 0:width] + prior) / (mass + prior_weight)
        code_ref[pl.ds(first, tile), :] = encoded(new)
        for k in range(tile // 128):
            square = jnp.where(diagonal, mass[k * 128 : (k + 1) * 128, :], 0.0)
            mass_ref[pl.ds(r * (tile // 128) + k, 1), :] = jnp.sum(square, axis=0, keepdims=True)

    pl.loop(0, tiles // 2)(run)
    if placing:
        pl.when(step == 0)(placing.place)
    pl.loop(tiles // 2, tiles)(run)

    terms = split_exactly(mass_ref[...])
    terms = jnp.concatenate([*terms, jnp.zeros_like(terms[0])], axis=0)
    code_ref[block_rows : block_rows + terms.shape[0], :] = terms.astype(jnp.bfloat16)
    if placing:
        pl.when(step == steps - 1)(placing.finish)


def flat(codes):
    own, *others = codes
    return own + [pltpu.with_memory_space_constraint(part, pltpu.VMEM) for part in sum(others, [])]


def updated_chunk(
    table, chunk, toks, lse, centroids, blocks, block_rows, after=(), received=None, joins=0
):
    all_count, width = toks.shape
    depth = divisor(all_count, 2048)
    tile = divisor(block_rows, 1024)
    rows = blocks * block_rows
    full = coded_rows(block_rows)
    anywhere = pl.BlockSpec(memory_space=pl.ANY)
    whole = lambda j, place: (0, 0)
    operands = [
        toks,
        lse,
        centroids,
        *(pltpu.with_memory_space_constraint(part, pltpu.VMEM) for part in after),
    ]
    in_specs = [
        pl.BlockSpec((all_count, width), whole),
        pl.BlockSpec(lse.shape, (lambda j, place: (0, 0, 0)) if joins else whole),
        pl.BlockSpec((block_rows, width), lambda j, table: (table[chunk, 0] + j, 0)),
    ] + [anywhere] * len(after)
    out_specs = [pl.BlockSpec((full, width), lambda j, place: (j, 0))]
    out_shape = [jax.ShapeDtypeStruct((blocks * full, width), jnp.bfloat16)]
    scratch_shapes = [
        pltpu.VMEM((2, tile, depth), jnp.bfloat16),
        pltpu.VMEM((tile, 2 * width), jnp.float32),
        pltpu.VMEM((block_rows // 128, 128), jnp.float32),
    ]
    aliases, pieces, placed_chunk = {}, [], None
    if joins:
        out_specs.append(pl.BlockSpec((1, all_count), whole))
        out_shape.append(jax.ShapeDtypeStruct((1, all_count), jnp.float32))
    if received:
        placed_chunk, codes, outs = received
        pieces = [len(parts) for parts in codes]
        operands += [*flat(codes), *outs]
        in_specs += [anywhere] * (sum(pieces) + 2)
        out_specs += [anywhere] * 2
        out_shape += [jax.ShapeDtypeStruct(out.shape, out.dtype) for out in outs]
        aliases = {len(operands) - 1: 1, len(operands): 2}
        scratch_shapes += Placing.scratch(len(codes), codes[0][0].shape[0] // full, block_rows, width)
    return pl.pallas_call(
        functools.partial(update_kernel, joins, len(after), placed_chunk, pieces, block_rows),
        grid_spec=pltpu.PrefetchScalarGridSpec(
            num_scalar_prefetch=1,
            grid=(blocks,),
            in_specs=in_specs,
            out_specs=out_specs,
            scratch_shapes=scratch_shapes,
        ),
        out_shape=out_shape,
        input_output_aliases=aliases,
        compiler_params=pltpu.CompilerParams(vmem_limit_bytes=vmem_bytes * 3 // 4),
        cost_estimate=pl.CostEstimate(
            flops=6 * all_count * rows * width // 8,
            bytes_accessed=(2 * all_count + 4 * rows) * width // 8,
            transcendentals=all_count * rows // 8,
        ),
        name="new_rows",
    )(table, *operands)


def place_kernel(chunks, block_rows, table_ref, *refs):
    count = sum(sum(pieces) for _, pieces in chunks)
    code_refs, outs, scratch = refs[:count], refs[count + 2 : count + 4], refs[count + 4 :]
    placings = []
    for chunk, pieces in chunks:
        used = code_refs[: sum(pieces)]
        placings.append(Placing(block_rows, table_ref, chunk, pieces, used, outs, scratch[:4]))
        code_refs, scratch = code_refs[sum(pieces) :], scratch[4:]
    for placing in placings:
        placing.fetch()
    for placing in placings:
        placing.place()
    for placing in placings:
        placing.finish()


def placed(table, received, outs, block_rows):
    operands, chunks, scratch_shapes = [], [], []
    for chunk, codes in received:
        chunks.append((chunk, [len(parts) for parts in codes]))
        operands += flat(codes)
        rows, width = codes[0][0].shape
        blocks = rows // coded_rows(block_rows)
        scratch_shapes += Placing.scratch(len(codes), blocks, block_rows, width)
    anywhere = pl.BlockSpec(memory_space=pl.ANY)
    return pl.pallas_call(
        functools.partial(place_kernel, chunks, block_rows),
        grid_spec=pltpu.PrefetchScalarGridSpec(
            num_scalar_prefetch=1,
            grid=(1,),
            in_specs=[anywhere] * (len(operands) + 2),
            out_specs=[anywhere] * 2,
            scratch_shapes=scratch_shapes,
        ),
        out_shape=[jax.ShapeDtypeStruct(out.shape, out.dtype) for out in outs],
        input_output_aliases={1 + len(operands): 0, 2 + len(operands): 1},
        compiler_params=pltpu.CompilerParams(vmem_limit_bytes=vmem_bytes // 2),
        name="placed_rows",
    )(table, *operands, *outs)


def blank(shape):
    return pl.pallas_call(
        lambda out_ref: None,
        out_specs=pl.BlockSpec(memory_space=pl.ANY),
        out_shape=jax.ShapeDtypeStruct(shape, jnp.float32),
        name="blank",
    )()


def from_others(value, axis):
    size = lax.axis_size(axis)
    found = [value]
    for s in range(1, size):
        pairs = [(partner(k, s, size), k) for k in range(size)]
        found.append(lax.ppermute(value, axis, pairs))
    return found


def partner(me, s, size):
    return me ^ s if size & (size - 1) == 0 else (me - s) % size


def chunk_plan(blocks):
    plan = []
    while blocks > 2:
        plan.append(2)
        blocks -= 2
    return plan + [1] * blocks


def local(tokens, centroids):
    tok_size, cent_size = lax.axis_size("tok"), lax.axis_size("cent")
    me = lax.axis_index("tok")
    cent_count, width = centroids.shape
    share_rows = cent_count // tok_size

    toks = lax.all_gather(tokens, "tok", axis=0, tiled=True)
    own_lse = local_lse(tokens, centroids, tok_size * cent_size)
    parts = lax.all_to_all(own_lse, ("tok", "cent"), 0, 0, tiled=True)

    block_rows = divisor(share_rows, 1024)
    plan = chunk_plan(share_rows // block_rows)
    sources = jnp.stack([partner(me, s, tok_size) for s in range(tok_size)])[None, :]
    starts = np.cumsum([0] + plan[:-1])[:, None] * tok_size
    table = (starts + sources * np.array(plan)[:, None]).astype(jnp.int32)
    outs = blank((cent_count, width)), blank((cent_count // 128, 128))
    waiting = []
    for k, blocks in enumerate(plan):
        arrived, received = [], None
        if len(waiting) > 1:
            arrived = sum(waiting[-2][1][1:], [])
            if blocks == 1:
                received = (*waiting.pop(0), outs)
                arrived = arrived[:1] if k + 1 == len(plan) else arrived
        operands = toks, lse if k else parts, centroids, blocks, block_rows, arrived, received
        codes, *rest = updated_chunk(table, k, *operands, joins=0 if k else tok_size)
        if not k:
            (lse,) = rest
        elif received:
            outs = rest
        waiting.append((k, [[part] for part in from_others(codes, "tok")]))
    if len(waiting) > 1:
        outs = placed(table, waiting[:-1], outs, block_rows)
    outs = placed(table, waiting[-1:], outs, block_rows)
    return outs[0], outs[1].reshape(cent_count)


def solution(mesh):
    placed_as = (P("tok", None), P("cent", None))
    return jax.shard_map(
        local, mesh=mesh, in_specs=placed_as, out_specs=(P("cent", None), P("cent")), check_vma=False
    )
```

```python
import functools

import jax
import jax.numpy as jnp
import numpy as np
from jax import lax
from jax.experimental import pallas as pl
from jax.experimental.pallas import tpu as pltpu
from jax.sharding import PartitionSpec as P

inverse_temp = 2.0
prior_weight = 0.05
safe_sum = 1e30
headroom = 60.0
code_scale = 2.0**24
slice_rows = 64
vmem_bytes = 56 * 1024 * 1024


def divisor(count, most):
    size = min(count, most)
    while count % size:
        size //= 2
    return size


def dot_nt(a, b):
    return lax.dot_general(a, b, (((1,), (1,)), ((), ())), preferred_element_type=jnp.float32)


def fold_rows(x, combine):
    parts = [x[k * 8 : (k + 1) * 8, :] for k in range(x.shape[0] // 8)]
    while len(parts) > 1:
        half = len(parts) // 2
        parts = [combine(parts[2 * k], parts[2 * k + 1]) for k in range(half)] + parts[2 * half :]
    return parts[0]


def split_exactly(x):
    high = x.astype(jnp.bfloat16).astype(jnp.float32)
    middle = (x - high).astype(jnp.bfloat16).astype(jnp.float32)
    return high, middle, x - high - middle


def stats_kernel(
    sub_rows, tok_cols, tok_ref, cent_ref, out_ref, flip_ref, base_ref, shift_ref, sums_ref, worst_ref
):
    step = pl.program_id(0)
    tok_count = tok_ref.shape[0]
    subs = cent_ref.shape[0] // sub_rows
    col_blocks = tok_count // tok_cols
    redo_cols = divisor(tok_cols, 256)
    redo_blocks = tok_count // redo_cols

    def columns(t, size=tok_cols):
        return pl.ds(pl.multiple_of(t * size, size), size)

    def dot(a, b):
        return jnp.dot(a, b, preferred_element_type=jnp.float32)

    width = tok_ref.shape[1]

    @pl.when(step == 0)
    def _():
        @pl.loop(0, col_blocks)
        def _(t):
            flipped = (tok_ref[columns(t), :] * jnp.bfloat16(inverse_temp)).T
            flip_ref[0:width, columns(t)] = flipped
            logits = dot(cent_ref[0:128, :], flipped)
            top = jnp.max(fold_rows(logits, jnp.maximum), axis=0, keepdims=True)
            base = top + headroom
            base_ref[:, columns(t)] = base
            row = lax.broadcasted_iota(jnp.int32, (width, tok_cols), 0)
            terms = jnp.zeros((width, tok_cols), jnp.float32)
            for k, term in enumerate(split_exactly(-base)):
                terms = jnp.where(row == k, term, terms)
            flip_ref[width:, columns(t)] = terms.astype(jnp.bfloat16)

    lane = lax.broadcasted_iota(jnp.int32, (sub_rows, width), 1)
    ones = jnp.where(lane < 3, 1.0, 0.0).astype(jnp.bfloat16)

    @pl.loop(0, col_blocks)
    def _(t):
        rhs = flip_ref[:, columns(t)]
        shift = base_ref[:, columns(t)]
        for sub in range(subs):
            total = jnp.zeros((8, tok_cols), jnp.float32)
            lhs = jnp.concatenate([cent_ref[pl.ds(sub * sub_rows, sub_rows), :], ones], axis=1)
            logits = dot(lhs, rhs)
            for first in range(0, sub_rows, slice_rows):
                scaled = jnp.exp(logits[first : first + slice_rows])
                total = total + fold_rows(scaled, jnp.add)
            sums_ref[step * subs + sub, :, columns(t)] = total
            shift_ref[step * subs + sub, :, columns(t)] = shift

    worst = jnp.float32(0.0)
    for sub in range(subs):
        for t in range(redo_blocks):
            block = jnp.max(sums_ref[step * subs + sub, :, t * redo_cols : (t + 1) * redo_cols])
            worst_ref[sub * redo_blocks + t] = block
            worst = jnp.maximum(worst, block)

    @pl.when(jnp.logical_not(worst < safe_sum))
    def _():
        @pl.loop(0, subs * redo_blocks)
        def _(k):
            @pl.when(jnp.logical_not(worst_ref[k] < safe_sum))
            def _():
                sub, t = k // redo_blocks, lax.rem(k, redo_blocks)
                first = pl.multiple_of(sub * sub_rows, sub_rows)
                rhs = flip_ref[0:width, columns(t, redo_cols)]
                logits = dot(cent_ref[pl.ds(first, sub_rows), :], rhs)
                top = jnp.max(fold_rows(logits, jnp.maximum), axis=0, keepdims=True)
                total = fold_rows(jnp.exp(logits - top), jnp.add)
                sums_ref[step * subs + sub, :, columns(t, redo_cols)] = total
                shift_ref[step * subs + sub, :, columns(t, redo_cols)] = top

    @pl.when(step == pl.num_programs(0) - 1)
    def _():
        @pl.loop(0, col_blocks)
        def _(t):
            shifts = shift_ref[:, :, columns(t)]
            top = jnp.max(shifts, axis=0)
            scale = jnp.exp(shifts - top[None])
            total = jnp.sum(sums_ref[:, :, columns(t)] * scale, axis=0)
            total = jnp.sum(total, axis=0, keepdims=True)
            out_ref[:, :, columns(t)] = jnp.broadcast_to(
                (top + jnp.log(total))[None], (out_ref.shape[0], 1, tok_cols)
            )


def local_lse(tokens, centroids, copies):
    tok_count, width = tokens.shape
    cent_count = centroids.shape[0]
    block_rows = divisor(cent_count, 4096)
    sub_rows = divisor(block_rows, 1024)
    tok_cols = divisor(tok_count, 512)
    blocks = cent_count // block_rows
    subs = cent_count // sub_rows
    flags = block_rows // sub_rows * (tok_count // divisor(tok_cols, 256))
    return pl.pallas_call(
        functools.partial(stats_kernel, sub_rows, tok_cols),
        grid=(blocks,),
        in_specs=[
            pl.BlockSpec((tok_count, width), lambda j: (0, 0)),
            pl.BlockSpec((block_rows, width), lambda j: (j, 0)),
        ],
        out_specs=pl.BlockSpec((copies, 1, tok_count), lambda j: (0, 0, 0)),
        out_shape=jax.ShapeDtypeStruct((copies, 1, tok_count), jnp.float32),
        scratch_shapes=[
            pltpu.VMEM((2 * width, tok_count), jnp.bfloat16),
            pltpu.VMEM((1, tok_count), jnp.float32),
            pltpu.VMEM((subs, 1, tok_count), jnp.float32),
            pltpu.VMEM((subs, 8, tok_count), jnp.float32),
            pltpu.SMEM((flags,), jnp.float32),
        ],
        compiler_params=pltpu.CompilerParams(vmem_limit_bytes=vmem_bytes),
        cost_estimate=pl.CostEstimate(
            flops=2 * tok_count * cent_count * width,
            bytes_accessed=(tok_count + cent_count) * width * 2,
            transcendentals=tok_count * cent_count,
        ),
        name="row_stats",
    )(tokens, centroids)


def encoded(x):
    x = x * code_scale
    return (x * jnp.abs(x) * (x * x)).astype(jnp.bfloat16)


def decoded(code):
    code = code.astype(jnp.float32)
    size = lax.rsqrt(lax.rsqrt(jnp.maximum(jnp.abs(code), 1e-37))) * (1.0 / code_scale)
    return jnp.where(code < 0, -size, jnp.where(code > 0, size, 0.0))


class Placing:
    def __init__(self, block_rows, table_ref, chunk, pieces, code_refs, outs, scratch):
        self.block_rows, self.table_ref, self.chunk = block_rows, table_ref, chunk
        self.pieces, self.code_refs = pieces, code_refs
        self.updated_ref, self.masses_ref = outs
        self.codes, self.values, self.masses, self.sems = scratch

    @staticmethod
    def scratch(sources, blocks, block_rows, width):
        return [
            pltpu.VMEM((sources, blocks * coded_rows(block_rows), width), jnp.bfloat16),
            pltpu.VMEM((sources, blocks * block_rows, width), jnp.float32),
            pltpu.VMEM((sources, blocks * block_rows // 128, 128), jnp.float32),
            pltpu.SemaphoreType.DMA((4, sources)),
        ]

    def copies_in(self):
        found, refs = [], list(self.code_refs)
        for s, count in enumerate(self.pieces):
            found.append([])
            first = 0
            for k in range(count):
                ref = refs.pop(0)
                target = self.codes.at[s, pl.ds(first, ref.shape[0]), :]
                found[s].append(pltpu.make_async_copy(ref, target, self.sems.at[3 * k, s]))
                first += ref.shape[0]
        return found

    def copies_out(self, s):
        rows, mass_rows = self.values.shape[1], self.masses.shape[1]
        start = self.table_ref[self.chunk, s]
        span = pl.ds(pl.multiple_of(start * self.block_rows, self.block_rows), rows)
        per_block = self.block_rows // 128
        mass_span = pl.ds(pl.multiple_of(start * per_block, per_block), mass_rows)
        return [
            pltpu.make_async_copy(self.values.at[s], self.updated_ref.at[span, :], self.sems.at[1, s]),
            pltpu.make_async_copy(self.masses.at[s], self.masses_ref.at[mass_span, :], self.sems.at[2, s]),
        ]

    def fetch(self):
        for copies in self.copies_in():
            for copy in copies:
                copy.start()

    def place(self):
        block_rows, per_block = self.block_rows, self.block_rows // 128
        full = coded_rows(block_rows)
        tile = divisor(block_rows, 256)
        for s, copies in enumerate(self.copies_in()):
            for copy in copies:
                copy.wait()

            @pl.loop(0, self.values.shape[1] // block_rows)
            def _(b):
                for k in range(block_rows // tile):
                    source = pl.ds(pl.multiple_of(b * full + k * tile, 32), tile)
                    target = pl.ds(pl.multiple_of(b * block_rows + k * tile, tile), tile)
                    self.values[s, target, :] = decoded(self.codes[s, source, :])
                last = pl.ds(pl.multiple_of(b * full + block_rows, 32), full - block_rows)
                terms = self.codes[s, last, :].astype(jnp.float32)
                mass = terms[:per_block] + terms[per_block : 2 * per_block]
                mass = mass + terms[2 * per_block : 3 * per_block]
                self.masses[s, pl.ds(pl.multiple_of(b * per_block, per_block), per_block), :] = mass

            for copy in self.copies_out(s):
                copy.start()

    def finish(self):
        for s in range(len(self.pieces)):
            for copy in self.copies_out(s):
                copy.wait()


def coded_rows(block_rows):
    return block_rows + block_rows // 32


def combine(groups, parts_ref, out_ref):
    per_group = parts_ref.shape[0] // groups
    count = parts_ref.shape[2]
    for t in range(groups):
        parts = [parts_ref[t * per_group + k] for k in range(per_group)]
        top = functools.reduce(jnp.maximum, parts)
        total = functools.reduce(jnp.add, [jnp.exp(part - top) for part in parts])
        out_ref[:, t * count : (t + 1) * count] = top + jnp.log(total)


def update_kernel(joins, unread, placed_chunk, pieces, block_rows, *refs):
    table_ref, tok_ref, lse_ref, cent_ref = refs[:4]
    refs = refs[4 + unread :]
    code_refs, refs = refs[: sum(pieces)], refs[sum(pieces) :]
    if pieces:
        code_ref, updated_ref, masses_ref = refs[2:5]
        scratch = refs[5:]
        outs = updated_ref, masses_ref
        placing = Placing(block_rows, table_ref, placed_chunk, pieces, code_refs, outs, scratch[3:])
    else:
        code_ref, scratch, placing = refs[0], refs[1:], None
    if joins:
        parts_ref, lse_ref, scratch = lse_ref, scratch[0], scratch[1:]
        pl.when(pl.program_id(0) == 0)(lambda: combine(joins, parts_ref, lse_ref))
    weights_ref, total_ref, mass_ref = scratch[:3]
    step, steps = pl.program_id(0), pl.num_programs(0)
    width = tok_ref.shape[1]
    _, tile, depth = weights_ref.shape
    piece = divisor(depth, 512)
    stages = tok_ref.shape[0] // depth
    tiles = block_rows // tile

    if placing:
        pl.when(step == 0)(placing.fetch)

    def weigh(first, stage):
        cents = cent_ref[pl.ds(first, tile), :] * jnp.bfloat16(inverse_temp)
        for k in range(depth // piece):
            span = pl.ds(stage * depth + k * piece, piece)
            logits = dot_nt(cents, tok_ref[span, :])
            lse = lse_ref[:, span]
            for r in range(0, tile, slice_rows):
                weights = jnp.exp(logits[r : r + slice_rows] - lse).astype(jnp.bfloat16)
                weights_ref[stage % 2, r : r + slice_rows, pl.ds(k * piece, piece)] = weights

    def gather_up(stage):
        toks = tok_ref[pl.ds(stage * depth, depth), :]
        rhs = jnp.concatenate([toks, jnp.ones_like(toks)], axis=1)
        part = jnp.dot(weights_ref[stage % 2], rhs, preferred_element_type=jnp.float32)
        if stage == 0:
            total_ref[...] = part
        else:
            total_ref[...] += part

    diagonal = lax.broadcasted_iota(jnp.int32, (128, 128), 0) == lax.broadcasted_iota(
        jnp.int32, (128, 128), 1
    )

    def run(r):
        first = pl.multiple_of(r * tile, tile)
        weigh(first, 0)
        for stage in range(1, stages):
            weigh(first, stage)
            gather_up(stage - 1)
        gather_up(stages - 1)
        mass = total_ref[:, width : 2 * width]
        prior = prior_weight * cent_ref[pl.ds(first, tile), :].astype(jnp.float32)
        new = (total_ref[:, 0:width] + prior) / (mass + prior_weight)
        code_ref[pl.ds(first, tile), :] = encoded(new)
        for k in range(tile // 128):
            square = jnp.where(diagonal, mass[k * 128 : (k + 1) * 128, :], 0.0)
            mass_ref[pl.ds(r * (tile // 128) + k, 1), :] = jnp.sum(square, axis=0, keepdims=True)

    pl.loop(0, tiles // 2)(run)
    if placing:
        pl.when(step == 0)(placing.place)
    pl.loop(tiles // 2, tiles)(run)

    terms = split_exactly(mass_ref[...])
    terms = jnp.concatenate([*terms, jnp.zeros_like(terms[0])], axis=0)
    code_ref[block_rows : block_rows + terms.shape[0], :] = terms.astype(jnp.bfloat16)
    if placing:
        pl.when(step == steps - 1)(placing.finish)


def updated_chunk(
    table, chunk, toks, lse, centroids, blocks, block_rows, after=(), received=None, joins=0
):
    all_count, width = toks.shape
    depth = divisor(all_count, 2048)
    tile = divisor(block_rows, 1024)
    rows = blocks * block_rows
    full = coded_rows(block_rows)
    anywhere = pl.BlockSpec(memory_space=pl.ANY)
    whole = lambda j, place: (0, 0)
    operands = [
        pltpu.with_memory_space_constraint(toks, pltpu.HBM),
        lse,
        pltpu.with_memory_space_constraint(centroids, pltpu.HBM),
        *after,
    ]
    in_specs = [
        pl.BlockSpec((all_count, width), whole),
        pl.BlockSpec(lse.shape, (lambda j, place: (0, 0, 0)) if joins else whole),
        pl.BlockSpec((block_rows, width), lambda j, table: (table[chunk, 0] + j, 0)),
    ] + [anywhere] * len(after)
    out_specs = [pl.BlockSpec((full, width), lambda j, place: (j, 0))]
    out_shape = [jax.ShapeDtypeStruct((blocks * full, width), jnp.bfloat16)]
    scratch_shapes = [
        pltpu.VMEM((2, tile, depth), jnp.bfloat16),
        pltpu.VMEM((tile, 2 * width), jnp.float32),
        pltpu.VMEM((block_rows // 128, 128), jnp.float32),
    ]
    aliases, pieces, placed_chunk = {}, [], None
    if joins:
        out_specs.append(pl.BlockSpec((1, all_count), whole))
        out_shape.append(jax.ShapeDtypeStruct((1, all_count), jnp.float32))
    if received:
        placed_chunk, codes, outs = received
        pieces = [len(parts) for parts in codes]
        operands += [pltpu.with_memory_space_constraint(part, pltpu.HBM) for part in sum(codes, [])]
        operands += outs
        in_specs += [anywhere] * (sum(pieces) + 2)
        out_specs += [anywhere] * 2
        out_shape += [jax.ShapeDtypeStruct(out.shape, out.dtype) for out in outs]
        aliases = {len(operands) - 1: 1, len(operands): 2}
        scratch_shapes += Placing.scratch(len(codes), codes[0][0].shape[0] // full, block_rows, width)
    return pl.pallas_call(
        functools.partial(update_kernel, joins, len(after), placed_chunk, pieces, block_rows),
        grid_spec=pltpu.PrefetchScalarGridSpec(
            num_scalar_prefetch=1,
            grid=(blocks,),
            in_specs=in_specs,
            out_specs=out_specs,
            scratch_shapes=scratch_shapes,
        ),
        out_shape=out_shape,
        input_output_aliases=aliases,
        compiler_params=pltpu.CompilerParams(vmem_limit_bytes=vmem_bytes * 3 // 4),
        cost_estimate=pl.CostEstimate(
            flops=6 * all_count * rows * width // 8,
            bytes_accessed=(2 * all_count + 4 * rows) * width // 8,
            transcendentals=all_count * rows // 8,
        ),
        name="new_rows",
    )(table, *operands)


def place_kernel(chunks, block_rows, table_ref, *refs):
    count = sum(sum(pieces) for _, pieces in chunks)
    code_refs, outs, scratch = refs[:count], refs[count + 2 : count + 4], refs[count + 4 :]
    placings = []
    for chunk, pieces in chunks:
        used = code_refs[: sum(pieces)]
        placings.append(Placing(block_rows, table_ref, chunk, pieces, used, outs, scratch[:4]))
        code_refs, scratch = code_refs[sum(pieces) :], scratch[4:]
    for placing in placings:
        placing.fetch()
    for placing in placings:
        placing.place()
    for placing in placings:
        placing.finish()


def placed(table, received, outs, block_rows):
    operands, chunks, scratch_shapes = [], [], []
    for chunk, codes in received:
        chunks.append((chunk, [len(parts) for parts in codes]))
        operands += sum(codes, [])
        rows, width = codes[0][0].shape
        blocks = rows // coded_rows(block_rows)
        scratch_shapes += Placing.scratch(len(codes), blocks, block_rows, width)
    anywhere = pl.BlockSpec(memory_space=pl.ANY)
    return pl.pallas_call(
        functools.partial(place_kernel, chunks, block_rows),
        grid_spec=pltpu.PrefetchScalarGridSpec(
            num_scalar_prefetch=1,
            grid=(1,),
            in_specs=[anywhere] * (len(operands) + 2),
            out_specs=[anywhere] * 2,
            scratch_shapes=scratch_shapes,
        ),
        out_shape=[jax.ShapeDtypeStruct(out.shape, out.dtype) for out in outs],
        input_output_aliases={1 + len(operands): 0, 2 + len(operands): 1},
        compiler_params=pltpu.CompilerParams(vmem_limit_bytes=vmem_bytes // 2),
        name="placed_rows",
    )(table, *operands, *outs)


def blank(shape):
    return pl.pallas_call(
        lambda out_ref: None,
        out_specs=pl.BlockSpec(memory_space=pl.ANY),
        out_shape=jax.ShapeDtypeStruct(shape, jnp.float32),
        name="blank",
    )()


def from_others(value, axis):
    size = lax.axis_size(axis)
    found = [value]
    for s in range(1, size):
        pairs = [(partner(k, s, size), k) for k in range(size)]
        found.append(lax.ppermute(value, axis, pairs))
    return found


def partner(me, s, size):
    return me ^ s if size & (size - 1) == 0 else (me - s) % size


def chunk_plan(blocks):
    plan = []
    while blocks > 2:
        plan.append(2)
        blocks -= 2
    return plan + [1] * blocks


def local(tokens, centroids):
    tok_size, cent_size = lax.axis_size("tok"), lax.axis_size("cent")
    me = lax.axis_index("tok")
    cent_count, width = centroids.shape
    share_rows = cent_count // tok_size

    toks = lax.all_gather(tokens, "tok", axis=0, tiled=True)
    own_lse = local_lse(tokens, centroids, tok_size * cent_size)
    parts = lax.all_to_all(own_lse, ("tok", "cent"), 0, 0, tiled=True)

    block_rows = divisor(share_rows, 1024)
    plan = chunk_plan(share_rows // block_rows)
    sources = jnp.stack([partner(me, s, tok_size) for s in range(tok_size)])[None, :]
    starts = np.cumsum([0] + plan[:-1])[:, None] * tok_size
    table = (starts + sources * np.array(plan)[:, None]).astype(jnp.int32)
    outs = blank((cent_count, width)), blank((cent_count // 128, 128))
    waiting = []
    for k, blocks in enumerate(plan):
        arrived, received = [], None
        if len(waiting) > 1:
            arrived = sum(waiting[-2][1][1:], [])
            if blocks == 1:
                received = (*waiting.pop(0), outs)
                arrived = arrived[:1] if k + 1 == len(plan) else arrived
        operands = toks, lse if k else parts, centroids, blocks, block_rows, arrived, received
        codes, *rest = updated_chunk(table, k, *operands, joins=0 if k else tok_size)
        if not k:
            (lse,) = rest
        elif received:
            outs = rest
        waiting.append((k, [[part] for part in from_others(codes, "tok")]))
    if len(waiting) > 1:
        outs = placed(table, waiting[:-1], outs, block_rows)
    outs = placed(table, waiting[-1:], outs, block_rows)
    return outs[0], outs[1].reshape(cent_count)


def solution(mesh):
    placed_as = (P("tok", None), P("cent", None))
    return jax.shard_map(
        local, mesh=mesh, in_specs=placed_as, out_specs=(P("cent", None), P("cent")), check_vma=False
    )
```

```python
import functools

import jax
import jax.numpy as jnp
import numpy as np
from jax import lax
from jax.experimental import pallas as pl
from jax.experimental.pallas import tpu as pltpu
from jax.sharding import PartitionSpec as P

inverse_temp = 2.0
prior_weight = 0.05
safe_sum = 1e30
headroom = 60.0
code_scale = 2.0**24
slice_rows = 64
vmem_bytes = 56 * 1024 * 1024


def divisor(count, most):
    size = min(count, most)
    while count % size:
        size //= 2
    return size


def dot_nt(a, b):
    return lax.dot_general(a, b, (((1,), (1,)), ((), ())), preferred_element_type=jnp.float32)


def fold_rows(x, combine):
    parts = [x[k * 8 : (k + 1) * 8, :] for k in range(x.shape[0] // 8)]
    while len(parts) > 1:
        half = len(parts) // 2
        parts = [combine(parts[2 * k], parts[2 * k + 1]) for k in range(half)] + parts[2 * half :]
    return parts[0]


def split_exactly(x):
    high = x.astype(jnp.bfloat16).astype(jnp.float32)
    middle = (x - high).astype(jnp.bfloat16).astype(jnp.float32)
    return high, middle, x - high - middle


def stats_kernel(
    sub_rows, tok_cols, tok_ref, cent_ref, out_ref, flip_ref, base_ref, shift_ref, sums_ref, worst_ref
):
    step = pl.program_id(0)
    tok_count = tok_ref.shape[0]
    subs = cent_ref.shape[0] // sub_rows
    col_blocks = tok_count // tok_cols
    redo_cols = divisor(tok_cols, 256)
    redo_blocks = tok_count // redo_cols

    def columns(t, size=tok_cols):
        return pl.ds(pl.multiple_of(t * size, size), size)

    def dot(a, b):
        return jnp.dot(a, b, preferred_element_type=jnp.float32)

    width = tok_ref.shape[1]

    @pl.when(step == 0)
    def _():
        @pl.loop(0, col_blocks)
        def _(t):
            flipped = (tok_ref[columns(t), :] * jnp.bfloat16(inverse_temp)).T
            flip_ref[0:width, columns(t)] = flipped
            logits = dot(cent_ref[0:128, :], flipped)
            top = jnp.max(fold_rows(logits, jnp.maximum), axis=0, keepdims=True)
            base = top + headroom
            base_ref[:, columns(t)] = base
            row = lax.broadcasted_iota(jnp.int32, (width, tok_cols), 0)
            terms = jnp.zeros((width, tok_cols), jnp.float32)
            for k, term in enumerate(split_exactly(-base)):
                terms = jnp.where(row == k, term, terms)
            flip_ref[width:, columns(t)] = terms.astype(jnp.bfloat16)

    lane = lax.broadcasted_iota(jnp.int32, (sub_rows, width), 1)
    ones = jnp.where(lane < 3, 1.0, 0.0).astype(jnp.bfloat16)

    @pl.loop(0, col_blocks)
    def _(t):
        rhs = flip_ref[:, columns(t)]
        shift = base_ref[:, columns(t)]
        for sub in range(subs):
            total = jnp.zeros((8, tok_cols), jnp.float32)
            lhs = jnp.concatenate([cent_ref[pl.ds(sub * sub_rows, sub_rows), :], ones], axis=1)
            logits = dot(lhs, rhs)
            for first in range(0, sub_rows, slice_rows):
                scaled = jnp.exp(logits[first : first + slice_rows])
                total = total + fold_rows(scaled, jnp.add)
            sums_ref[step * subs + sub, :, columns(t)] = total
            shift_ref[step * subs + sub, :, columns(t)] = shift

    worst = jnp.float32(0.0)
    for sub in range(subs):
        for t in range(redo_blocks):
            block = jnp.max(sums_ref[step * subs + sub, :, t * redo_cols : (t + 1) * redo_cols])
            worst_ref[sub * redo_blocks + t] = block
            worst = jnp.maximum(worst, block)

    @pl.when(jnp.logical_not(worst < safe_sum))
    def _():
        @pl.loop(0, subs * redo_blocks)
        def _(k):
            @pl.when(jnp.logical_not(worst_ref[k] < safe_sum))
            def _():
                sub, t = k // redo_blocks, lax.rem(k, redo_blocks)
                first = pl.multiple_of(sub * sub_rows, sub_rows)
                rhs = flip_ref[0:width, columns(t, redo_cols)]
                logits = dot(cent_ref[pl.ds(first, sub_rows), :], rhs)
                top = jnp.max(fold_rows(logits, jnp.maximum), axis=0, keepdims=True)
                total = fold_rows(jnp.exp(logits - top), jnp.add)
                sums_ref[step * subs + sub, :, columns(t, redo_cols)] = total
                shift_ref[step * subs + sub, :, columns(t, redo_cols)] = top

    @pl.when(step == pl.num_programs(0) - 1)
    def _():
        @pl.loop(0, col_blocks)
        def _(t):
            shifts = shift_ref[:, :, columns(t)]
            top = jnp.max(shifts, axis=0)
            scale = jnp.exp(shifts - top[None])
            total = jnp.sum(sums_ref[:, :, columns(t)] * scale, axis=0)
            total = jnp.sum(total, axis=0, keepdims=True)
            out_ref[:, :, columns(t)] = jnp.broadcast_to(
                (top + jnp.log(total))[None], (out_ref.shape[0], 1, tok_cols)
            )


def local_lse(tokens, centroids, copies):
    tok_count, width = tokens.shape
    cent_count = centroids.shape[0]
    block_rows = divisor(cent_count, 4096)
    sub_rows = divisor(block_rows, 1024)
    tok_cols = divisor(tok_count, 512)
    blocks = cent_count // block_rows
    subs = cent_count // sub_rows
    flags = block_rows // sub_rows * (tok_count // divisor(tok_cols, 256))
    return pl.pallas_call(
        functools.partial(stats_kernel, sub_rows, tok_cols),
        grid=(blocks,),
        in_specs=[
            pl.BlockSpec((tok_count, width), lambda j: (0, 0)),
            pl.BlockSpec((block_rows, width), lambda j: (j, 0)),
        ],
        out_specs=pl.BlockSpec((copies, 1, tok_count), lambda j: (0, 0, 0)),
        out_shape=jax.ShapeDtypeStruct((copies, 1, tok_count), jnp.float32),
        scratch_shapes=[
            pltpu.VMEM((2 * width, tok_count), jnp.bfloat16),
            pltpu.VMEM((1, tok_count), jnp.float32),
            pltpu.VMEM((subs, 1, tok_count), jnp.float32),
            pltpu.VMEM((subs, 8, tok_count), jnp.float32),
            pltpu.SMEM((flags,), jnp.float32),
        ],
        compiler_params=pltpu.CompilerParams(vmem_limit_bytes=vmem_bytes),
        cost_estimate=pl.CostEstimate(
            flops=2 * tok_count * cent_count * width,
            bytes_accessed=(tok_count + cent_count) * width * 2,
            transcendentals=tok_count * cent_count,
        ),
        name="row_stats",
    )(tokens, centroids)


def encoded(x):
    x = x * code_scale
    return (x * jnp.abs(x) * (x * x)).astype(jnp.bfloat16)


def decoded(code):
    code = code.astype(jnp.float32)
    size = lax.rsqrt(lax.rsqrt(jnp.maximum(jnp.abs(code), 1e-37))) * (1.0 / code_scale)
    return jnp.where(code < 0, -size, jnp.where(code > 0, size, 0.0))


class Placing:
    def __init__(self, block_rows, table_ref, chunk, pieces, code_refs, outs, scratch):
        self.block_rows, self.table_ref, self.chunk = block_rows, table_ref, chunk
        self.pieces, self.code_refs = pieces, code_refs
        self.updated_ref, self.masses_ref = outs
        self.codes, self.values, self.masses, self.sems = scratch

    @staticmethod
    def scratch(sources, blocks, block_rows, width):
        return [
            pltpu.VMEM((sources, blocks * coded_rows(block_rows), width), jnp.bfloat16),
            pltpu.VMEM((sources, blocks * block_rows, width), jnp.float32),
            pltpu.VMEM((sources, blocks * block_rows // 128, 128), jnp.float32),
            pltpu.SemaphoreType.DMA((4, sources)),
        ]

    def copies_in(self):
        found, refs = [], list(self.code_refs)
        for s, count in enumerate(self.pieces):
            found.append([])
            first = 0
            for k in range(count):
                ref = refs.pop(0)
                target = self.codes.at[s, pl.ds(first, ref.shape[0]), :]
                found[s].append(pltpu.make_async_copy(ref, target, self.sems.at[3 * k, s]))
                first += ref.shape[0]
        return found

    def copies_out(self, s):
        rows, mass_rows = self.values.shape[1], self.masses.shape[1]
        start = self.table_ref[self.chunk, s]
        span = pl.ds(pl.multiple_of(start * self.block_rows, self.block_rows), rows)
        per_block = self.block_rows // 128
        mass_span = pl.ds(pl.multiple_of(start * per_block, per_block), mass_rows)
        return [
            pltpu.make_async_copy(self.values.at[s], self.updated_ref.at[span, :], self.sems.at[1, s]),
            pltpu.make_async_copy(self.masses.at[s], self.masses_ref.at[mass_span, :], self.sems.at[2, s]),
        ]

    def fetch(self):
        for copies in self.copies_in():
            for copy in copies:
                copy.start()

    def place(self):
        block_rows, per_block = self.block_rows, self.block_rows // 128
        full = coded_rows(block_rows)
        tile = divisor(block_rows, 256)
        for s, copies in enumerate(self.copies_in()):
            for copy in copies:
                copy.wait()

            @pl.loop(0, self.values.shape[1] // block_rows)
            def _(b):
                for k in range(block_rows // tile):
                    source = pl.ds(pl.multiple_of(b * full + k * tile, 32), tile)
                    target = pl.ds(pl.multiple_of(b * block_rows + k * tile, tile), tile)
                    self.values[s, target, :] = decoded(self.codes[s, source, :])
                last = pl.ds(pl.multiple_of(b * full + block_rows, 32), full - block_rows)
                terms = self.codes[s, last, :].astype(jnp.float32)
                mass = terms[:per_block] + terms[per_block : 2 * per_block]
                mass = mass + terms[2 * per_block : 3 * per_block]
                self.masses[s, pl.ds(pl.multiple_of(b * per_block, per_block), per_block), :] = mass

            for copy in self.copies_out(s):
                copy.start()

    def finish(self):
        for s in range(len(self.pieces)):
            for copy in self.copies_out(s):
                copy.wait()


def coded_rows(block_rows):
    return block_rows + block_rows // 32


def combine(groups, parts_ref, out_ref):
    per_group = parts_ref.shape[0] // groups
    count = parts_ref.shape[2]
    for t in range(groups):
        parts = [parts_ref[t * per_group + k] for k in range(per_group)]
        top = functools.reduce(jnp.maximum, parts)
        total = functools.reduce(jnp.add, [jnp.exp(part - top) for part in parts])
        out_ref[:, t * count : (t + 1) * count] = top + jnp.log(total)


def update_kernel(chunk, joins, unread, placed_chunk, pieces, block_rows, *refs):
    table_ref, tok_ref, lse_ref, cent_ref = refs[:4]
    refs = refs[4 + unread :]
    code_refs, refs = refs[: sum(pieces)], refs[sum(pieces) :]
    if pieces:
        code_ref, updated_ref, masses_ref = refs[2:5]
        scratch = refs[5:]
        outs = updated_ref, masses_ref
        placing = Placing(block_rows, table_ref, placed_chunk, pieces, code_refs, outs, scratch[6:])
    else:
        code_ref, scratch, placing = refs[0], refs[1:], None
    if joins:
        parts_ref, lse_ref, scratch = lse_ref, scratch[0], scratch[1:]
    weights_ref, total_ref, mass_ref, toks_ref, cents_ref, sems = scratch[:6]
    rows, width = cents_ref.shape
    _, tile, depth = weights_ref.shape
    piece = divisor(depth, 512)
    stages = toks_ref.shape[0] // depth
    full = coded_rows(block_rows)

    first_row = pl.multiple_of(table_ref[chunk, 0] * block_rows, block_rows)
    loads = [pltpu.make_async_copy(cent_ref.at[pl.ds(first_row, rows), :], cents_ref, sems.at[0])]
    for stage in range(stages):
        span = pl.ds(stage * depth, depth)
        loads.append(pltpu.make_async_copy(tok_ref.at[span, :], toks_ref.at[span, :], sems.at[1 + stage]))
    for load in loads:
        load.start()
    if placing:
        placing.fetch()
    if joins:
        combine(joins, parts_ref, lse_ref)

    def weigh(first, stage):
        cents = cents_ref[pl.ds(first, tile), :] * jnp.bfloat16(inverse_temp)
        for k in range(depth // piece):
            span = pl.ds(stage * depth + k * piece, piece)
            logits = dot_nt(cents, toks_ref[span, :])
            lse = lse_ref[:, span]
            for r in range(0, tile, slice_rows):
                weights = jnp.exp(logits[r : r + slice_rows] - lse).astype(jnp.bfloat16)
                weights_ref[stage % 2, r : r + slice_rows, pl.ds(k * piece, piece)] = weights

    def gather_up(stage):
        toks = toks_ref[pl.ds(stage * depth, depth), :]
        rhs = jnp.concatenate([toks, jnp.ones_like(toks)], axis=1)
        part = jnp.dot(weights_ref[stage % 2], rhs, preferred_element_type=jnp.float32)
        if stage == 0:
            total_ref[...] = part
        else:
            total_ref[...] += part

    diagonal = lax.broadcasted_iota(jnp.int32, (128, 128), 0) == lax.broadcasted_iota(
        jnp.int32, (128, 128), 1
    )

    def run(r, waits):
        first = r * tile
        for stage in range(stages):
            if waits:
                waits[stage].wait()
            weigh(first, stage)
            if stage:
                gather_up(stage - 1)
        gather_up(stages - 1)
        mass = total_ref[:, width : 2 * width]
        prior = prior_weight * cents_ref[pl.ds(first, tile), :].astype(jnp.float32)
        new = (total_ref[:, 0:width] + prior) / (mass + prior_weight)
        code_ref[pl.ds(first + first // block_rows * (full - block_rows), tile), :] = encoded(new)
        for k in range(tile // 128):
            square = jnp.where(diagonal, mass[k * 128 : (k + 1) * 128, :], 0.0)
            mass_ref[pl.ds(first // 128 + k, 1), :] = jnp.sum(square, axis=0, keepdims=True)

    loads[0].wait()
    for r in range(rows // tile):
        run(r, () if r else loads[1:])
        if placing and not r:
            placing.place()

    per_block = block_rows // 128
    for block in range(rows // block_rows):
        terms = split_exactly(mass_ref[block * per_block : (block + 1) * per_block, :])
        terms = jnp.concatenate([*terms, jnp.zeros_like(terms[0])], axis=0)
        last = block * full + block_rows
        code_ref[last : last + terms.shape[0], :] = terms.astype(jnp.bfloat16)
    if placing:
        placing.finish()


def updated_chunk(
    table, chunk, toks, lse, centroids, blocks, block_rows, after=(), received=None, joins=0
):
    all_count, width = toks.shape
    depth = divisor(all_count, 2048)
    tile = divisor(block_rows, 1024)
    rows = blocks * block_rows
    full = coded_rows(block_rows)
    anywhere = pl.BlockSpec(memory_space=pl.ANY)
    whole = lambda j, place: (0, 0)
    operands = [
        pltpu.with_memory_space_constraint(toks, pltpu.HBM),
        lse,
        pltpu.with_memory_space_constraint(centroids, pltpu.HBM),
        *after,
    ]
    in_specs = [
        anywhere,
        pl.BlockSpec(lse.shape, (lambda j, table: (0, 0, 0)) if joins else whole),
        anywhere,
    ] + [anywhere] * len(after)
    out_specs = [pl.BlockSpec((blocks * full, width), whole)]
    out_shape = [jax.ShapeDtypeStruct((blocks * full, width), jnp.bfloat16)]
    scratch_shapes = [
        pltpu.VMEM((2, tile, depth), jnp.bfloat16),
        pltpu.VMEM((tile, 2 * width), jnp.float32),
        pltpu.VMEM((rows // 128, 128), jnp.float32),
        pltpu.VMEM((all_count, width), jnp.bfloat16),
        pltpu.VMEM((rows, width), jnp.bfloat16),
        pltpu.SemaphoreType.DMA((1 + all_count // depth,)),
    ]
    aliases, pieces, placed_chunk = {}, [], None
    if joins:
        out_specs.append(pl.BlockSpec((1, all_count), whole))
        out_shape.append(jax.ShapeDtypeStruct((1, all_count), jnp.float32))
    if received:
        placed_chunk, codes, outs = received
        pieces = [len(parts) for parts in codes]
        operands += [pltpu.with_memory_space_constraint(part, pltpu.HBM) for part in sum(codes, [])]
        operands += outs
        in_specs += [anywhere] * (sum(pieces) + 2)
        out_specs += [anywhere] * 2
        out_shape += [jax.ShapeDtypeStruct(out.shape, out.dtype) for out in outs]
        aliases = {len(operands) - 1: 1, len(operands): 2}
        scratch_shapes += Placing.scratch(len(codes), codes[0][0].shape[0] // full, block_rows, width)
    return pl.pallas_call(
        functools.partial(
            update_kernel, chunk, joins, len(after), placed_chunk, pieces, block_rows
        ),
        grid_spec=pltpu.PrefetchScalarGridSpec(
            num_scalar_prefetch=1,
            grid=(1,),
            in_specs=in_specs,
            out_specs=out_specs,
            scratch_shapes=scratch_shapes,
        ),
        out_shape=out_shape,
        input_output_aliases=aliases,
        compiler_params=pltpu.CompilerParams(vmem_limit_bytes=vmem_bytes * 3 // 4),
        cost_estimate=pl.CostEstimate(
            flops=6 * all_count * rows * width // 8,
            bytes_accessed=(2 * all_count + 4 * rows) * width // 8,
            transcendentals=all_count * rows // 8,
        ),
        name="new_rows",
    )(table, *operands)


def place_kernel(chunks, block_rows, table_ref, *refs):
    count = sum(sum(pieces) for _, pieces in chunks)
    code_refs, outs, scratch = refs[:count], refs[count + 2 : count + 4], refs[count + 4 :]
    placings = []
    for chunk, pieces in chunks:
        used = code_refs[: sum(pieces)]
        placings.append(Placing(block_rows, table_ref, chunk, pieces, used, outs, scratch[:4]))
        code_refs, scratch = code_refs[sum(pieces) :], scratch[4:]
    for placing in placings:
        placing.fetch()
    for placing in placings:
        placing.place()
    for placing in placings:
        placing.finish()


def placed(table, received, outs, block_rows):
    operands, chunks, scratch_shapes = [], [], []
    for chunk, codes in received:
        chunks.append((chunk, [len(parts) for parts in codes]))
        operands += sum(codes, [])
        rows, width = codes[0][0].shape
        blocks = rows // coded_rows(block_rows)
        scratch_shapes += Placing.scratch(len(codes), blocks, block_rows, width)
    anywhere = pl.BlockSpec(memory_space=pl.ANY)
    return pl.pallas_call(
        functools.partial(place_kernel, chunks, block_rows),
        grid_spec=pltpu.PrefetchScalarGridSpec(
            num_scalar_prefetch=1,
            grid=(1,),
            in_specs=[anywhere] * (len(operands) + 2),
            out_specs=[anywhere] * 2,
            scratch_shapes=scratch_shapes,
        ),
        out_shape=[jax.ShapeDtypeStruct(out.shape, out.dtype) for out in outs],
        input_output_aliases={1 + len(operands): 0, 2 + len(operands): 1},
        compiler_params=pltpu.CompilerParams(vmem_limit_bytes=vmem_bytes // 2),
        name="placed_rows",
    )(table, *operands, *outs)


def blank(shape):
    return pl.pallas_call(
        lambda out_ref: None,
        out_specs=pl.BlockSpec(memory_space=pl.ANY),
        out_shape=jax.ShapeDtypeStruct(shape, jnp.float32),
        name="blank",
    )()


def from_others(value, axis):
    size = lax.axis_size(axis)
    found = [value]
    for s in range(1, size):
        pairs = [(partner(k, s, size), k) for k in range(size)]
        found.append(lax.ppermute(value, axis, pairs))
    return found


def partner(me, s, size):
    return me ^ s if size & (size - 1) == 0 else (me - s) % size


def chunk_plan(blocks):
    plan = []
    while blocks > 2:
        plan.append(2)
        blocks -= 2
    return plan + [1] * blocks


def local(tokens, centroids):
    tok_size, cent_size = lax.axis_size("tok"), lax.axis_size("cent")
    me = lax.axis_index("tok")
    cent_count, width = centroids.shape
    share_rows = cent_count // tok_size

    toks = lax.all_gather(tokens, "tok", axis=0, tiled=True)
    own_lse = local_lse(tokens, centroids, tok_size * cent_size)
    parts = lax.all_to_all(own_lse, ("tok", "cent"), 0, 0, tiled=True)

    block_rows = divisor(share_rows, 1024)
    plan = chunk_plan(share_rows // block_rows)
    sources = jnp.stack([partner(me, s, tok_size) for s in range(tok_size)])[None, :]
    starts = np.cumsum([0] + plan[:-1])[:, None] * tok_size
    table = (starts + sources * np.array(plan)[:, None]).astype(jnp.int32)
    outs = blank((cent_count, width)), blank((cent_count // 128, 128))
    waiting = []
    for k, blocks in enumerate(plan):
        arrived, received = [], None
        if len(waiting) > 1:
            arrived = sum(waiting[-2][1][1:], [])
            if blocks == 1:
                received = (*waiting.pop(0), outs)
                arrived = arrived[:1] if k + 1 == len(plan) else arrived
        operands = toks, lse if k else parts, centroids, blocks, block_rows, arrived, received
        codes, *rest = updated_chunk(table, k, *operands, joins=0 if k else tok_size)
        if not k:
            (lse,) = rest
        elif received:
            outs = rest
        waiting.append((k, [[part] for part in from_others(codes, "tok")]))
    if len(waiting) > 1:
        outs = placed(table, waiting[:-1], outs, block_rows)
    outs = placed(table, waiting[-1:], outs, block_rows)
    return outs[0], outs[1].reshape(cent_count)


def solution(mesh):
    placed_as = (P("tok", None), P("cent", None))
    return jax.shard_map(
        local, mesh=mesh, in_specs=placed_as, out_specs=(P("cent", None), P("cent")), check_vma=False
    )
```

```python
import functools

import jax
import jax.numpy as jnp
import numpy as np
from jax import lax
from jax.experimental import pallas as pl
from jax.experimental.pallas import tpu as pltpu
from jax.sharding import PartitionSpec as P

inverse_temp = 2.0
prior_weight = 0.05
safe_sum = 1e30
headroom = 60.0
code_scale = 2.0**24
slice_rows = 64
vmem_bytes = 56 * 1024 * 1024


def divisor(count, most):
    size = min(count, most)
    while count % size:
        size //= 2
    return size


def dot_nt(a, b):
    return lax.dot_general(a, b, (((1,), (1,)), ((), ())), preferred_element_type=jnp.float32)


def fold_rows(x, combine):
    parts = [x[k * 8 : (k + 1) * 8, :] for k in range(x.shape[0] // 8)]
    while len(parts) > 1:
        half = len(parts) // 2
        parts = [combine(parts[2 * k], parts[2 * k + 1]) for k in range(half)] + parts[2 * half :]
    return parts[0]


def split_exactly(x):
    high = x.astype(jnp.bfloat16).astype(jnp.float32)
    middle = (x - high).astype(jnp.bfloat16).astype(jnp.float32)
    return high, middle, x - high - middle


def stats_kernel(
    sub_rows, tok_cols, tok_ref, cent_ref, out_ref, flip_ref, base_ref, shift_ref, sums_ref, worst_ref
):
    step = pl.program_id(0)
    tok_count = tok_ref.shape[0]
    subs = cent_ref.shape[0] // sub_rows
    col_blocks = tok_count // tok_cols
    redo_cols = divisor(tok_cols, 256)
    redo_blocks = tok_count // redo_cols

    def columns(t, size=tok_cols):
        return pl.ds(pl.multiple_of(t * size, size), size)

    def dot(a, b):
        return jnp.dot(a, b, preferred_element_type=jnp.float32)

    width = tok_ref.shape[1]

    @pl.when(step == 0)
    def _():
        @pl.loop(0, col_blocks)
        def _(t):
            flipped = (tok_ref[columns(t), :] * jnp.bfloat16(inverse_temp)).T
            flip_ref[0:width, columns(t)] = flipped
            logits = dot(cent_ref[0:128, :], flipped)
            top = jnp.max(fold_rows(logits, jnp.maximum), axis=0, keepdims=True)
            base = top + headroom
            base_ref[:, columns(t)] = base
            row = lax.broadcasted_iota(jnp.int32, (width, tok_cols), 0)
            terms = jnp.zeros((width, tok_cols), jnp.float32)
            for k, term in enumerate(split_exactly(-base)):
                terms = jnp.where(row == k, term, terms)
            flip_ref[width:, columns(t)] = terms.astype(jnp.bfloat16)

    lane = lax.broadcasted_iota(jnp.int32, (sub_rows, width), 1)
    ones = jnp.where(lane < 3, 1.0, 0.0).astype(jnp.bfloat16)

    @pl.loop(0, col_blocks)
    def _(t):
        rhs = flip_ref[:, columns(t)]
        shift = base_ref[:, columns(t)]
        for sub in range(subs):
            total = jnp.zeros((8, tok_cols), jnp.float32)
            lhs = jnp.concatenate([cent_ref[pl.ds(sub * sub_rows, sub_rows), :], ones], axis=1)
            logits = dot(lhs, rhs)
            for first in range(0, sub_rows, slice_rows):
                scaled = jnp.exp(logits[first : first + slice_rows])
                total = total + fold_rows(scaled, jnp.add)
            sums_ref[step * subs + sub, :, columns(t)] = total
            shift_ref[step * subs + sub, :, columns(t)] = shift

    worst = jnp.float32(0.0)
    for sub in range(subs):
        for t in range(redo_blocks):
            block = jnp.max(sums_ref[step * subs + sub, :, t * redo_cols : (t + 1) * redo_cols])
            worst_ref[sub * redo_blocks + t] = block
            worst = jnp.maximum(worst, block)

    @pl.when(jnp.logical_not(worst < safe_sum))
    def _():
        @pl.loop(0, subs * redo_blocks)
        def _(k):
            @pl.when(jnp.logical_not(worst_ref[k] < safe_sum))
            def _():
                sub, t = k // redo_blocks, lax.rem(k, redo_blocks)
                first = pl.multiple_of(sub * sub_rows, sub_rows)
                rhs = flip_ref[0:width, columns(t, redo_cols)]
                logits = dot(cent_ref[pl.ds(first, sub_rows), :], rhs)
                top = jnp.max(fold_rows(logits, jnp.maximum), axis=0, keepdims=True)
                total = fold_rows(jnp.exp(logits - top), jnp.add)
                sums_ref[step * subs + sub, :, columns(t, redo_cols)] = total
                shift_ref[step * subs + sub, :, columns(t, redo_cols)] = top

    @pl.when(step == pl.num_programs(0) - 1)
    def _():
        @pl.loop(0, col_blocks)
        def _(t):
            shifts = shift_ref[:, :, columns(t)]
            top = jnp.max(shifts, axis=0)
            scale = jnp.exp(shifts - top[None])
            total = jnp.sum(sums_ref[:, :, columns(t)] * scale, axis=0)
            total = jnp.sum(total, axis=0, keepdims=True)
            out_ref[:, :, columns(t)] = jnp.broadcast_to(
                (top + jnp.log(total))[None], (out_ref.shape[0], 1, tok_cols)
            )


def local_lse(tokens, centroids, copies):
    tok_count, width = tokens.shape
    cent_count = centroids.shape[0]
    block_rows = divisor(cent_count, 4096)
    sub_rows = divisor(block_rows, 1024)
    tok_cols = divisor(tok_count, 512)
    blocks = cent_count // block_rows
    subs = cent_count // sub_rows
    flags = block_rows // sub_rows * (tok_count // divisor(tok_cols, 256))
    return pl.pallas_call(
        functools.partial(stats_kernel, sub_rows, tok_cols),
        grid=(blocks,),
        in_specs=[
            pl.BlockSpec((tok_count, width), lambda j: (0, 0)),
            pl.BlockSpec((block_rows, width), lambda j: (j, 0)),
        ],
        out_specs=pl.BlockSpec((copies, 1, tok_count), lambda j: (0, 0, 0)),
        out_shape=jax.ShapeDtypeStruct((copies, 1, tok_count), jnp.float32),
        scratch_shapes=[
            pltpu.VMEM((2 * width, tok_count), jnp.bfloat16),
            pltpu.VMEM((1, tok_count), jnp.float32),
            pltpu.VMEM((subs, 1, tok_count), jnp.float32),
            pltpu.VMEM((subs, 8, tok_count), jnp.float32),
            pltpu.SMEM((flags,), jnp.float32),
        ],
        compiler_params=pltpu.CompilerParams(vmem_limit_bytes=vmem_bytes),
        cost_estimate=pl.CostEstimate(
            flops=2 * tok_count * cent_count * width,
            bytes_accessed=(tok_count + cent_count) * width * 2,
            transcendentals=tok_count * cent_count,
        ),
        name="row_stats",
    )(tokens, centroids)


def encoded(x):
    x = x * code_scale
    return (x * jnp.abs(x) * (x * x)).astype(jnp.bfloat16)


def decoded(code):
    code = code.astype(jnp.float32)
    size = lax.rsqrt(lax.rsqrt(jnp.maximum(jnp.abs(code), 1e-37))) * (1.0 / code_scale)
    return jnp.where(code < 0, -size, jnp.where(code > 0, size, 0.0))


class Placing:
    def __init__(self, block_rows, table_ref, chunk, pieces, code_refs, outs, scratch):
        self.block_rows, self.table_ref, self.chunk = block_rows, table_ref, chunk
        self.pieces, self.code_refs = pieces, code_refs
        self.updated_ref, self.masses_ref = outs
        self.codes, self.values, self.masses, self.sems = scratch

    @staticmethod
    def scratch(sources, blocks, block_rows, width):
        return [
            pltpu.VMEM((sources, blocks * coded_rows(block_rows), width), jnp.bfloat16),
            pltpu.VMEM((sources, blocks * block_rows, width), jnp.float32),
            pltpu.VMEM((sources, blocks * block_rows // 128, 128), jnp.float32),
            pltpu.SemaphoreType.DMA((4, sources)),
        ]

    def copies_in(self):
        found, refs = [], list(self.code_refs)
        for s, count in enumerate(self.pieces):
            found.append([])
            first = 0
            for k in range(count):
                ref = refs.pop(0)
                target = self.codes.at[s, pl.ds(first, ref.shape[0]), :]
                found[s].append(pltpu.make_async_copy(ref, target, self.sems.at[3 * k, s]))
                first += ref.shape[0]
        return found

    def copies_out(self, s):
        rows, mass_rows = self.values.shape[1], self.masses.shape[1]
        start = self.table_ref[self.chunk, s]
        span = pl.ds(pl.multiple_of(start * self.block_rows, self.block_rows), rows)
        per_block = self.block_rows // 128
        mass_span = pl.ds(pl.multiple_of(start * per_block, per_block), mass_rows)
        return [
            pltpu.make_async_copy(self.values.at[s], self.updated_ref.at[span, :], self.sems.at[1, s]),
            pltpu.make_async_copy(self.masses.at[s], self.masses_ref.at[mass_span, :], self.sems.at[2, s]),
        ]

    def fetch(self):
        for copies in self.copies_in():
            for copy in copies:
                copy.start()

    def place(self):
        block_rows, per_block = self.block_rows, self.block_rows // 128
        full = coded_rows(block_rows)
        tile = divisor(block_rows, 256)
        for s, copies in enumerate(self.copies_in()):
            for copy in copies:
                copy.wait()

            @pl.loop(0, self.values.shape[1] // block_rows)
            def _(b):
                for k in range(block_rows // tile):
                    source = pl.ds(pl.multiple_of(b * full + k * tile, 32), tile)
                    target = pl.ds(pl.multiple_of(b * block_rows + k * tile, tile), tile)
                    self.values[s, target, :] = decoded(self.codes[s, source, :])
                last = pl.ds(pl.multiple_of(b * full + block_rows, 32), full - block_rows)
                terms = self.codes[s, last, :].astype(jnp.float32)
                mass = terms[:per_block] + terms[per_block : 2 * per_block]
                mass = mass + terms[2 * per_block : 3 * per_block]
                self.masses[s, pl.ds(pl.multiple_of(b * per_block, per_block), per_block), :] = mass

            for copy in self.copies_out(s):
                copy.start()

    def finish(self):
        for s in range(len(self.pieces)):
            for copy in self.copies_out(s):
                copy.wait()


def coded_rows(block_rows):
    return block_rows + block_rows // 32


def combine(groups, parts_ref, out_ref):
    per_group = parts_ref.shape[0] // groups
    count = parts_ref.shape[2]
    for t in range(groups):
        parts = [parts_ref[t * per_group + k] for k in range(per_group)]
        top = functools.reduce(jnp.maximum, parts)
        total = functools.reduce(jnp.add, [jnp.exp(part - top) for part in parts])
        out_ref[:, t * count : (t + 1) * count] = top + jnp.log(total)


def update_kernel(joins, unread, placed_chunk, pieces, block_rows, *refs):
    table_ref, tok_ref, lse_ref, cent_ref = refs[:4]
    refs = refs[4 + unread :]
    code_refs, refs = refs[: sum(pieces)], refs[sum(pieces) :]
    if pieces:
        code_ref, updated_ref, masses_ref = refs[2:5]
        scratch = refs[5:]
        outs = updated_ref, masses_ref
        placing = Placing(block_rows, table_ref, placed_chunk, pieces, code_refs, outs, scratch[3:])
    else:
        code_ref, scratch, placing = refs[0], refs[1:], None
    if joins:
        parts_ref, lse_ref, scratch = lse_ref, scratch[0], scratch[1:]
        pl.when(pl.program_id(0) == 0)(lambda: combine(joins, parts_ref, lse_ref))
    weights_ref, total_ref, mass_ref = scratch[:3]
    step, steps = pl.program_id(0), pl.num_programs(0)
    width = tok_ref.shape[1]
    _, tile, depth = weights_ref.shape
    piece = divisor(depth, 512)
    stages = tok_ref.shape[0] // depth
    tiles = block_rows // tile

    if placing:
        pl.when(step == 0)(placing.fetch)

    def weigh(first, stage):
        cents = cent_ref[pl.ds(first, tile), :] * jnp.bfloat16(inverse_temp)
        for k in range(depth // piece):
            span = pl.ds(stage * depth + k * piece, piece)
            logits = dot_nt(cents, tok_ref[span, :])
            lse = lse_ref[:, span]
            for r in range(0, tile, slice_rows):
                weights = jnp.exp(logits[r : r + slice_rows] - lse).astype(jnp.bfloat16)
                weights_ref[stage % 2, r : r + slice_rows, pl.ds(k * piece, piece)] = weights

    def gather_up(stage):
        toks = tok_ref[pl.ds(stage * depth, depth), :]
        rhs = jnp.concatenate([toks, jnp.ones_like(toks)], axis=1)
        part = jnp.dot(weights_ref[stage % 2], rhs, preferred_element_type=jnp.float32)
        if stage == 0:
            total_ref[...] = part
        else:
            total_ref[...] += part

    diagonal = lax.broadcasted_iota(jnp.int32, (128, 128), 0) == lax.broadcasted_iota(
        jnp.int32, (128, 128), 1
    )

    def run(r):
        first = pl.multiple_of(r * tile, tile)
        weigh(first, 0)
        for stage in range(1, stages):
            weigh(first, stage)
            gather_up(stage - 1)
        gather_up(stages - 1)
        mass = total_ref[:, width : 2 * width]
        prior = prior_weight * cent_ref[pl.ds(first, tile), :].astype(jnp.float32)
        new = (total_ref[:, 0:width] + prior) / (mass + prior_weight)
        code_ref[pl.ds(first, tile), :] = encoded(new)
        for k in range(tile // 128):
            square = jnp.where(diagonal, mass[k * 128 : (k + 1) * 128, :], 0.0)
            mass_ref[pl.ds(r * (tile // 128) + k, 1), :] = jnp.sum(square, axis=0, keepdims=True)

    pl.loop(0, tiles // 2)(run)
    if placing:
        pl.when(step == 0)(placing.place)
    pl.loop(tiles // 2, tiles)(run)

    terms = split_exactly(mass_ref[...])
    terms = jnp.concatenate([*terms, jnp.zeros_like(terms[0])], axis=0)
    code_ref[block_rows : block_rows + terms.shape[0], :] = terms.astype(jnp.bfloat16)
    if placing:
        pl.when(step == steps - 1)(placing.finish)


def updated_chunk(
    table, chunk, toks, lse, centroids, blocks, block_rows, after=(), received=None, joins=0
):
    all_count, width = toks.shape
    depth = divisor(all_count, 2048)
    tile = divisor(block_rows, 1024)
    rows = blocks * block_rows
    full = coded_rows(block_rows)
    anywhere = pl.BlockSpec(memory_space=pl.ANY)
    whole = lambda j, place: (0, 0)
    operands = [
        pltpu.with_memory_space_constraint(toks, pltpu.HBM),
        lse,
        pltpu.with_memory_space_constraint(centroids, pltpu.HBM),
        *after,
    ]
    in_specs = [
        pl.BlockSpec((all_count, width), whole),
        pl.BlockSpec(lse.shape, (lambda j, place: (0, 0, 0)) if joins else whole),
        pl.BlockSpec((block_rows, width), lambda j, table: (table[chunk, 0] + j, 0)),
    ] + [anywhere] * len(after)
    out_specs = [pl.BlockSpec((full, width), lambda j, place: (j, 0))]
    out_shape = [jax.ShapeDtypeStruct((blocks * full, width), jnp.bfloat16)]
    scratch_shapes = [
        pltpu.VMEM((2, tile, depth), jnp.bfloat16),
        pltpu.VMEM((tile, 2 * width), jnp.float32),
        pltpu.VMEM((block_rows // 128, 128), jnp.float32),
    ]
    aliases, pieces, placed_chunk = {}, [], None
    if joins:
        out_specs.append(pl.BlockSpec((1, all_count), whole))
        out_shape.append(jax.ShapeDtypeStruct((1, all_count), jnp.float32))
    if received:
        placed_chunk, codes, outs = received
        pieces = [len(parts) for parts in codes]
        operands += [pltpu.with_memory_space_constraint(part, pltpu.HBM) for part in sum(codes, [])]
        operands += outs
        in_specs += [anywhere] * (sum(pieces) + 2)
        out_specs += [anywhere] * 2
        out_shape += [jax.ShapeDtypeStruct(out.shape, out.dtype) for out in outs]
        aliases = {len(operands) - 1: 1, len(operands): 2}
        scratch_shapes += Placing.scratch(len(codes), codes[0][0].shape[0] // full, block_rows, width)
    return pl.pallas_call(
        functools.partial(update_kernel, joins, len(after), placed_chunk, pieces, block_rows),
        grid_spec=pltpu.PrefetchScalarGridSpec(
            num_scalar_prefetch=1,
            grid=(blocks,),
            in_specs=in_specs,
            out_specs=out_specs,
            scratch_shapes=scratch_shapes,
        ),
        out_shape=out_shape,
        input_output_aliases=aliases,
        compiler_params=pltpu.CompilerParams(vmem_limit_bytes=vmem_bytes * 3 // 4),
        cost_estimate=pl.CostEstimate(
            flops=6 * all_count * rows * width // 8,
            bytes_accessed=(2 * all_count + 4 * rows) * width // 8,
            transcendentals=all_count * rows // 8,
        ),
        name="new_rows",
    )(table, *operands)


def place_kernel(chunks, block_rows, table_ref, *refs):
    count = sum(sum(pieces) for _, pieces in chunks)
    code_refs, outs, scratch = refs[:count], refs[count + 2 : count + 4], refs[count + 4 :]
    placings = []
    for chunk, pieces in chunks:
        used = code_refs[: sum(pieces)]
        placings.append(Placing(block_rows, table_ref, chunk, pieces, used, outs, scratch[:4]))
        code_refs, scratch = code_refs[sum(pieces) :], scratch[4:]
    for placing in placings:
        placing.fetch()
    for placing in placings:
        placing.place()
    for placing in placings:
        placing.finish()


def placed(table, received, outs, block_rows):
    operands, chunks, scratch_shapes = [], [], []
    for chunk, codes in received:
        chunks.append((chunk, [len(parts) for parts in codes]))
        operands += sum(codes, [])
        rows, width = codes[0][0].shape
        blocks = rows // coded_rows(block_rows)
        scratch_shapes += Placing.scratch(len(codes), blocks, block_rows, width)
    anywhere = pl.BlockSpec(memory_space=pl.ANY)
    return pl.pallas_call(
        functools.partial(place_kernel, chunks, block_rows),
        grid_spec=pltpu.PrefetchScalarGridSpec(
            num_scalar_prefetch=1,
            grid=(1,),
            in_specs=[anywhere] * (len(operands) + 2),
            out_specs=[anywhere] * 2,
            scratch_shapes=scratch_shapes,
        ),
        out_shape=[jax.ShapeDtypeStruct(out.shape, out.dtype) for out in outs],
        input_output_aliases={1 + len(operands): 0, 2 + len(operands): 1},
        compiler_params=pltpu.CompilerParams(vmem_limit_bytes=vmem_bytes // 2),
        name="placed_rows",
    )(table, *operands, *outs)


def blank(shape):
    return pl.pallas_call(
        lambda out_ref: None,
        out_specs=pl.BlockSpec(memory_space=pl.ANY),
        out_shape=jax.ShapeDtypeStruct(shape, jnp.float32),
        name="blank",
    )()


def from_others(value, axis):
    size = lax.axis_size(axis)
    found = [value]
    for s in range(1, size):
        pairs = [(partner(k, s, size), k) for k in range(size)]
        found.append(lax.ppermute(value, axis, pairs))
    return found


def partner(me, s, size):
    return me ^ s if size & (size - 1) == 0 else (me - s) % size


def chunk_plan(blocks):
    plan = [1] if blocks > 1 else []
    blocks -= len(plan)
    while blocks:
        plan.insert(0, min(blocks, 2 if blocks > 3 else 3))
        blocks -= plan[0]
    return plan


def local(tokens, centroids):
    tok_size, cent_size = lax.axis_size("tok"), lax.axis_size("cent")
    me = lax.axis_index("tok")
    cent_count, width = centroids.shape
    share_rows = cent_count // tok_size

    toks = lax.all_gather(tokens, "tok", axis=0, tiled=True)
    own_lse = local_lse(tokens, centroids, tok_size * cent_size)
    parts = lax.all_to_all(own_lse, ("tok", "cent"), 0, 0, tiled=True)

    block_rows = divisor(share_rows, 1024)
    plan = chunk_plan(share_rows // block_rows)
    sources = jnp.stack([partner(me, s, tok_size) for s in range(tok_size)])[None, :]
    starts = np.cumsum([0] + plan[:-1])[:, None] * tok_size
    table = (starts + sources * np.array(plan)[:, None]).astype(jnp.int32)
    outs = blank((cent_count, width)), blank((cent_count // 128, 128))
    waiting = []
    for k, blocks in enumerate(plan):
        arrived, received = [], None
        if len(waiting) > 1:
            arrived = sum(waiting[-2][1][1:2], [])
            if blocks == 1:
                received = (*waiting.pop(0), outs)
        operands = toks, lse if k else parts, centroids, blocks, block_rows, arrived, received
        codes, *rest = updated_chunk(table, k, *operands, joins=0 if k else tok_size)
        if not k:
            (lse,) = rest
        elif received:
            outs = rest
        waiting.append((k, [[part] for part in from_others(codes, "tok")]))
    if len(waiting) > 1:
        outs = placed(table, waiting[:-1], outs, block_rows)
    outs = placed(table, waiting[-1:], outs, block_rows)
    return outs[0], outs[1].reshape(cent_count)


def solution(mesh):
    placed_as = (P("tok", None), P("cent", None))
    return jax.shard_map(
        local, mesh=mesh, in_specs=placed_as, out_specs=(P("cent", None), P("cent")), check_vma=False
    )
```

```python
import functools

import jax
import jax.numpy as jnp
import numpy as np
from jax import lax
from jax.experimental import pallas as pl
from jax.experimental.pallas import tpu as pltpu
from jax.sharding import PartitionSpec as P

inverse_temp = 2.0
prior_weight = 0.05
safe_sum = 1e30
headroom = 60.0
code_scale = 2.0**24
slice_rows = 64
vmem_bytes = 56 * 1024 * 1024


def divisor(count, most):
    size = min(count, most)
    while count % size:
        size //= 2
    return size


def dot_nt(a, b):
    return lax.dot_general(a, b, (((1,), (1,)), ((), ())), preferred_element_type=jnp.float32)


def fold_rows(x, combine):
    parts = [x[k * 8 : (k + 1) * 8, :] for k in range(x.shape[0] // 8)]
    while len(parts) > 1:
        half = len(parts) // 2
        parts = [combine(parts[2 * k], parts[2 * k + 1]) for k in range(half)] + parts[2 * half :]
    return parts[0]


def split_exactly(x):
    high = x.astype(jnp.bfloat16).astype(jnp.float32)
    middle = (x - high).astype(jnp.bfloat16).astype(jnp.float32)
    return high, middle, x - high - middle


def stats_kernel(
    sub_rows, tok_cols, tok_ref, cent_ref, out_ref, flip_ref, base_ref, shift_ref, sums_ref, worst_ref
):
    step = pl.program_id(0)
    tok_count = tok_ref.shape[0]
    subs = cent_ref.shape[0] // sub_rows
    col_blocks = tok_count // tok_cols
    redo_cols = divisor(tok_cols, 256)
    redo_blocks = tok_count // redo_cols

    def columns(t, size=tok_cols):
        return pl.ds(pl.multiple_of(t * size, size), size)

    def dot(a, b):
        return jnp.dot(a, b, preferred_element_type=jnp.float32)

    width = tok_ref.shape[1]

    @pl.when(step == 0)
    def _():
        @pl.loop(0, col_blocks)
        def _(t):
            flipped = (tok_ref[columns(t), :] * jnp.bfloat16(inverse_temp)).T
            flip_ref[0:width, columns(t)] = flipped
            logits = dot(cent_ref[0:128, :], flipped)
            top = jnp.max(fold_rows(logits, jnp.maximum), axis=0, keepdims=True)
            base = top + headroom
            base_ref[:, columns(t)] = base
            row = lax.broadcasted_iota(jnp.int32, (width, tok_cols), 0)
            terms = jnp.zeros((width, tok_cols), jnp.float32)
            for k, term in enumerate(split_exactly(-base)):
                terms = jnp.where(row == k, term, terms)
            flip_ref[width:, columns(t)] = terms.astype(jnp.bfloat16)

    lane = lax.broadcasted_iota(jnp.int32, (sub_rows, width), 1)
    ones = jnp.where(lane < 3, 1.0, 0.0).astype(jnp.bfloat16)

    @pl.loop(0, col_blocks)
    def _(t):
        rhs = flip_ref[:, columns(t)]
        shift = base_ref[:, columns(t)]
        for sub in range(subs):
            total = jnp.zeros((8, tok_cols), jnp.float32)
            lhs = jnp.concatenate([cent_ref[pl.ds(sub * sub_rows, sub_rows), :], ones], axis=1)
            logits = dot(lhs, rhs)
            for first in range(0, sub_rows, slice_rows):
                scaled = jnp.exp(logits[first : first + slice_rows])
                total = total + fold_rows(scaled, jnp.add)
            sums_ref[step * subs + sub, :, columns(t)] = total
            shift_ref[step * subs + sub, :, columns(t)] = shift

    worst = jnp.float32(0.0)
    for sub in range(subs):
        for t in range(redo_blocks):
            block = jnp.max(sums_ref[step * subs + sub, :, t * redo_cols : (t + 1) * redo_cols])
            worst_ref[sub * redo_blocks + t] = block
            worst = jnp.maximum(worst, block)

    @pl.when(jnp.logical_not(worst < safe_sum))
    def _():
        @pl.loop(0, subs * redo_blocks)
        def _(k):
            @pl.when(jnp.logical_not(worst_ref[k] < safe_sum))
            def _():
                sub, t = k // redo_blocks, lax.rem(k, redo_blocks)
                first = pl.multiple_of(sub * sub_rows, sub_rows)
                rhs = flip_ref[0:width, columns(t, redo_cols)]
                logits = dot(cent_ref[pl.ds(first, sub_rows), :], rhs)
                top = jnp.max(fold_rows(logits, jnp.maximum), axis=0, keepdims=True)
                total = fold_rows(jnp.exp(logits - top), jnp.add)
                sums_ref[step * subs + sub, :, columns(t, redo_cols)] = total
                shift_ref[step * subs + sub, :, columns(t, redo_cols)] = top

    @pl.when(step == pl.num_programs(0) - 1)
    def _():
        @pl.loop(0, col_blocks)
        def _(t):
            shifts = shift_ref[:, :, columns(t)]
            top = jnp.max(shifts, axis=0)
            scale = jnp.exp(shifts - top[None])
            total = jnp.sum(sums_ref[:, :, columns(t)] * scale, axis=0)
            total = jnp.sum(total, axis=0, keepdims=True)
            out_ref[:, :, columns(t)] = jnp.broadcast_to(
                (top + jnp.log(total))[None], (out_ref.shape[0], 1, tok_cols)
            )


def local_lse(tokens, centroids, copies):
    tok_count, width = tokens.shape
    cent_count = centroids.shape[0]
    block_rows = divisor(cent_count, 4096)
    sub_rows = divisor(block_rows, 1024)
    tok_cols = divisor(tok_count, 512)
    blocks = cent_count // block_rows
    subs = cent_count // sub_rows
    flags = block_rows // sub_rows * (tok_count // divisor(tok_cols, 256))
    return pl.pallas_call(
        functools.partial(stats_kernel, sub_rows, tok_cols),
        grid=(blocks,),
        in_specs=[
            pl.BlockSpec((tok_count, width), lambda j: (0, 0)),
            pl.BlockSpec((block_rows, width), lambda j: (j, 0)),
        ],
        out_specs=pl.BlockSpec((copies, 1, tok_count), lambda j: (0, 0, 0)),
        out_shape=jax.ShapeDtypeStruct((copies, 1, tok_count), jnp.float32),
        scratch_shapes=[
            pltpu.VMEM((2 * width, tok_count), jnp.bfloat16),
            pltpu.VMEM((1, tok_count), jnp.float32),
            pltpu.VMEM((subs, 1, tok_count), jnp.float32),
            pltpu.VMEM((subs, 8, tok_count), jnp.float32),
            pltpu.SMEM((flags,), jnp.float32),
        ],
        compiler_params=pltpu.CompilerParams(vmem_limit_bytes=vmem_bytes),
        cost_estimate=pl.CostEstimate(
            flops=2 * tok_count * cent_count * width,
            bytes_accessed=(tok_count + cent_count) * width * 2,
            transcendentals=tok_count * cent_count,
        ),
        name="row_stats",
    )(tokens, centroids)


def encoded(x):
    x = x * code_scale
    return (x * jnp.abs(x) * (x * x)).astype(jnp.bfloat16)


def decoded(code):
    code = code.astype(jnp.float32)
    size = lax.rsqrt(lax.rsqrt(jnp.maximum(jnp.abs(code), 1e-37))) * (1.0 / code_scale)
    return jnp.where(code < 0, -size, jnp.where(code > 0, size, 0.0))


class Placing:
    def __init__(self, block_rows, table_ref, chunk, pieces, code_refs, outs, scratch):
        self.block_rows, self.table_ref, self.chunk = block_rows, table_ref, chunk
        self.pieces, self.code_refs = pieces, code_refs
        self.updated_ref, self.masses_ref = outs
        self.codes, self.values, self.masses, self.sems = scratch

    @staticmethod
    def scratch(sources, blocks, block_rows, width):
        return [
            pltpu.VMEM((sources, blocks * coded_rows(block_rows), width), jnp.bfloat16),
            pltpu.VMEM((sources, blocks * block_rows, width), jnp.float32),
            pltpu.VMEM((sources, blocks * block_rows // 128, 128), jnp.float32),
            pltpu.SemaphoreType.DMA((4, sources)),
        ]

    def copies_in(self):
        found, refs = [], list(self.code_refs)
        for s, count in enumerate(self.pieces):
            found.append([])
            first = 0
            for k in range(count):
                ref = refs.pop(0)
                target = self.codes.at[s, pl.ds(first, ref.shape[0]), :]
                found[s].append(pltpu.make_async_copy(ref, target, self.sems.at[3 * k, s]))
                first += ref.shape[0]
        return found

    def copies_out(self, s):
        rows, mass_rows = self.values.shape[1], self.masses.shape[1]
        start = self.table_ref[self.chunk, s]
        span = pl.ds(pl.multiple_of(start * self.block_rows, self.block_rows), rows)
        per_block = self.block_rows // 128
        mass_span = pl.ds(pl.multiple_of(start * per_block, per_block), mass_rows)
        return [
            pltpu.make_async_copy(self.values.at[s], self.updated_ref.at[span, :], self.sems.at[1, s]),
            pltpu.make_async_copy(self.masses.at[s], self.masses_ref.at[mass_span, :], self.sems.at[2, s]),
        ]

    def fetch(self):
        for copies in self.copies_in():
            for copy in copies:
                copy.start()

    def place(self):
        block_rows, per_block = self.block_rows, self.block_rows // 128
        full = coded_rows(block_rows)
        tile = divisor(block_rows, 256)
        for s, copies in enumerate(self.copies_in()):
            for copy in copies:
                copy.wait()

            @pl.loop(0, self.values.shape[1] // block_rows)
            def _(b):
                for k in range(block_rows // tile):
                    source = pl.ds(pl.multiple_of(b * full + k * tile, 32), tile)
                    target = pl.ds(pl.multiple_of(b * block_rows + k * tile, tile), tile)
                    self.values[s, target, :] = decoded(self.codes[s, source, :])
                last = pl.ds(pl.multiple_of(b * full + block_rows, 32), full - block_rows)
                terms = self.codes[s, last, :].astype(jnp.float32)
                mass = terms[:per_block] + terms[per_block : 2 * per_block]
                mass = mass + terms[2 * per_block : 3 * per_block]
                self.masses[s, pl.ds(pl.multiple_of(b * per_block, per_block), per_block), :] = mass

            for copy in self.copies_out(s):
                copy.start()

    def finish(self):
        for s in range(len(self.pieces)):
            for copy in self.copies_out(s):
                copy.wait()


def coded_rows(block_rows):
    return block_rows + block_rows // 32


def combine(groups, parts_ref, out_ref):
    per_group = parts_ref.shape[0] // groups
    count = parts_ref.shape[2]
    for t in range(groups):
        parts = [parts_ref[t * per_group + k] for k in range(per_group)]
        top = functools.reduce(jnp.maximum, parts)
        total = functools.reduce(jnp.add, [jnp.exp(part - top) for part in parts])
        out_ref[:, t * count : (t + 1) * count] = top + jnp.log(total)


def update_kernel(joins, unread, placed_chunk, pieces, block_rows, *refs):
    table_ref, tok_ref, lse_ref, cent_ref = refs[:4]
    refs = refs[4 + unread :]
    code_refs, refs = refs[: sum(pieces)], refs[sum(pieces) :]
    if pieces:
        code_ref, updated_ref, masses_ref = refs[2:5]
        scratch = refs[5:]
        outs = updated_ref, masses_ref
        placing = Placing(block_rows, table_ref, placed_chunk, pieces, code_refs, outs, scratch[3:])
    else:
        code_ref, scratch, placing = refs[0], refs[1:], None
    if joins:
        parts_ref, lse_ref, scratch = lse_ref, scratch[0], scratch[1:]
        pl.when(pl.program_id(0) == 0)(lambda: combine(joins, parts_ref, lse_ref))
    weights_ref, total_ref, mass_ref = scratch[:3]
    step, steps = pl.program_id(0), pl.num_programs(0)
    width = tok_ref.shape[1]
    _, tile, depth = weights_ref.shape
    piece = divisor(depth, 512)
    stages = tok_ref.shape[0] // depth
    tiles = block_rows // tile

    if placing:
        pl.when(step == 0)(placing.fetch)

    def weigh(first, stage):
        cents = cent_ref[pl.ds(first, tile), :] * jnp.bfloat16(inverse_temp)
        for k in range(depth // piece):
            span = pl.ds(pl.multiple_of(stage * depth + k * piece, piece), piece)
            logits = dot_nt(cents, tok_ref[span, :])
            lse = lse_ref[:, span]
            for r in range(0, tile, slice_rows):
                weights = jnp.exp(logits[r : r + slice_rows] - lse).astype(jnp.bfloat16)
                weights_ref[lax.rem(stage, 2), r : r + slice_rows, pl.ds(k * piece, piece)] = weights

    def gather_up(stage):
        toks = tok_ref[pl.ds(pl.multiple_of(stage * depth, depth), depth), :]
        rhs = jnp.concatenate([toks, jnp.ones_like(toks)], axis=1)
        total_ref[...] += jnp.dot(
            weights_ref[lax.rem(stage, 2)], rhs, preferred_element_type=jnp.float32
        )

    diagonal = lax.broadcasted_iota(jnp.int32, (128, 128), 0) == lax.broadcasted_iota(
        jnp.int32, (128, 128), 1
    )

    def run(r):
        first = pl.multiple_of(r * tile, tile)
        weigh(first, jnp.int32(0))
        total_ref[...] = jnp.zeros_like(total_ref)

        @pl.loop(1, stages)
        def _(stage):
            weigh(first, stage)
            gather_up(stage - 1)

        gather_up(jnp.int32(stages - 1))
        mass = total_ref[:, width : 2 * width]
        prior = prior_weight * cent_ref[pl.ds(first, tile), :].astype(jnp.float32)
        new = (total_ref[:, 0:width] + prior) / (mass + prior_weight)
        code_ref[pl.ds(first, tile), :] = encoded(new)
        for k in range(tile // 128):
            square = jnp.where(diagonal, mass[k * 128 : (k + 1) * 128, :], 0.0)
            mass_ref[pl.ds(r * (tile // 128) + k, 1), :] = jnp.sum(square, axis=0, keepdims=True)

    pl.loop(0, tiles // 2)(run)
    if placing:
        pl.when(step == 0)(placing.place)
    pl.loop(tiles // 2, tiles)(run)

    terms = split_exactly(mass_ref[...])
    terms = jnp.concatenate([*terms, jnp.zeros_like(terms[0])], axis=0)
    code_ref[block_rows : block_rows + terms.shape[0], :] = terms.astype(jnp.bfloat16)
    if placing:
        pl.when(step == steps - 1)(placing.finish)


def updated_chunk(
    table, chunk, toks, lse, centroids, blocks, block_rows, after=(), received=None, joins=0
):
    all_count, width = toks.shape
    depth = divisor(all_count, 2048)
    tile = divisor(block_rows, 1024)
    rows = blocks * block_rows
    full = coded_rows(block_rows)
    anywhere = pl.BlockSpec(memory_space=pl.ANY)
    whole = lambda j, place: (0, 0)
    operands = [
        pltpu.with_memory_space_constraint(toks, pltpu.HBM),
        lse,
        pltpu.with_memory_space_constraint(centroids, pltpu.HBM),
        *after,
    ]
    in_specs = [
        pl.BlockSpec((all_count, width), whole),
        pl.BlockSpec(lse.shape, (lambda j, place: (0, 0, 0)) if joins else whole),
        pl.BlockSpec((block_rows, width), lambda j, table: (table[chunk, 0] + j, 0)),
    ] + [anywhere] * len(after)
    out_specs = [pl.BlockSpec((full, width), lambda j, place: (j, 0))]
    out_shape = [jax.ShapeDtypeStruct((blocks * full, width), jnp.bfloat16)]
    scratch_shapes = [
        pltpu.VMEM((2, tile, depth), jnp.bfloat16),
        pltpu.VMEM((tile, 2 * width), jnp.float32),
        pltpu.VMEM((block_rows // 128, 128), jnp.float32),
    ]
    aliases, pieces, placed_chunk = {}, [], None
    if joins:
        out_specs.append(pl.BlockSpec((1, all_count), whole))
        out_shape.append(jax.ShapeDtypeStruct((1, all_count), jnp.float32))
    if received:
        placed_chunk, codes, outs = received
        pieces = [len(parts) for parts in codes]
        operands += [pltpu.with_memory_space_constraint(part, pltpu.HBM) for part in sum(codes, [])]
        operands += outs
        in_specs += [anywhere] * (sum(pieces) + 2)
        out_specs += [anywhere] * 2
        out_shape += [jax.ShapeDtypeStruct(out.shape, out.dtype) for out in outs]
        aliases = {len(operands) - 1: 1, len(operands): 2}
        scratch_shapes += Placing.scratch(len(codes), codes[0][0].shape[0] // full, block_rows, width)
    return pl.pallas_call(
        functools.partial(update_kernel, joins, len(after), placed_chunk, pieces, block_rows),
        grid_spec=pltpu.PrefetchScalarGridSpec(
            num_scalar_prefetch=1,
            grid=(blocks,),
            in_specs=in_specs,
            out_specs=out_specs,
            scratch_shapes=scratch_shapes,
        ),
        out_shape=out_shape,
        input_output_aliases=aliases,
        compiler_params=pltpu.CompilerParams(vmem_limit_bytes=vmem_bytes * 3 // 4),
        cost_estimate=pl.CostEstimate(
            flops=6 * all_count * rows * width // 8,
            bytes_accessed=(2 * all_count + 4 * rows) * width // 8,
            transcendentals=all_count * rows // 8,
        ),
        name="new_rows",
    )(table, *operands)


def place_kernel(chunks, block_rows, table_ref, *refs):
    count = sum(sum(pieces) for _, pieces in chunks)
    code_refs, outs, scratch = refs[:count], refs[count + 2 : count + 4], refs[count + 4 :]
    placings = []
    for chunk, pieces in chunks:
        used = code_refs[: sum(pieces)]
        placings.append(Placing(block_rows, table_ref, chunk, pieces, used, outs, scratch[:4]))
        code_refs, scratch = code_refs[sum(pieces) :], scratch[4:]
    for placing in placings:
        placing.fetch()
    for placing in placings:
        placing.place()
    for placing in placings:
        placing.finish()


def placed(table, received, outs, block_rows):
    operands, chunks, scratch_shapes = [], [], []
    for chunk, codes in received:
        chunks.append((chunk, [len(parts) for parts in codes]))
        operands += sum(codes, [])
        rows, width = codes[0][0].shape
        blocks = rows // coded_rows(block_rows)
        scratch_shapes += Placing.scratch(len(codes), blocks, block_rows, width)
    anywhere = pl.BlockSpec(memory_space=pl.ANY)
    return pl.pallas_call(
        functools.partial(place_kernel, chunks, block_rows),
        grid_spec=pltpu.PrefetchScalarGridSpec(
            num_scalar_prefetch=1,
            grid=(1,),
            in_specs=[anywhere] * (len(operands) + 2),
            out_specs=[anywhere] * 2,
            scratch_shapes=scratch_shapes,
        ),
        out_shape=[jax.ShapeDtypeStruct(out.shape, out.dtype) for out in outs],
        input_output_aliases={1 + len(operands): 0, 2 + len(operands): 1},
        compiler_params=pltpu.CompilerParams(vmem_limit_bytes=vmem_bytes // 2),
        name="placed_rows",
    )(table, *operands, *outs)


def blank(shape):
    return pl.pallas_call(
        lambda out_ref: None,
        out_specs=pl.BlockSpec(memory_space=pl.ANY),
        out_shape=jax.ShapeDtypeStruct(shape, jnp.float32),
        name="blank",
    )()


def from_others(value, axis):
    size = lax.axis_size(axis)
    found = [value]
    for s in range(1, size):
        pairs = [(partner(k, s, size), k) for k in range(size)]
        found.append(lax.ppermute(value, axis, pairs))
    return found


def partner(me, s, size):
    return me ^ s if size & (size - 1) == 0 else (me - s) % size


def chunk_plan(blocks):
    plan = []
    while blocks > 2:
        plan.append(2)
        blocks -= 2
    return plan + [1] * blocks


def local(tokens, centroids):
    tok_size, cent_size = lax.axis_size("tok"), lax.axis_size("cent")
    me = lax.axis_index("tok")
    cent_count, width = centroids.shape
    share_rows = cent_count // tok_size

    toks = lax.all_gather(tokens, "tok", axis=0, tiled=True)
    own_lse = local_lse(tokens, centroids, tok_size * cent_size)
    parts = lax.all_to_all(own_lse, ("tok", "cent"), 0, 0, tiled=True)

    block_rows = divisor(share_rows, 1024)
    plan = chunk_plan(share_rows // block_rows)
    sources = jnp.stack([partner(me, s, tok_size) for s in range(tok_size)])[None, :]
    starts = np.cumsum([0] + plan[:-1])[:, None] * tok_size
    table = (starts + sources * np.array(plan)[:, None]).astype(jnp.int32)
    outs = blank((cent_count, width)), blank((cent_count // 128, 128))
    waiting = []
    for k, blocks in enumerate(plan):
        arrived, received = [], None
        if len(waiting) > 1:
            arrived = sum(waiting[-2][1][1:], [])
            if blocks == 1:
                received = (*waiting.pop(0), outs)
                arrived = arrived[:1] if k + 1 == len(plan) else arrived
        operands = toks, lse if k else parts, centroids, blocks, block_rows, arrived, received
        codes, *rest = updated_chunk(table, k, *operands, joins=0 if k else tok_size)
        if not k:
            (lse,) = rest
        elif received:
            outs = rest
        waiting.append((k, [[part] for part in from_others(codes, "tok")]))
    if len(waiting) > 1:
        outs = placed(table, waiting[:-1], outs, block_rows)
    outs = placed(table, waiting[-1:], outs, block_rows)
    return outs[0], outs[1].reshape(cent_count)


def solution(mesh):
    placed_as = (P("tok", None), P("cent", None))
    return jax.shard_map(
        local, mesh=mesh, in_specs=placed_as, out_specs=(P("cent", None), P("cent")), check_vma=False
    )
```

```python
import functools

import jax
import jax.numpy as jnp
import numpy as np
from jax import lax
from jax.experimental import pallas as pl
from jax.experimental.pallas import tpu as pltpu
from jax.sharding import PartitionSpec as P

inverse_temp = 2.0
prior_weight = 0.05
safe_sum = 1e30
headroom = 60.0
code_scale = 2.0**24
slice_rows = 64
vmem_bytes = 56 * 1024 * 1024


def divisor(count, most):
    size = min(count, most)
    while count % size:
        size //= 2
    return size


def dot_nt(a, b):
    return lax.dot_general(a, b, (((1,), (1,)), ((), ())), preferred_element_type=jnp.float32)


def fold_rows(x, combine):
    parts = [x[k * 8 : (k + 1) * 8, :] for k in range(x.shape[0] // 8)]
    while len(parts) > 1:
        half = len(parts) // 2
        parts = [combine(parts[2 * k], parts[2 * k + 1]) for k in range(half)] + parts[2 * half :]
    return parts[0]


def split_exactly(x):
    high = x.astype(jnp.bfloat16).astype(jnp.float32)
    middle = (x - high).astype(jnp.bfloat16).astype(jnp.float32)
    return high, middle, x - high - middle


def stats_kernel(
    sub_rows, tok_cols, tok_ref, cent_ref, out_ref, flip_ref, base_ref, shift_ref, sums_ref, worst_ref
):
    step = pl.program_id(0)
    tok_count = tok_ref.shape[0]
    subs = cent_ref.shape[0] // sub_rows
    col_blocks = tok_count // tok_cols
    redo_cols = divisor(tok_cols, 256)
    redo_blocks = tok_count // redo_cols

    def columns(t, size=tok_cols):
        return pl.ds(pl.multiple_of(t * size, size), size)

    def dot(a, b):
        return jnp.dot(a, b, preferred_element_type=jnp.float32)

    width = tok_ref.shape[1]

    @pl.when(step == 0)
    def _():
        @pl.loop(0, col_blocks)
        def _(t):
            flipped = (tok_ref[columns(t), :] * jnp.bfloat16(inverse_temp)).T
            flip_ref[0:width, columns(t)] = flipped
            logits = dot(cent_ref[0:128, :], flipped)
            top = jnp.max(fold_rows(logits, jnp.maximum), axis=0, keepdims=True)
            base = top + headroom
            base_ref[:, columns(t)] = base
            row = lax.broadcasted_iota(jnp.int32, (width, tok_cols), 0)
            terms = jnp.zeros((width, tok_cols), jnp.float32)
            for k, term in enumerate(split_exactly(-base)):
                terms = jnp.where(row == k, term, terms)
            flip_ref[width:, columns(t)] = terms.astype(jnp.bfloat16)

    lane = lax.broadcasted_iota(jnp.int32, (sub_rows, width), 1)
    ones = jnp.where(lane < 3, 1.0, 0.0).astype(jnp.bfloat16)

    @pl.loop(0, col_blocks)
    def _(t):
        rhs = flip_ref[:, columns(t)]
        shift = base_ref[:, columns(t)]
        for sub in range(subs):
            total = jnp.zeros((8, tok_cols), jnp.float32)
            lhs = jnp.concatenate([cent_ref[pl.ds(sub * sub_rows, sub_rows), :], ones], axis=1)
            logits = dot(lhs, rhs)
            for first in range(0, sub_rows, slice_rows):
                scaled = jnp.exp(logits[first : first + slice_rows])
                total = total + fold_rows(scaled, jnp.add)
            sums_ref[step * subs + sub, :, columns(t)] = total
            shift_ref[step * subs + sub, :, columns(t)] = shift

    worst = jnp.float32(0.0)
    for sub in range(subs):
        for t in range(redo_blocks):
            block = jnp.max(sums_ref[step * subs + sub, :, t * redo_cols : (t + 1) * redo_cols])
            worst_ref[sub * redo_blocks + t] = block
            worst = jnp.maximum(worst, block)

    @pl.when(jnp.logical_not(worst < safe_sum))
    def _():
        @pl.loop(0, subs * redo_blocks)
        def _(k):
            @pl.when(jnp.logical_not(worst_ref[k] < safe_sum))
            def _():
                sub, t = k // redo_blocks, lax.rem(k, redo_blocks)
                first = pl.multiple_of(sub * sub_rows, sub_rows)
                rhs = flip_ref[0:width, columns(t, redo_cols)]
                logits = dot(cent_ref[pl.ds(first, sub_rows), :], rhs)
                top = jnp.max(fold_rows(logits, jnp.maximum), axis=0, keepdims=True)
                total = fold_rows(jnp.exp(logits - top), jnp.add)
                sums_ref[step * subs + sub, :, columns(t, redo_cols)] = total
                shift_ref[step * subs + sub, :, columns(t, redo_cols)] = top

    @pl.when(step == pl.num_programs(0) - 1)
    def _():
        @pl.loop(0, col_blocks)
        def _(t):
            shifts = shift_ref[:, :, columns(t)]
            top = jnp.max(shifts, axis=0)
            scale = jnp.exp(shifts - top[None])
            total = jnp.sum(sums_ref[:, :, columns(t)] * scale, axis=0)
            total = jnp.sum(total, axis=0, keepdims=True)
            out_ref[:, :, columns(t)] = jnp.broadcast_to(
                (top + jnp.log(total))[None], (out_ref.shape[0], 1, tok_cols)
            )


def local_lse(tokens, centroids, copies):
    tok_count, width = tokens.shape
    cent_count = centroids.shape[0]
    block_rows = divisor(cent_count, 4096)
    sub_rows = divisor(block_rows, 1024)
    tok_cols = divisor(tok_count, 512)
    blocks = cent_count // block_rows
    subs = cent_count // sub_rows
    flags = block_rows // sub_rows * (tok_count // divisor(tok_cols, 256))
    return pl.pallas_call(
        functools.partial(stats_kernel, sub_rows, tok_cols),
        grid=(blocks,),
        in_specs=[
            pl.BlockSpec((tok_count, width), lambda j: (0, 0)),
            pl.BlockSpec((block_rows, width), lambda j: (j, 0)),
        ],
        out_specs=pl.BlockSpec((copies, 1, tok_count), lambda j: (0, 0, 0)),
        out_shape=jax.ShapeDtypeStruct((copies, 1, tok_count), jnp.float32),
        scratch_shapes=[
            pltpu.VMEM((2 * width, tok_count), jnp.bfloat16),
            pltpu.VMEM((1, tok_count), jnp.float32),
            pltpu.VMEM((subs, 1, tok_count), jnp.float32),
            pltpu.VMEM((subs, 8, tok_count), jnp.float32),
            pltpu.SMEM((flags,), jnp.float32),
        ],
        compiler_params=pltpu.CompilerParams(vmem_limit_bytes=vmem_bytes),
        cost_estimate=pl.CostEstimate(
            flops=2 * tok_count * cent_count * width,
            bytes_accessed=(tok_count + cent_count) * width * 2,
            transcendentals=tok_count * cent_count,
        ),
        name="row_stats",
    )(tokens, centroids)


def encoded(x):
    x = x * code_scale
    return (x * jnp.abs(x) * (x * x)).astype(jnp.bfloat16)


def decoded(code):
    code = code.astype(jnp.float32)
    size = lax.rsqrt(lax.rsqrt(jnp.maximum(jnp.abs(code), 1e-37))) * (1.0 / code_scale)
    return jnp.where(code < 0, -size, jnp.where(code > 0, size, 0.0))


class Placing:
    def __init__(self, block_rows, table_ref, chunk, pieces, code_refs, outs, scratch):
        self.block_rows, self.table_ref, self.chunk = block_rows, table_ref, chunk
        self.pieces, self.code_refs = pieces, code_refs
        self.updated_ref, self.masses_ref = outs
        self.codes, self.values, self.masses, self.sems = scratch

    @staticmethod
    def scratch(sources, blocks, block_rows, width):
        return [
            pltpu.VMEM((sources, blocks * coded_rows(block_rows), width), jnp.bfloat16),
            pltpu.VMEM((sources, blocks * block_rows, width), jnp.float32),
            pltpu.VMEM((sources, blocks * block_rows // 128, 128), jnp.float32),
            pltpu.SemaphoreType.DMA((4, sources)),
        ]

    def copies_in(self):
        found, refs = [], list(self.code_refs)
        for s, count in enumerate(self.pieces):
            found.append([])
            first = 0
            for k in range(count):
                ref = refs.pop(0)
                target = self.codes.at[s, pl.ds(first, ref.shape[0]), :]
                found[s].append(pltpu.make_async_copy(ref, target, self.sems.at[3 * k, s]))
                first += ref.shape[0]
        return found

    def copies_out(self, s):
        rows, mass_rows = self.values.shape[1], self.masses.shape[1]
        start = self.table_ref[self.chunk, s]
        span = pl.ds(pl.multiple_of(start * self.block_rows, self.block_rows), rows)
        per_block = self.block_rows // 128
        mass_span = pl.ds(pl.multiple_of(start * per_block, per_block), mass_rows)
        return [
            pltpu.make_async_copy(self.values.at[s], self.updated_ref.at[span, :], self.sems.at[1, s]),
            pltpu.make_async_copy(self.masses.at[s], self.masses_ref.at[mass_span, :], self.sems.at[2, s]),
        ]

    def fetch(self):
        for copies in self.copies_in():
            for copy in copies:
                copy.start()

    def place(self):
        block_rows, per_block = self.block_rows, self.block_rows // 128
        full = coded_rows(block_rows)
        tile = divisor(block_rows, 256)
        for s, copies in enumerate(self.copies_in()):
            for copy in copies:
                copy.wait()

            @pl.loop(0, self.values.shape[1] // block_rows)
            def _(b):
                for k in range(block_rows // tile):
                    source = pl.ds(pl.multiple_of(b * full + k * tile, 32), tile)
                    target = pl.ds(pl.multiple_of(b * block_rows + k * tile, tile), tile)
                    self.values[s, target, :] = decoded(self.codes[s, source, :])
                last = pl.ds(pl.multiple_of(b * full + block_rows, 32), full - block_rows)
                terms = self.codes[s, last, :].astype(jnp.float32)
                mass = terms[:per_block] + terms[per_block : 2 * per_block]
                mass = mass + terms[2 * per_block : 3 * per_block]
                self.masses[s, pl.ds(pl.multiple_of(b * per_block, per_block), per_block), :] = mass

            for copy in self.copies_out(s):
                copy.start()

    def finish(self):
        for s in range(len(self.pieces)):
            for copy in self.copies_out(s):
                copy.wait()


def coded_rows(block_rows):
    return block_rows + block_rows // 32


def combine(groups, parts_ref, out_ref):
    per_group = parts_ref.shape[0] // groups
    count = parts_ref.shape[2]
    for t in range(groups):
        parts = [parts_ref[t * per_group + k] for k in range(per_group)]
        top = functools.reduce(jnp.maximum, parts)
        total = functools.reduce(jnp.add, [jnp.exp(part - top) for part in parts])
        out_ref[:, t * count : (t + 1) * count] = top + jnp.log(total)


def update_kernel(joins, unread, placed_chunk, pieces, block_rows, *refs):
    table_ref, tok_ref, lse_ref, cent_ref = refs[:4]
    refs = refs[4 + unread :]
    code_refs, refs = refs[: sum(pieces)], refs[sum(pieces) :]
    if pieces:
        code_ref, updated_ref, masses_ref = refs[2:5]
        scratch = refs[5:]
        outs = updated_ref, masses_ref
        placing = Placing(block_rows, table_ref, placed_chunk, pieces, code_refs, outs, scratch[3:])
    else:
        code_ref, scratch, placing = refs[0], refs[1:], None
    if joins:
        parts_ref, lse_ref, scratch = lse_ref, scratch[0], scratch[1:]
        pl.when(pl.program_id(0) == 0)(lambda: combine(joins, parts_ref, lse_ref))
    weights_ref, total_ref, mass_ref = scratch[:3]
    step, steps = pl.program_id(0), pl.num_programs(0)
    width = tok_ref.shape[1]
    _, tile, depth = weights_ref.shape
    piece = divisor(depth, 512)
    stages = tok_ref.shape[0] // depth
    tiles = block_rows // tile

    if placing:
        pl.when(step == 0)(placing.fetch)

    def weigh(first, stage):
        cents = cent_ref[pl.ds(first, tile), :] * jnp.bfloat16(inverse_temp)
        for k in range(depth // piece):
            span = pl.ds(stage * depth + k * piece, piece)
            logits = dot_nt(cents, tok_ref[span, :])
            lse = lse_ref[:, span]
            for r in range(0, tile, slice_rows):
                weights = jnp.exp(logits[r : r + slice_rows] - lse).astype(jnp.bfloat16)
                weights_ref[stage % 2, r : r + slice_rows, pl.ds(k * piece, piece)] = weights

    def gather_up(stage):
        toks = tok_ref[pl.ds(stage * depth, depth), :]
        rhs = jnp.concatenate([toks, jnp.ones_like(toks)], axis=1)
        part = jnp.dot(weights_ref[stage % 2], rhs, preferred_element_type=jnp.float32)
        if stage == 0:
            total_ref[...] = part
        else:
            total_ref[...] += part

    diagonal = lax.broadcasted_iota(jnp.int32, (128, 128), 0) == lax.broadcasted_iota(
        jnp.int32, (128, 128), 1
    )

    def run(r):
        first = pl.multiple_of(r * tile, tile)
        weigh(first, 0)
        for stage in range(1, stages):
            weigh(first, stage)
            gather_up(stage - 1)
        gather_up(stages - 1)
        mass = total_ref[:, width : 2 * width]
        prior = prior_weight * cent_ref[pl.ds(first, tile), :].astype(jnp.float32)
        new = (total_ref[:, 0:width] + prior) / (mass + prior_weight)
        code_ref[pl.ds(first, tile), :] = encoded(new)
        for k in range(tile // 128):
            square = jnp.where(diagonal, mass[k * 128 : (k + 1) * 128, :], 0.0)
            mass_ref[pl.ds(r * (tile // 128) + k, 1), :] = jnp.sum(square, axis=0, keepdims=True)

    pl.loop(0, tiles // 2)(run)
    if placing:
        pl.when(step == 0)(placing.place)
    pl.loop(tiles // 2, tiles)(run)

    terms = split_exactly(mass_ref[...])
    terms = jnp.concatenate([*terms, jnp.zeros_like(terms[0])], axis=0)
    code_ref[block_rows : block_rows + terms.shape[0], :] = terms.astype(jnp.bfloat16)
    if placing:
        pl.when(step == steps - 1)(placing.finish)


def updated_chunk(
    table, chunk, toks, lse, centroids, blocks, block_rows, after=(), received=None, joins=0
):
    all_count, width = toks.shape
    depth = divisor(all_count, 1024)
    tile = divisor(block_rows, 1024)
    rows = blocks * block_rows
    full = coded_rows(block_rows)
    anywhere = pl.BlockSpec(memory_space=pl.ANY)
    whole = lambda j, place: (0, 0)
    operands = [
        pltpu.with_memory_space_constraint(toks, pltpu.HBM),
        lse,
        pltpu.with_memory_space_constraint(centroids, pltpu.HBM),
        *after,
    ]
    in_specs = [
        pl.BlockSpec((all_count, width), whole),
        pl.BlockSpec(lse.shape, (lambda j, place: (0, 0, 0)) if joins else whole),
        pl.BlockSpec((block_rows, width), lambda j, table: (table[chunk, 0] + j, 0)),
    ] + [anywhere] * len(after)
    out_specs = [pl.BlockSpec((full, width), lambda j, place: (j, 0))]
    out_shape = [jax.ShapeDtypeStruct((blocks * full, width), jnp.bfloat16)]
    scratch_shapes = [
        pltpu.VMEM((2, tile, depth), jnp.bfloat16),
        pltpu.VMEM((tile, 2 * width), jnp.float32),
        pltpu.VMEM((block_rows // 128, 128), jnp.float32),
    ]
    aliases, pieces, placed_chunk = {}, [], None
    if joins:
        out_specs.append(pl.BlockSpec((1, all_count), whole))
        out_shape.append(jax.ShapeDtypeStruct((1, all_count), jnp.float32))
    if received:
        placed_chunk, codes, outs = received
        pieces = [len(parts) for parts in codes]
        operands += [pltpu.with_memory_space_constraint(part, pltpu.HBM) for part in sum(codes, [])]
        operands += outs
        in_specs += [anywhere] * (sum(pieces) + 2)
        out_specs += [anywhere] * 2
        out_shape += [jax.ShapeDtypeStruct(out.shape, out.dtype) for out in outs]
        aliases = {len(operands) - 1: 1, len(operands): 2}
        scratch_shapes += Placing.scratch(len(codes), codes[0][0].shape[0] // full, block_rows, width)
    return pl.pallas_call(
        functools.partial(update_kernel, joins, len(after), placed_chunk, pieces, block_rows),
        grid_spec=pltpu.PrefetchScalarGridSpec(
            num_scalar_prefetch=1,
            grid=(blocks,),
            in_specs=in_specs,
            out_specs=out_specs,
            scratch_shapes=scratch_shapes,
        ),
        out_shape=out_shape,
        input_output_aliases=aliases,
        compiler_params=pltpu.CompilerParams(vmem_limit_bytes=vmem_bytes * 3 // 4),
        cost_estimate=pl.CostEstimate(
            flops=6 * all_count * rows * width // 8,
            bytes_accessed=(2 * all_count + 4 * rows) * width // 8,
            transcendentals=all_count * rows // 8,
        ),
        name="new_rows",
    )(table, *operands)


def place_kernel(chunks, block_rows, table_ref, *refs):
    count = sum(sum(pieces) for _, pieces in chunks)
    code_refs, outs, scratch = refs[:count], refs[count + 2 : count + 4], refs[count + 4 :]
    placings = []
    for chunk, pieces in chunks:
        used = code_refs[: sum(pieces)]
        placings.append(Placing(block_rows, table_ref, chunk, pieces, used, outs, scratch[:4]))
        code_refs, scratch = code_refs[sum(pieces) :], scratch[4:]
    for placing in placings:
        placing.fetch()
    for placing in placings:
        placing.place()
    for placing in placings:
        placing.finish()


def placed(table, received, outs, block_rows):
    operands, chunks, scratch_shapes = [], [], []
    for chunk, codes in received:
        chunks.append((chunk, [len(parts) for parts in codes]))
        operands += sum(codes, [])
        rows, width = codes[0][0].shape
        blocks = rows // coded_rows(block_rows)
        scratch_shapes += Placing.scratch(len(codes), blocks, block_rows, width)
    anywhere = pl.BlockSpec(memory_space=pl.ANY)
    return pl.pallas_call(
        functools.partial(place_kernel, chunks, block_rows),
        grid_spec=pltpu.PrefetchScalarGridSpec(
            num_scalar_prefetch=1,
            grid=(1,),
            in_specs=[anywhere] * (len(operands) + 2),
            out_specs=[anywhere] * 2,
            scratch_shapes=scratch_shapes,
        ),
        out_shape=[jax.ShapeDtypeStruct(out.shape, out.dtype) for out in outs],
        input_output_aliases={1 + len(operands): 0, 2 + len(operands): 1},
        compiler_params=pltpu.CompilerParams(vmem_limit_bytes=vmem_bytes // 2),
        name="placed_rows",
    )(table, *operands, *outs)


def blank(shape):
    return pl.pallas_call(
        lambda out_ref: None,
        out_specs=pl.BlockSpec(memory_space=pl.ANY),
        out_shape=jax.ShapeDtypeStruct(shape, jnp.float32),
        name="blank",
    )()


def from_others(value, axis):
    size = lax.axis_size(axis)
    found = [value]
    for s in range(1, size):
        pairs = [(partner(k, s, size), k) for k in range(size)]
        found.append(lax.ppermute(value, axis, pairs))
    return found


def partner(me, s, size):
    return me ^ s if size & (size - 1) == 0 else (me - s) % size


def chunk_plan(blocks):
    plan = []
    while blocks > 2:
        plan.append(2)
        blocks -= 2
    return plan + [1] * blocks


def local(tokens, centroids):
    tok_size, cent_size = lax.axis_size("tok"), lax.axis_size("cent")
    me = lax.axis_index("tok")
    cent_count, width = centroids.shape
    share_rows = cent_count // tok_size

    toks = lax.all_gather(tokens, "tok", axis=0, tiled=True)
    own_lse = local_lse(tokens, centroids, tok_size * cent_size)
    parts = lax.all_to_all(own_lse, ("tok", "cent"), 0, 0, tiled=True)

    block_rows = divisor(share_rows, 1024)
    plan = chunk_plan(share_rows // block_rows)
    sources = jnp.stack([partner(me, s, tok_size) for s in range(tok_size)])[None, :]
    starts = np.cumsum([0] + plan[:-1])[:, None] * tok_size
    table = (starts + sources * np.array(plan)[:, None]).astype(jnp.int32)
    outs = blank((cent_count, width)), blank((cent_count // 128, 128))
    waiting = []
    for k, blocks in enumerate(plan):
        arrived, received = [], None
        if len(waiting) > 1:
            arrived = sum(waiting[-2][1][1:], [])
            if blocks == 1:
                received = (*waiting.pop(0), outs)
                arrived = arrived[:1] if k + 1 == len(plan) else arrived
        operands = toks, lse if k else parts, centroids, blocks, block_rows, arrived, received
        codes, *rest = updated_chunk(table, k, *operands, joins=0 if k else tok_size)
        if not k:
            (lse,) = rest
        elif received:
            outs = rest
        waiting.append((k, [[part] for part in from_others(codes, "tok")]))
    if len(waiting) > 1:
        outs = placed(table, waiting[:-1], outs, block_rows)
    outs = placed(table, waiting[-1:], outs, block_rows)
    return outs[0], outs[1].reshape(cent_count)


def solution(mesh):
    placed_as = (P("tok", None), P("cent", None))
    return jax.shard_map(
        local, mesh=mesh, in_specs=placed_as, out_specs=(P("cent", None), P("cent")), check_vma=False
    )
```
